32 devices in a mesh: groups: 2 (over x), leaf: 4 (over y, core), inner: 4 (over z).
Axes of the slice: x: 2, y: 2, z: 4, core: 2. Of those that a mesh axis runs over, the one named last changes fastest.
Arguments:
- anomalies: bfloat16 [65536, 256], P(('leaf', 'inner'), 'groups'), parts along dimension 1, may hold values from -6 to 6
- leaf_basis: bfloat16 [128, 64, 512], P(('leaf', 'inner')), may hold values from -0.25 to 0.25
- near_blocks: bfloat16 [128, 5, 512, 512], P(('leaf', 'inner')), may hold values from -0.125 to 0.125
- near_ids: int32 [128, 5], P(('leaf', 'inner')), may hold values from 0 to 127, as said below
- transfer_leaf: bfloat16 [128, 64, 64], P(('leaf', 'inner')), may hold values from -0.25 to 0.25
- transfer_mid: bfloat16 [16, 64, 64], P(('leaf', 'inner')), may hold values from -0.375 to 0.375
- far_ids: int32 [16, 4], P(('leaf', 'inner')), may hold values from 0 to 15, as said below
- far_count: int32 [16], P(('leaf', 'inner')), may hold values from 1 to 4
- mid_couple: bfloat16 [16, 4, 64, 64], P(('leaf', 'inner')), may hold values from -0.375 to 0.375
- top_couple: bfloat16 [4, 4, 64, 64], P('leaf'), may hold values from -0.375 to 0.375
Outputs:
- localized: bfloat16 [65536, 256], P(('leaf', 'inner'), 'groups'), parts along dimension 1
The draws below stay inside these ranges and needn't reach their ends.
There are 2 independent parts, one for each index of `groups`. The reference program is written for one: setup_inputs(seed, part) draws one part's arguments, and reference() takes and returns one part's arrays. A program takes and returns all parts, laid end to end along the dimension named above; an argument that names none is the same for every part. Nothing has to cross between parts.
Inputs may be any that keep to these rules, and one draw needn't show every extreme that they name: `near_ids`: slot 0 of leaf l is l itself; the other slots name leaves at most 8 leaves away from l, repeats allowed. `far_ids`: the partners of cluster c are distinct, differ from c - 1, c and c + 1, and lie in row groups c // 4 - 1 to c // 4 + 1 (row group of d: d // 4); slots from far_count[c] on are ignored.
All inputs are finite; a program needn't handle non-finite values.
Results may differ from the reference program's by a relative error of at most 0.0065.
Values may be sent and summed in bfloat16 or wider, within the bound.
No kernel may reach another device: no remote copies, remote signals or barrier semaphores. Data moves between devices by JAX's collectives and lax.ppermute only.
A program may use at most 128 MiB of HBM per device.

```python
import jax
import jax.numpy as jnp
from jax import lax

LEAF = 512
RANK = 64
COLS = 128
LEAF_DEV = 8
NEAR = 5
FAR = 4
LEAVES = 128
CLUSTERS = 16
ROWS = 65536
N_LEAF = 4
N_INNER = 4


def draw_near_ids(key, part):
    key = jax.random.fold_in(key, 11)
    leaves = LEAF_DEV * N_LEAF * N_INNER
    first_key, second_key = jax.random.split(key)
    distance = jax.random.randint(first_key, (leaves, NEAR - 1), 1, LEAF_DEV + 1)
    direction = 2 * jax.random.randint(second_key, (leaves, NEAR - 1), 0, 2) - 1
    leaf_ids = jnp.arange(leaves, dtype=jnp.int32)[:, None]
    target = leaf_ids + direction * distance
    outside = (target < 0) | (target >= leaves)
    target = jnp.where(outside, leaf_ids - direction * distance, target)
    return jnp.concatenate([leaf_ids, target], axis=1).astype(jnp.int32)


def draw_far_ids(key, part):
    key = jax.random.fold_in(key, 23)
    clusters = N_LEAF * N_INNER
    own_ids = jnp.arange(clusters, dtype=jnp.int32)[:, None]
    other_ids = jnp.arange(clusters, dtype=jnp.int32)[None, :]
    valid = (jnp.abs(own_ids // N_INNER - other_ids // N_INNER) <= 1) & (jnp.abs(own_ids - other_ids) >= 2)
    scores = jax.random.randint(key, (clusters, clusters), 0, 4096) * clusters + other_ids
    scores = jnp.where(valid, scores, 4096 * clusters + other_ids)
    ordering = jnp.argsort(scores, axis=1)
    return ordering[:, :FAR].astype(jnp.int32)


def draw_far_count(key, part):
    key = jax.random.fold_in(key, 37)
    clusters = N_LEAF * N_INNER
    first_key, second_key = jax.random.split(key)
    counts = jax.random.randint(first_key, (clusters,), 1, FAR + 1)
    picked = jax.random.randint(second_key, (), 0, clusters)
    return jnp.where(jnp.arange(clusters, dtype=jnp.int32) == picked, FAR, counts).astype(jnp.int32)


def block_scale(own_key, shape, cuts, least, high):
    def one(dim, parts):
        steps = jax.random.uniform(jax.random.fold_in(jax.random.fold_in(own_key, 6), dim), (parts,), jnp.float32, least / len(cuts), high / len(cuts))
        return jnp.repeat(jnp.exp(steps), shape[dim] // parts).reshape((-1,) + (1,) * (len(shape) - dim - 1))

    factor_of = one(*cuts[0])
    for cut in cuts[1:]:
        factor_of = factor_of * one(*cut)
    return factor_of


def scatter_about(key, shape, spread, bound, shards=(), kind=jnp.bfloat16):
    array = jax.random.normal(key, shape, jnp.float32) * spread
    if len(shards) > 0:
        array = block_scale(key, shape, shards, -0.22, 0.18) * array
    return jnp.clip(array, min=-bound, max=bound).astype(kind)


def setup_inputs(seed: int = 0, part: int = 0) -> dict:
    splits = jax.random.split(jax.random.key(seed), 11)
    part_keys = jax.random.split(jax.random.fold_in(splits[10], part), 11)
    anomalies = scatter_about(part_keys[0], (ROWS, COLS), 1.0, 6.0, ((0, 16),))
    leaf_basis = scatter_about(splits[1], (LEAVES, RANK, LEAF), LEAF ** -0.5, 0.25, ((0, 16),))
    near_blocks = scatter_about(splits[2], (LEAVES, NEAR, LEAF, LEAF), (LEAF * NEAR) ** -0.5, 0.125, ((0, 16),))
    near_ids = draw_near_ids(jax.random.fold_in(splits[10], 71), part)
    transfer_leaf = scatter_about(splits[4], (LEAVES, RANK, RANK), (RANK * LEAF_DEV) ** -0.5, 0.25, ((0, 16),))
    transfer_mid = scatter_about(splits[5], (CLUSTERS, RANK, RANK), (RANK * N_INNER) ** -0.5, 0.375, ((0, 16),))
    far_ids = draw_far_ids(jax.random.fold_in(splits[10], 71), part)
    far_count = draw_far_count(jax.random.fold_in(splits[10], 71), part)
    mid_couple = scatter_about(splits[8], (CLUSTERS, FAR, RANK, RANK), (RANK * FAR) ** -0.5, 0.375, ((0, 16),))
    top_couple = scatter_about(splits[9], (N_LEAF, N_LEAF, RANK, RANK), (RANK * N_LEAF) ** -0.5, 0.375, ((0, 4),))
    return dict(anomalies=anomalies, leaf_basis=leaf_basis, near_blocks=near_blocks, near_ids=near_ids, transfer_leaf=transfer_leaf, transfer_mid=transfer_mid, far_ids=far_ids, far_count=far_count, mid_couple=mid_couple, top_couple=top_couple)


def reference(anomalies, leaf_basis, near_blocks, near_ids, transfer_leaf, transfer_mid, far_ids, far_count, mid_couple, top_couple):
    leaves = LEAF_DEV * N_LEAF * N_INNER
    clusters = N_LEAF * N_INNER
    blocks = anomalies.reshape(leaves, LEAF, COLS)
    skeleton = jnp.einsum('lri,lin->lrn', leaf_basis.astype(jnp.float32), blocks.astype(jnp.float32)).astype(jnp.bfloat16)
    lifted = jnp.einsum('lrs,lrn->lsn', transfer_leaf.astype(jnp.float32), skeleton.astype(jnp.float32))
    mid_skel = lifted.reshape(clusters, LEAF_DEV, RANK, COLS).sum(axis=1).astype(jnp.bfloat16)
    raised = jnp.einsum('crs,crn->csn', transfer_mid.astype(jnp.float32), mid_skel.astype(jnp.float32))
    top_skel = raised.reshape(N_LEAF, N_INNER, RANK, COLS).sum(axis=1).astype(jnp.bfloat16)
    group_ids = jnp.arange(N_LEAF, dtype=jnp.int32)
    admissible = jnp.abs(group_ids[:, None] - group_ids[None, :]) >= 2
    coupling = jnp.where(admissible[:, :, None, None], top_couple.astype(jnp.float32), 0.0)
    top_down = jnp.einsum('ghrs,hsn->grn', coupling, top_skel.astype(jnp.float32)).astype(jnp.bfloat16)
    chosen = mid_skel[far_ids].astype(jnp.float32)
    partial_terms = jnp.einsum('ckrs,cksn->ckrn', mid_couple.astype(jnp.float32), chosen)
    live_slots = jnp.arange(FAR, dtype=jnp.int32)[None, :] < far_count[:, None]
    far_sum = jnp.sum(jnp.where(live_slots[:, :, None, None], partial_terms, 0.0), axis=1)
    parent_down = jnp.repeat(top_down, N_INNER, axis=0).astype(jnp.float32)
    mid_down = (far_sum + jnp.einsum('crs,csn->crn', transfer_mid.astype(jnp.float32), parent_down)).astype(jnp.bfloat16)
    cluster_down = jnp.repeat(mid_down, LEAF_DEV, axis=0).astype(jnp.float32)
    leaf_down = jnp.einsum('lrs,lsn->lrn', transfer_leaf.astype(jnp.float32), cluster_down).astype(jnp.bfloat16)
    far_out = jnp.einsum('lri,lrn->lin', leaf_basis.astype(jnp.float32), leaf_down.astype(jnp.float32))

    def near_leaf(leaf_index):
        gathered = blocks[near_ids[leaf_index]].astype(jnp.float32)
        return jnp.einsum('kij,kjn->in', near_blocks[leaf_index].astype(jnp.float32), gathered)

    near_out = lax.map(near_leaf, jnp.arange(leaves, dtype=jnp.int32))
    return (far_out + near_out).astype(jnp.bfloat16).reshape(leaves * LEAF, COLS)
```

```python
import functools

import jax
import jax.numpy as jnp
from jax import lax
from jax.experimental import pallas as pl
from jax.experimental.pallas import tpu as pltpu
from jax.sharding import PartitionSpec as P

MIB = 1 << 20
VMEM = pl.BlockSpec(memory_space=pltpu.VMEM)
SMEM = pl.BlockSpec(memory_space=pltpu.SMEM)
ANY = pl.BlockSpec(memory_space=pl.ANY)
HBM = pl.BlockSpec(memory_space=pltpu.HBM)


def dot(a, b):
    return lax.dot_general(a, b, (((1,), (0,)), ((), ())), preferred_element_type=jnp.float32)


def dot_t(a, b):
    return lax.dot_general(a, b, (((0,), (0,)), ((), ())), preferred_element_type=jnp.float32)


def call(kernel, out_shape, in_specs, out_specs, scratch, flops, moved, vmem):
    return pl.pallas_call(
        kernel,
        out_shape=out_shape,
        in_specs=in_specs,
        out_specs=out_specs,
        scratch_shapes=scratch,
        cost_estimate=pl.CostEstimate(flops=flops, bytes_accessed=moved, transcendentals=0),
        compiler_params=pltpu.CompilerParams(vmem_limit_bytes=vmem),
    )


def up_kernel(x_ref, basis_ref, leaf_map_ref, mid_map_ref, out_ref):
    leaves, rank, rows = basis_ref.shape
    mid = jnp.zeros((rank, x_ref.shape[1]), jnp.float32)
    for leaf in range(leaves):
        skeleton = dot(basis_ref[leaf], x_ref[leaf * rows : (leaf + 1) * rows, :])
        mid += dot_t(leaf_map_ref[leaf], skeleton.astype(jnp.bfloat16))
    mid = mid.astype(jnp.bfloat16)
    out_ref[:rank, :] = mid
    out_ref[rank:, :] = dot_t(mid_map_ref[0], mid).astype(jnp.bfloat16)


def group_kernel(count, *refs):
    parts, out_ref, top_ref = refs[:count], refs[count], refs[count + 1]
    rank = top_ref.shape[0]
    top = jnp.zeros(top_ref.shape, jnp.float32)
    for i, part in enumerate(parts):
        out_ref[i * rank : (i + 1) * rank, :] = part[:rank, :]
        top += part[rank:, :].astype(jnp.float32)
    top = top.astype(jnp.bfloat16)
    out_ref[count * rank :, :] = top
    top_ref[...] = top


def down_kernel(leaf_size, inner_size, *refs):
    far_ids, far_count, own, before, after = refs[:5]
    tops = dict(zip(range(2, leaf_size - 1), refs[5:]))
    couple, mid_couple, mid_map, leaf_map, out_ref, window = refs[5 + len(tops) :]
    rank = mid_map.shape[1]
    group = lax.axis_index("leaf")
    inner = lax.axis_index("inner")
    last = inner_size * rank
    top_down = jnp.zeros((rank, own.shape[1]), jnp.float32)
    for shift in range(1, leaf_size):
        source = lax.rem(group - shift + leaf_size, leaf_size)
        if shift == 1:
            top = before[last:, :]
        elif shift == leaf_size - 1:
            top = after[last:, :]
        else:
            top = tops[shift][...]
        term = dot(couple[0, source], top)
        top_down += jnp.where(jnp.abs(source - group) >= 2, term, 0.0)
    for i, part in enumerate((before, own, after)):
        window[i * last : (i + 1) * last, :] = part[:last, :]
    total = dot(mid_map[0], top_down.astype(jnp.bfloat16))
    for slot in range(mid_couple.shape[1]):
        live = slot < far_count[0]
        partner = jnp.where(live, far_ids[0, slot], group * inner_size)
        side = partner // inner_size - group + 1
        place = lax.rem(inner - lax.rem(partner, inner_size) + inner_size, inner_size)
        at = pl.multiple_of((side * inner_size + place) * rank, rank)
        term = dot(mid_couple[0, slot], window[pl.ds(at, rank), :])
        total += jnp.where(live, term, 0.0)
    total = total.astype(jnp.bfloat16)
    for leaf in range(leaf_map.shape[0]):
        out_ref[leaf * rank : (leaf + 1) * rank, :] = dot(leaf_map[leaf], total).astype(jnp.bfloat16)


def listed(ids_ref, slot_list, place_list, ends, place_of):
    leaves, near = ids_ref.shape
    first = (lax.axis_index("leaf") * lax.axis_size("inner") + lax.axis_index("inner")) * leaves

    def one(leaf, count):
        for k in range(near):
            at_hand, place = place_of(ids_ref[leaf, k] - first)
            slot_list[count] = leaf * near + k
            place_list[count] = place
            count += at_hand.astype(jnp.int32)
        ends[leaf] = count
        return count

    return lax.fori_loop(0, leaves, one, 0)


def near_products(blocks_ref, near, lists, count, buffer, sems, start_ready, leaf_done, x_ref, total):
    slot_list, place_list, ends = lists
    depth, rows, _ = buffer.shape
    leaves = blocks_ref.shape[0]

    def copy(i):
        slot = slot_list[i]
        at = lax.rem(i, depth)
        return pltpu.make_async_copy(blocks_ref.at[slot // near, lax.rem(slot, near)], buffer.at[at], sems.at[at])

    def begin(i, carry):
        copy(i).start()
        return carry

    lax.fori_loop(0, jnp.minimum(count, depth), begin, 0)
    start_ready()

    def one(leaf, begin_at):
        end_at = ends[leaf]

        def product(i, carry):
            copy(i).wait()
            at = pl.multiple_of(place_list[i] * rows, rows)
            here = pl.ds(pl.multiple_of(leaf * rows, rows), rows)
            total[here, :] += dot(buffer[lax.rem(i, depth)], x_ref[pl.ds(at, rows), :])

            @pl.when(i + depth < count)
            def _():
                copy(i + depth).start()

            return carry

        lax.fori_loop(begin_at, end_at, product, 0)
        leaf_done(leaf)
        return end_at

    lax.fori_loop(0, leaves, one, 0)


def own_kernel(ids_ref, x_ref, blocks_ref, total, slot_list, place_list, ends, buffer, sems):
    leaves, near = ids_ref.shape

    def place_of(offset):
        return (offset >= 0) & (offset < leaves), offset

    lists = (slot_list, place_list, ends)
    count = listed(ids_ref, *lists, place_of)

    def clear():
        total[...] = jnp.zeros_like(total)

    near_products(blocks_ref, near, lists, count, buffer, sems, clear, lambda leaf: None, x_ref, total)


def close_kernel(ids_ref, before, after, blocks_ref, sum_ref, down_ref, basis_ref, total, slot_list, place_list, ends, buffer, sems, x_ref, x_sems):
    leaves, near = ids_ref.shape
    half = leaves // 2
    rank, rows = basis_ref.shape[1:]

    def place_of(offset):
        ahead = offset >= leaves
        ok = ((offset < 0) & (offset >= -half)) | (ahead & (offset < leaves + half))
        return ok, jnp.where(ahead, offset - leaves + half, offset + half)

    lists = (slot_list, place_list, ends)
    count = listed(ids_ref, *lists, place_of)

    def ready():
        cut = half * rows
        one = pltpu.make_async_copy(before, x_ref.at[:cut], x_sems.at[0])
        two = pltpu.make_async_copy(after, x_ref.at[cut:], x_sems.at[1])
        one.start()
        two.start()
        for leaf in range(leaves):
            here = slice(leaf * rows, (leaf + 1) * rows)
            total[here, :] = sum_ref[here, :] + dot_t(basis_ref[leaf], down_ref[leaf * rank : (leaf + 1) * rank, :])
        one.wait()
        two.wait()

    near_products(blocks_ref, near, lists, count, buffer, sems, ready, lambda leaf: None, x_ref, total)


def last_kernel(ids_ref, before, after, blocks_ref, sum_ref, out_ref, slot_list, place_list, ends, buffer, sems, x_ref, x_sems, total, result, out_sems):
    leaves, near = ids_ref.shape
    half = leaves // 2
    rows = buffer.shape[1]

    def place_of(offset):
        ahead = offset >= leaves
        ok = (offset < -half) | (offset >= leaves + half)
        return ok, jnp.where(ahead, offset - leaves, offset + leaves)

    lists = (slot_list, place_list, ends)
    cut = half * rows
    loads = (
        pltpu.make_async_copy(sum_ref, total, x_sems.at[2]),
        pltpu.make_async_copy(before, x_ref.at[:cut], x_sems.at[0]),
        pltpu.make_async_copy(after, x_ref.at[cut:], x_sems.at[1]),
    )
    for load in loads:
        load.start()
    count = listed(ids_ref, *lists, place_of)

    def ready():
        for load in loads:
            load.wait()

    def store(leaf):
        here = pl.ds(pl.multiple_of(leaf * rows, rows), rows)
        return pltpu.make_async_copy(result.at[here], out_ref.at[here], out_sems.at[leaf])

    def leaf_done(leaf):
        here = pl.ds(pl.multiple_of(leaf * rows, rows), rows)
        result[here, :] = total[here, :].astype(result.dtype)
        store(leaf).start()

    near_products(blocks_ref, near, lists, count, buffer, sems, ready, leaf_done, x_ref, total)
    for leaf in range(leaves):
        store(leaf).wait()


def local(anomalies, leaf_basis, near_blocks, near_ids, transfer_leaf, transfer_mid, far_ids, far_count, mid_couple, top_couple):
    leaves, rank, rows = leaf_basis.shape
    near = near_blocks.shape[1]
    columns = anomalies.shape[1]
    inner_size = lax.axis_size("inner")
    leaf_size = lax.axis_size("leaf")
    devices = leaf_size * inner_size
    half = leaves // 2
    cut = half * rows
    bf16 = jnp.bfloat16

    def shaped(*shape, dtype=bf16):
        return jax.ShapeDtypeStruct(shape, dtype)

    def shifted(x, axis, size, shift):
        return lax.ppermute(x, axis, [(i, (i + shift) % size) for i in range(size)])

    up = [(i, i + 1) for i in range(devices - 1)]
    down = [(j, i) for i, j in up]
    both = ("leaf", "inner")
    first, second = anomalies[:cut], anomalies[cut:]
    before_close = lax.ppermute(second, both, up)
    after_close = lax.ppermute(first, both, down)

    part = call(up_kernel, shaped(2 * rank, columns), [VMEM] * 4, VMEM, [], 2 * rows * rank * leaves * columns, anomalies.size * 3, 16 * MIB)(
        anomalies, leaf_basis, transfer_leaf, transfer_mid
    )
    parts = [part] + [shifted(part, "inner", inner_size, s) for s in range(1, inner_size)]

    first, second, _ = lax.optimization_barrier((first, second, part))
    before_far = lax.ppermute(first, both, up)
    after_far = lax.ppermute(second, both, down)

    def scratch(depth):
        slots = leaves * near + 1
        return [
            pltpu.SMEM((slots,), jnp.int32),
            pltpu.SMEM((slots,), jnp.int32),
            pltpu.SMEM((leaves,), jnp.int32),
            pltpu.VMEM((depth, rows, rows), bf16),
            pltpu.SemaphoreType.DMA((depth,)),
        ]

    wide = shaped(leaves * rows, columns, dtype=jnp.float32)
    flops = 2 * rows * rows * columns
    own_sum = call(own_kernel, wide, [SMEM, VMEM, HBM], VMEM, scratch(8), 20 * flops, 20 * rows * rows * 2, 16 * MIB)(
        near_ids, anomalies, near_blocks
    )

    group, top = call(functools.partial(group_kernel, inner_size), (shaped((inner_size + 1) * rank, columns), shaped(rank, columns)), [VMEM] * inner_size, (VMEM, VMEM), [], 1000, 1000, 16 * MIB)(*parts)
    before_group = shifted(group, "leaf", leaf_size, 1)
    after_group = shifted(group, "leaf", leaf_size, leaf_size - 1)
    tops = [shifted(top, "leaf", leaf_size, s) for s in range(2, leaf_size - 1)]
    leaf_down = call(
        functools.partial(down_kernel, leaf_size, inner_size),
        shaped(leaves * rank, columns),
        [SMEM, SMEM] + [VMEM] * (7 + len(tops)),
        VMEM,
        [pltpu.VMEM((3 * inner_size * rank, columns), bf16)],
        1000,
        1000,
        16 * MIB,
    )(far_ids, far_count, group, before_group, after_group, *tops, top_couple, mid_couple, transfer_mid, transfer_leaf)

    close_scratch = scratch(8) + [pltpu.VMEM((2 * cut, columns), bf16), pltpu.SemaphoreType.DMA((3,))]
    close_sum = call(close_kernel, wide, [SMEM, ANY, ANY, HBM, VMEM, VMEM, VMEM], VMEM, close_scratch, 12 * flops, 12 * rows * rows * 2, 24 * MIB)(
        near_ids, before_close, after_close, near_blocks, own_sum, leaf_down, leaf_basis
    )
    last_scratch = scratch(16) + [
        pltpu.VMEM((2 * cut, columns), bf16),
        pltpu.SemaphoreType.DMA((3,)),
        pltpu.VMEM((leaves * rows, columns), jnp.float32),
        pltpu.VMEM((leaves * rows, columns), bf16),
        pltpu.SemaphoreType.DMA((leaves,)),
    ]
    return call(last_kernel, shaped(leaves * rows, columns), [SMEM, ANY, ANY, HBM, ANY], ANY, last_scratch, 6 * flops, 6 * rows * rows * 2, 24 * MIB)(
        near_ids, before_far, after_far, near_blocks, close_sum
    )


def solution(mesh):
    return jax.shard_map(
        local,
        mesh=mesh,
        in_specs=(
            P(("leaf", "inner"), "groups"),
            P(("leaf", "inner"), None, None),
            P(("leaf", "inner"), None, None, None),
            P(("leaf", "inner"), None),
            P(("leaf", "inner"), None, None),
            P(("leaf", "inner"), None, None),
            P(("leaf", "inner"), None),
            P(("leaf", "inner")),
            P(("leaf", "inner"), None, None, None),
            P("leaf", None, None, None),
        ),
        out_specs=P(("leaf", "inner"), "groups"),
        check_vma=False,
    )
```

```python
import functools

import jax
import jax.numpy as jnp
from jax import lax
from jax.experimental import pallas as pl
from jax.experimental.pallas import tpu as pltpu
from jax.sharding import PartitionSpec as P

VMEM_GRANT = 46 << 20
VMEM = pl.BlockSpec(memory_space=pltpu.VMEM)
SMEM = pl.BlockSpec(memory_space=pltpu.SMEM)
ANY = pl.BlockSpec(memory_space=pl.ANY)


def dot(a, b):
    return lax.dot_general(a, b, (((1,), (0,)), ((), ())), preferred_element_type=jnp.float32)


def dot_t(a, b):
    return lax.dot_general(a, b, (((0,), (0,)), ((), ())), preferred_element_type=jnp.float32)


def call(kernel, out_shape, in_specs, out_specs, scratch, flops, moved, vmem):
    return pl.pallas_call(
        kernel,
        out_shape=out_shape,
        in_specs=in_specs,
        out_specs=out_specs,
        scratch_shapes=scratch,
        cost_estimate=pl.CostEstimate(flops=flops, bytes_accessed=moved, transcendentals=0),
        compiler_params=pltpu.CompilerParams(vmem_limit_bytes=vmem),
    )


def up_kernel(x_ref, basis_ref, leaf_map_ref, mid_map_ref, out_ref):
    leaves, rank, rows = basis_ref.shape
    mid = jnp.zeros((rank, x_ref.shape[1]), jnp.float32)
    for leaf in range(leaves):
        skeleton = dot(basis_ref[leaf], x_ref[leaf * rows : (leaf + 1) * rows, :])
        mid += dot_t(leaf_map_ref[leaf], skeleton.astype(jnp.bfloat16))
    mid = mid.astype(jnp.bfloat16)
    out_ref[:rank, :] = mid
    out_ref[rank:, :] = dot_t(mid_map_ref[0], mid).astype(jnp.bfloat16)


def group_kernel(count, parts_ref, out_ref, top_ref):
    rank = top_ref.shape[0]
    top = jnp.zeros(top_ref.shape, jnp.float32)
    for i in range(count):
        out_ref[i * rank : (i + 1) * rank, :] = parts_ref[2 * i * rank : (2 * i + 1) * rank, :]
        top += parts_ref[(2 * i + 1) * rank : (2 * i + 2) * rank, :].astype(jnp.float32)
    top = top.astype(jnp.bfloat16)
    out_ref[count * rank :, :] = top
    top_ref[...] = top


def down_kernel(leaf_size, inner_size, *refs):
    far_ids, far_count, own, before, after = refs[:5]
    tops = dict(zip(range(2, leaf_size - 1), refs[5:]))
    couple, mid_couple, mid_map, leaf_map, out_ref, window = refs[5 + len(tops) :]
    rank = mid_map.shape[1]
    group = lax.axis_index("leaf")
    inner = lax.axis_index("inner")
    last = inner_size * rank
    top_down = jnp.zeros((rank, own.shape[1]), jnp.float32)
    for shift in range(1, leaf_size):
        source = lax.rem(group - shift + leaf_size, leaf_size)
        if shift == 1:
            top = before[last:, :]
        elif shift == leaf_size - 1:
            top = after[last:, :]
        else:
            top = tops[shift][...]
        term = dot(couple[0, source], top)
        top_down += jnp.where(jnp.abs(source - group) >= 2, term, 0.0)
    for i, part in enumerate((before, own, after)):
        window[i * last : (i + 1) * last, :] = part[:last, :]
    total = dot(mid_map[0], top_down.astype(jnp.bfloat16))
    for slot in range(mid_couple.shape[1]):
        live = slot < far_count[0]
        partner = jnp.where(live, far_ids[0, slot], group * inner_size)
        side = partner // inner_size - group + 1
        place = inner ^ lax.rem(partner, inner_size)
        at = pl.multiple_of((side * inner_size + place) * rank, rank)
        term = dot(mid_couple[0, slot], window[pl.ds(at, rank), :])
        total += jnp.where(live, term, 0.0)
    total = total.astype(jnp.bfloat16)
    for leaf in range(leaf_map.shape[0]):
        out_ref[leaf * rank : (leaf + 1) * rank, :] = dot(leaf_map[leaf], total).astype(jnp.bfloat16)


def listed(ids_ref, slot_list, place_list, ends, place_of):
    leaves, near = ids_ref.shape
    first = (lax.axis_index("leaf") * lax.axis_size("inner") + lax.axis_index("inner")) * leaves

    def one(leaf, count):
        for k in range(near):
            at_hand, place = place_of(ids_ref[leaf, k] - first)
            slot_list[count] = leaf * near + k
            place_list[count] = place
            count += at_hand.astype(jnp.int32)
        ends[leaf] = count
        return count

    return lax.fori_loop(0, leaves, one, 0)


def near_products(blocks_ref, near, lists, count, buffer, sems, start_ready, leaf_done, x_ref, total):
    slot_list, place_list, ends = lists
    depth, rows, _ = buffer.shape
    leaves = blocks_ref.shape[0]

    def copy(i):
        slot = slot_list[i]
        at = lax.rem(i, depth)
        return pltpu.make_async_copy(blocks_ref.at[slot // near, lax.rem(slot, near)], buffer.at[at], sems.at[at])

    def begin(i, carry):
        copy(i).start()
        return carry

    lax.fori_loop(0, jnp.minimum(count, depth), begin, 0)
    start_ready()

    def one(leaf, begin_at):
        end_at = ends[leaf]

        def product(i, carry):
            copy(i).wait()
            at = pl.multiple_of(place_list[i] * rows, rows)
            here = pl.ds(pl.multiple_of(leaf * rows, rows), rows)
            total[here, :] += dot(buffer[lax.rem(i, depth)], x_ref[pl.ds(at, rows), :])

            @pl.when(i + depth < count)
            def _():
                copy(i + depth).start()

            return carry

        lax.fori_loop(begin_at, end_at, product, 0)
        leaf_done(leaf)
        return end_at

    lax.fori_loop(0, leaves, one, 0)


def own_kernel(ids_ref, x_ref, blocks_ref, total, slot_list, place_list, ends, buffer, sems):
    leaves, near = ids_ref.shape

    def place_of(offset):
        return (offset >= 0) & (offset < leaves), offset

    lists = (slot_list, place_list, ends)
    count = listed(ids_ref, *lists, place_of)

    def clear():
        total[...] = jnp.zeros_like(total)

    near_products(blocks_ref, near, lists, count, buffer, sems, clear, lambda leaf: None, x_ref, total)


def close_kernel(early, step, ids_ref, *refs):
    parts = refs[: 2 * early]
    blocks_ref, sum_ref, down_ref, basis_ref, total, slot_list, place_list, ends, buffer, sems, x_ref, x_sems = refs[2 * early :]
    leaves, near = ids_ref.shape
    rank, rows = basis_ref.shape[1:]
    size = step * rows
    reach = early * step

    def place_of(offset):
        ahead = offset >= leaves
        ok = ((offset < 0) & (offset >= -reach)) | (ahead & (offset < leaves + reach))
        return ok, jnp.where(ahead, offset - leaves + reach, offset + reach)

    loads = []
    for wave in range(early):
        for side, place in enumerate((early - 1 - wave, early + wave)):
            index = 2 * wave + side
            loads.append(pltpu.make_async_copy(parts[index], x_ref.at[place * size : (place + 1) * size], x_sems.at[index]))
    for load in loads:
        load.start()
    lists = (slot_list, place_list, ends)
    count = listed(ids_ref, *lists, place_of)

    def ready():
        for leaf in range(leaves):
            here = slice(leaf * rows, (leaf + 1) * rows)
            total[here, :] = sum_ref[here, :] + dot_t(basis_ref[leaf], down_ref[leaf * rank : (leaf + 1) * rank, :])
        for load in loads:
            load.wait()

    near_products(blocks_ref, near, lists, count, buffer, sems, ready, lambda leaf: None, x_ref, total)


def last_kernel(step, ids_ref, before, after, blocks_ref, sum_ref, out_ref, slot_list, place_list, ends, buffer, sems, x_ref, x_sems, total, result, out_sems):
    leaves, near = ids_ref.shape
    rows = buffer.shape[1]
    size = step * rows

    def place_of(offset):
        ok = (offset < step - leaves) | (offset >= 2 * leaves - step)
        return ok, jnp.where(offset >= leaves, offset - 2 * leaves + 2 * step, offset + leaves)

    lists = (slot_list, place_list, ends)
    loads = (
        pltpu.make_async_copy(sum_ref, total, x_sems.at[2]),
        pltpu.make_async_copy(before, x_ref.at[:size], x_sems.at[0]),
        pltpu.make_async_copy(after, x_ref.at[size:], x_sems.at[1]),
    )
    for load in loads:
        load.start()
    count = listed(ids_ref, *lists, place_of)

    def ready():
        for load in loads:
            load.wait()

    def store(leaf):
        here = pl.ds(pl.multiple_of(leaf * rows, rows), rows)
        return pltpu.make_async_copy(result.at[here], out_ref.at[here], out_sems.at[leaf])

    def leaf_done(leaf):
        here = pl.ds(pl.multiple_of(leaf * rows, rows), rows)
        result[here, :] = total[here, :].astype(result.dtype)
        store(leaf).start()

    near_products(blocks_ref, near, lists, count, buffer, sems, ready, leaf_done, x_ref, total)
    for leaf in range(leaves):
        store(leaf).wait()


def local(anomalies, leaf_basis, near_blocks, near_ids, transfer_leaf, transfer_mid, far_ids, far_count, mid_couple, top_couple):
    leaves, rank, rows = leaf_basis.shape
    near = near_blocks.shape[1]
    columns = anomalies.shape[1]
    inner_size = lax.axis_size("inner")
    leaf_size = lax.axis_size("leaf")
    devices = leaf_size * inner_size
    bf16 = jnp.bfloat16
    waves = 4
    step = leaves // waves

    def shaped(*shape, dtype=bf16):
        return jax.ShapeDtypeStruct(shape, dtype)

    def shifted(x, axis, size, shift):
        return lax.ppermute(x, axis, [(i, (i + shift) % size) for i in range(size)])

    up = [(i, i + 1) for i in range(devices - 1)]
    down = [(j, i) for i, j in up]

    size = step * rows
    quarters = [lax.slice_in_dim(anomalies, i * size, (i + 1) * size) for i in range(waves)]

    def halo_parts(number):
        return quarters[waves - 1 - number], quarters[number]

    def wave(x, number):
        ahead = lax.ppermute(lax.slice_in_dim(x, (waves - 1 - number) * size, (waves - number) * size), ("leaf", "inner"), up)
        back = lax.ppermute(lax.slice_in_dim(x, number * size, (number + 1) * size), ("leaf", "inner"), down)
        return ahead, back

    def scratch(depth):
        slots = leaves * near + 1
        return [
            pltpu.SMEM((slots,), jnp.int32),
            pltpu.SMEM((slots,), jnp.int32),
            pltpu.SMEM((leaves,), jnp.int32),
            pltpu.VMEM((depth, rows, rows), bf16),
            pltpu.SemaphoreType.DMA((depth,)),
        ]

    halo = [wave(anomalies, 0)]
    x_up, _ = lax.optimization_barrier((anomalies, halo_parts(0)))
    part = call(up_kernel, shaped(2 * rank, columns), [VMEM] * 4, VMEM, [], 2 * rows * rank * leaves * columns, anomalies.size * 3, VMEM_GRANT)(
        x_up, leaf_basis, transfer_leaf, transfer_mid
    )
    later, gathered = lax.optimization_barrier((anomalies, part))
    halo.append(wave(later, 1))
    reach = 1
    while reach < inner_size:
        partner = lax.ppermute(gathered, "inner", [(i, i ^ reach) for i in range(inner_size)])
        partner, gathered, halo[0] = lax.optimization_barrier((partner, gathered, halo[0]))
        gathered = jnp.concatenate([gathered, partner])
        if reach == 1:
            later, gathered = lax.optimization_barrier((anomalies, gathered))
            halo.append(wave(later, 2))
        reach *= 2
    gathered, halo[1] = lax.optimization_barrier((gathered, halo[1]))
    group, top = call(functools.partial(group_kernel, inner_size), (shaped((inner_size + 1) * rank, columns), shaped(rank, columns)), [VMEM], (VMEM, VMEM), [], 1000, 1000, VMEM_GRANT)(gathered)
    later, group, top = lax.optimization_barrier((anomalies, group, top))
    before_group = shifted(group, "leaf", leaf_size, 1)
    after_group = shifted(group, "leaf", leaf_size, leaf_size - 1)
    tops = [shifted(top, "leaf", leaf_size, s) for s in range(2, leaf_size - 1)]
    halo.append(wave(later, 3))

    wide = shaped(leaves * rows, columns, dtype=jnp.float32)
    flops = 2 * rows * rows * columns
    x_own, _ = lax.optimization_barrier((anomalies, group))
    own_sum = call(own_kernel, wide, [SMEM, VMEM, ANY], VMEM, scratch(8), 20 * flops, 20 * rows * rows * 2, VMEM_GRANT)(
        near_ids, x_own, near_blocks
    )
    leaf_down = call(
        functools.partial(down_kernel, leaf_size, inner_size),
        shaped(leaves * rank, columns),
        [SMEM, SMEM] + [VMEM] * (7 + len(tops)),
        VMEM,
        [pltpu.VMEM((3 * inner_size * rank, columns), bf16)],
        1000,
        1000,
        VMEM_GRANT,
    )(far_ids, far_count, group, before_group, after_group, *tops, top_couple, mid_couple, transfer_mid, transfer_leaf)

    early = waves - 1
    close_scratch = scratch(16) + [pltpu.VMEM((2 * early * step * rows, columns), bf16), pltpu.SemaphoreType.DMA((2 * early,))]
    close_sum = call(functools.partial(close_kernel, early, step), wide, [SMEM] + [ANY] * (2 * early + 1) + [VMEM] * 3, VMEM, close_scratch, 16 * flops, 16 * rows * rows * 2, VMEM_GRANT)(
        near_ids, *[x for pair in halo[:early] for x in pair], near_blocks, own_sum, leaf_down, leaf_basis
    )
    last_scratch = scratch(16) + [
        pltpu.VMEM((2 * step * rows, columns), bf16),
        pltpu.SemaphoreType.DMA((3,)),
        pltpu.VMEM((leaves * rows, columns), jnp.float32),
        pltpu.VMEM((leaves * rows, columns), bf16),
        pltpu.SemaphoreType.DMA((leaves,)),
    ]
    return call(functools.partial(last_kernel, step), shaped(leaves * rows, columns), [SMEM, ANY, ANY, ANY, ANY], ANY, last_scratch, 6 * flops, 6 * rows * rows * 2, VMEM_GRANT)(
        near_ids, *halo[early], near_blocks, close_sum
    )


def solution(mesh):
    return jax.shard_map(
        local,
        mesh=mesh,
        in_specs=(
            P(("leaf", "inner"), "groups"),
            P(("leaf", "inner"), None, None),
            P(("leaf", "inner"), None, None, None),
            P(("leaf", "inner"), None),
            P(("leaf", "inner"), None, None),
            P(("leaf", "inner"), None, None),
            P(("leaf", "inner"), None),
            P(("leaf", "inner")),
            P(("leaf", "inner"), None, None, None),
            P("leaf", None, None, None),
        ),
        out_specs=P(("leaf", "inner"), "groups"),
        check_vma=False,
    )
```

```python
import functools

import jax
import jax.numpy as jnp
from jax import lax
from jax.experimental import pallas as pl
from jax.experimental.pallas import tpu as pltpu
from jax.sharding import PartitionSpec as P

MIB = 1 << 20
VMEM = pl.BlockSpec(memory_space=pltpu.VMEM)
SMEM = pl.BlockSpec(memory_space=pltpu.SMEM)
ANY = pl.BlockSpec(memory_space=pl.ANY)


def held(x, space):
    return pltpu.with_memory_space_constraint(x, space)


def resident(*shape):
    return pltpu.VMEM(shape, jnp.bfloat16)


def dot(a, b):
    return lax.dot_general(a, b, (((1,), (0,)), ((), ())), preferred_element_type=jnp.float32)


def dot_t(a, b):
    return lax.dot_general(a, b, (((0,), (0,)), ((), ())), preferred_element_type=jnp.float32)


def call(kernel, out_shape, in_specs, out_specs, scratch, flops, moved, vmem, aliases=None):
    return pl.pallas_call(
        kernel,
        out_shape=out_shape,
        in_specs=in_specs,
        out_specs=out_specs,
        scratch_shapes=scratch,
        cost_estimate=pl.CostEstimate(flops=flops, bytes_accessed=moved, transcendentals=0),
        compiler_params=pltpu.CompilerParams(vmem_limit_bytes=vmem),
        input_output_aliases=aliases or {},
    )


def up_kernel(early, x_ref, basis_ref, leaf_map_ref, mid_map_ref, out_ref, *refs):
    pieces, (x, basis, leaf_map, mid_map, sems, piece_sems) = refs[:4], refs[4:]
    leaves, rank, rows = basis.shape
    loads = [pltpu.make_async_copy(leaf_map_ref, leaf_map, sems.at[leaves]), pltpu.make_async_copy(mid_map_ref, mid_map, sems.at[leaves + 1])]
    parts = []
    for leaf in range(leaves):
        here = slice(leaf * rows, (leaf + 1) * rows)
        parts.append(pltpu.make_async_copy(x_ref.at[here], x.at[here], sems.at[leaf]))
        parts.append(pltpu.make_async_copy(basis_ref.at[leaf], basis.at[leaf], sems.at[leaves + 2 + leaf]))
    for load in parts[:2] + loads + parts[2:]:
        load.start()
    cuts = ((leaves - early, leaves), (0, early), (0, leaves - early), (early, leaves))
    copies = [pltpu.make_async_copy(x_ref.at[a * rows : b * rows], piece, piece_sems.at[i]) for i, (piece, (a, b)) in enumerate(zip(pieces, cuts))]
    for copy in copies:
        copy.start()
    mid = jnp.zeros((rank, x.shape[1]), jnp.float32)
    for leaf in range(leaves):
        parts[2 * leaf].wait()
        parts[2 * leaf + 1].wait()
        if leaf == 0:
            loads[0].wait()
        skeleton = dot(basis[leaf], x[leaf * rows : (leaf + 1) * rows, :])
        mid += dot_t(leaf_map[leaf], skeleton.astype(jnp.bfloat16))
    loads[1].wait()
    mid = mid.astype(jnp.bfloat16)
    out_ref[:rank, :] = mid
    out_ref[rank:, :] = dot_t(mid_map[0], mid).astype(jnp.bfloat16)
    for copy in copies:
        copy.wait()


def gate_kernel(*refs):
    pass


def group_kernel(count, parts_ref, out_ref, top_ref):
    rank = top_ref.shape[0]
    top = jnp.zeros(top_ref.shape, jnp.float32)
    for i in range(count):
        out_ref[i * rank : (i + 1) * rank, :] = parts_ref[2 * i * rank : (2 * i + 1) * rank, :]
        top += parts_ref[(2 * i + 1) * rank : (2 * i + 2) * rank, :].astype(jnp.float32)
    top = top.astype(jnp.bfloat16)
    out_ref[count * rank :, :] = top
    top_ref[...] = top


def down_kernel(leaf_size, inner_size, *refs):
    far_ids, far_count, own, before, after = refs[:5]
    tops = dict(zip(range(2, leaf_size - 1), refs[5:]))
    couple, mid_couple, mid_map, leaf_map, out_ref, window = refs[5 + len(tops) :]
    rank = mid_map.shape[1]
    group = lax.axis_index("leaf")
    inner = lax.axis_index("inner")
    last = inner_size * rank
    top_down = jnp.zeros((rank, own.shape[1]), jnp.float32)
    for shift in range(1, leaf_size):
        source = lax.rem(group - shift + leaf_size, leaf_size)
        if shift == 1:
            top = before[last:, :]
        elif shift == leaf_size - 1:
            top = after[last:, :]
        else:
            top = tops[shift][...]
        term = dot(couple[0, source], top)
        top_down += jnp.where(jnp.abs(source - group) >= 2, term, 0.0)
    for i, part in enumerate((before, own, after)):
        window[i * last : (i + 1) * last, :] = part[:last, :]
    total = dot(mid_map[0], top_down.astype(jnp.bfloat16))
    for slot in range(mid_couple.shape[1]):
        live = slot < far_count[0]
        partner = jnp.where(live, far_ids[0, slot], group * inner_size)
        side = partner // inner_size - group + 1
        place = inner ^ lax.rem(partner, inner_size)
        at = pl.multiple_of((side * inner_size + place) * rank, rank)
        term = dot(mid_couple[0, slot], window[pl.ds(at, rank), :])
        total += jnp.where(live, term, 0.0)
    total = total.astype(jnp.bfloat16)
    for leaf in range(leaf_map.shape[0]):
        out_ref[leaf * rank : (leaf + 1) * rank, :] = dot(leaf_map[leaf], total).astype(jnp.bfloat16)


def listed(ids_ref, lists, kind_of):
    leaves, near = ids_ref.shape
    first = (lax.axis_index("leaf") * lax.axis_size("inner") + lax.axis_index("inner")) * leaves

    def one(leaf, counts):
        for k in range(near):
            offset = ids_ref[leaf, k] - first
            grown = []
            for (slots, places), count, (member, place) in zip(lists, counts, kind_of(offset)):
                slots[count] = leaf * near + k
                places[count] = place
                grown.append(count + member.astype(jnp.int32))
            counts = tuple(grown)
        return counts

    return lax.fori_loop(0, leaves, one, (jnp.int32(0),) * len(lists))


def add_products(near, kind, count, blocks, x_ref, total, arrived=lambda slot: None):
    slots, places = kind
    rows = blocks.shape[1]

    def product(i):
        slot = slots[i]
        arrived(slot)
        at = pl.multiple_of(places[i] * rows, rows)
        here = pl.ds(pl.multiple_of(slot // near * rows, rows), rows)
        return here, dot(blocks[slot], x_ref[pl.ds(at, rows), :])

    def pair(j, carry):
        one, first = product(2 * j)
        two, second = product(2 * j + 1)
        total[one, :] += first
        total[two, :] += second
        return carry

    lax.fori_loop(0, count // 2, pair, 0)

    @pl.when(lax.rem(count, 2) == 1)
    def _():
        here, term = product(count - 1)
        total[here, :] += term


def own_kernel(ids_ref, x_any, blocks_ref, total, blocks, own_slots, own_places, other_slots, other_places, x_ref, x_sem, sems):
    leaves, near = ids_ref.shape
    load = pltpu.make_async_copy(x_any, x_ref, x_sem)
    load.start()

    def kind_of(offset):
        own = (offset >= 0) & (offset < leaves)
        return (own, offset), (jnp.logical_not(own), 0)

    kinds = ((own_slots, own_places), (other_slots, other_places))
    own_count, other_count = listed(ids_ref, kinds, kind_of)

    def copy(slot):
        return pltpu.make_async_copy(blocks_ref.at[slot], blocks.at[slot], sems.at[slot])

    def begin(slots):
        def one(i, carry):
            copy(slots[i]).start()
            return carry

        return one

    lax.fori_loop(0, own_count, begin(own_slots), 0)
    lax.fori_loop(0, other_count, begin(other_slots), 0)
    total[...] = jnp.zeros_like(total)
    load.wait()
    add_products(near, kinds[0], own_count, blocks, x_ref, total, lambda slot: copy(slot).wait())

    def finish(i, carry):
        copy(other_slots[i]).wait()
        return carry

    lax.fori_loop(0, other_count, finish, 0)


def close_kernel(early, ids_ref, before, after, blocks, sum_ref, down_ref, basis_ref, total, *lists):
    leaves, near = ids_ref.shape
    rank, rows = basis_ref.shape[1:]

    def kind_of(offset):
        return ((offset < 0) & (offset >= -early), offset + early), ((offset >= leaves) & (offset < leaves + early), offset - leaves)

    kinds = (lists[:2], lists[2:])
    counts = listed(ids_ref, kinds, kind_of)
    for leaf in range(leaves):
        here = slice(leaf * rows, (leaf + 1) * rows)
        total[here, :] = sum_ref[here, :] + dot_t(basis_ref[leaf], down_ref[leaf * rank : (leaf + 1) * rank, :])
    for kind, count, x_ref in zip(kinds, counts, (before, after)):
        add_products(near, kind, count, blocks, x_ref, total)


def last_kernel(early, ids_ref, before, after, blocks, sum_ref, out_ref, *refs):
    lists, (total, result, sems) = refs[:4], refs[4:]
    leaves, near = ids_ref.shape
    rows = blocks.shape[1]

    def kind_of(offset):
        return (offset < -early, offset + leaves), (offset >= leaves + early, offset - leaves - early)

    kinds = (lists[:2], lists[2:])
    counts = listed(ids_ref, kinds, kind_of)
    total[...] = sum_ref[...]
    for kind, count, x_ref in zip(kinds, counts, (before, after)):
        add_products(near, kind, count, blocks, x_ref, total)
    stores = []
    for leaf in range(leaves):
        here = slice(leaf * rows, (leaf + 1) * rows)
        result[here, :] = total[here, :].astype(result.dtype)
        stores.append(pltpu.make_async_copy(result.at[here], out_ref.at[here], sems.at[leaf]))
        stores[-1].start()
    for store in stores:
        store.wait()


def local(anomalies, leaf_basis, near_blocks, near_ids, transfer_leaf, transfer_mid, far_ids, far_count, mid_couple, top_couple):
    leaves, rank, rows = leaf_basis.shape
    near = near_blocks.shape[1]
    columns = anomalies.shape[1]
    inner_size = lax.axis_size("inner")
    leaf_size = lax.axis_size("leaf")
    devices = leaf_size * inner_size
    bf16 = jnp.bfloat16
    early = leaves - leaves * 3 // 8
    late = leaves - early

    def shaped(*shape, dtype=bf16):
        return jax.ShapeDtypeStruct(shape, dtype)

    def shifted(x, axis, size, shift):
        return lax.ppermute(x, axis, [(i, (i + shift) % size) for i in range(size)])

    up = [(i, i + 1) for i in range(devices - 1)]
    down = [(j, i) for i, j in up]

    def wave(ahead, back):
        return lax.ppermute(ahead, ("leaf", "inner"), up), lax.ppermute(back, ("leaf", "inner"), down)

    x_hbm = held(anomalies, pltpu.HBM)
    ids = near_ids
    part, *pieces = call(
        functools.partial(up_kernel, early),
        [resident(2 * rank, columns)] + [shaped(n * rows, columns) for n in (early, early, late, late)],
        [ANY] * 4,
        [VMEM] + [ANY] * 4,
        [
            pltpu.VMEM(anomalies.shape, bf16),
            pltpu.VMEM(leaf_basis.shape, bf16),
            pltpu.VMEM(transfer_leaf.shape, bf16),
            pltpu.VMEM(transfer_mid.shape, bf16),
            pltpu.SemaphoreType.DMA((2 * leaves + 2,)),
            pltpu.SemaphoreType.DMA((4,)),
        ],
        2 * rows * rank * leaves * columns,
        anomalies.size * 3,
        8 * MIB,
    )(x_hbm, *[held(x, pltpu.HBM) for x in (leaf_basis, transfer_leaf, transfer_mid)])

    first_pieces = call(gate_kernel, [shaped(early * rows, columns)] * 2, [ANY] * 3, [ANY] * 2, [], 1000, 1000, 8 * MIB, {1: 0, 2: 1})(part, *pieces[:2])
    gathered = part
    reach = 1
    while reach < inner_size:
        partner = lax.ppermute(gathered, "inner", [(i, i ^ reach) for i in range(inner_size)])
        if reach == 1:
            partner, first_pieces = lax.optimization_barrier((partner, first_pieces))
        gathered = jnp.concatenate([gathered, partner])
        if reach == 1:
            gathered, x_own, last_pieces = lax.optimization_barrier((gathered, anomalies, pieces[2:]))
            near_halo = wave(*first_pieces)
            far_halo = wave(*last_pieces)
        reach *= 2

    slots = leaves * near
    lists = [pltpu.SMEM((slots + 1,), jnp.int32)] * 4
    wide = shaped(leaves * rows, columns, dtype=jnp.float32)
    flops = 2 * rows * rows * columns
    own_sum, blocks = call(
        own_kernel,
        (wide, resident(slots, rows, rows)),
        [SMEM, ANY, ANY],
        (VMEM, VMEM),
        lists + [pltpu.VMEM(anomalies.shape, bf16), pltpu.SemaphoreType.DMA, pltpu.SemaphoreType.DMA((slots,))],
        20 * flops,
        slots * rows * rows * 4,
        12 * MIB,
    )(ids, held(x_own, pltpu.HBM), held(near_blocks.reshape(slots, rows, rows), pltpu.HBM))

    blocks = held(blocks, pltpu.VMEM)
    gathered, near_halo, own_sum = lax.optimization_barrier((gathered, near_halo, own_sum))
    group, top = call(functools.partial(group_kernel, inner_size), (shaped((inner_size + 1) * rank, columns), shaped(rank, columns)), [VMEM], (VMEM, VMEM), [], 1000, 1000, 8 * MIB)(gathered)
    before_group = shifted(group, "leaf", leaf_size, 1)
    after_group = shifted(group, "leaf", leaf_size, leaf_size - 1)
    tops = [shifted(top, "leaf", leaf_size, s) for s in range(2, leaf_size - 1)]
    leaf_down = call(
        functools.partial(down_kernel, leaf_size, inner_size),
        shaped(leaves * rank, columns),
        [SMEM, SMEM] + [VMEM] * (7 + len(tops)),
        VMEM,
        [pltpu.VMEM((3 * inner_size * rank, columns), bf16)],
        1000,
        1000,
        8 * MIB,
    )(far_ids, far_count, group, before_group, after_group, *tops, top_couple, mid_couple, transfer_mid, transfer_leaf)

    close_sum = call(functools.partial(close_kernel, early), wide, [SMEM] + [VMEM] * 6, VMEM, lists, 15 * flops, 15 * rows * rows * 2, 8 * MIB)(
        ids, *near_halo, blocks, own_sum, leaf_down, leaf_basis
    )
    last_scratch = lists + [
        pltpu.VMEM((leaves * rows, columns), jnp.float32),
        pltpu.VMEM((leaves * rows, columns), bf16),
        pltpu.SemaphoreType.DMA((leaves,)),
    ]
    return call(functools.partial(last_kernel, early), shaped(leaves * rows, columns), [SMEM] + [VMEM] * 4, ANY, last_scratch, 4 * flops, 4 * rows * rows * 2, 8 * MIB)(
        ids, *far_halo, blocks, close_sum
    )


def solution(mesh):
    return jax.shard_map(
        local,
        mesh=mesh,
        in_specs=(
            P(("leaf", "inner"), "groups"),
            P(("leaf", "inner"), None, None),
            P(("leaf", "inner"), None, None, None),
            P(("leaf", "inner"), None),
            P(("leaf", "inner"), None, None),
            P(("leaf", "inner"), None, None),
            P(("leaf", "inner"), None),
            P(("leaf", "inner")),
            P(("leaf", "inner"), None, None, None),
            P("leaf", None, None, None),
        ),
        out_specs=P(("leaf", "inner"), "groups"),
        check_vma=False,
    )
```

```python
import functools

import jax
import jax.numpy as jnp
from jax import lax
from jax.experimental import pallas as pl
from jax.experimental.pallas import tpu as pltpu
from jax.sharding import PartitionSpec as P

MIB = 1 << 20
VMEM = pl.BlockSpec(memory_space=pltpu.VMEM)
SMEM = pl.BlockSpec(memory_space=pltpu.SMEM)
ANY = pl.BlockSpec(memory_space=pl.ANY)


def held(x, space):
    return pltpu.with_memory_space_constraint(x, space)


def resident(*shape):
    return pltpu.VMEM(shape, jnp.bfloat16)


def dot(a, b):
    return lax.dot_general(a, b, (((1,), (0,)), ((), ())), preferred_element_type=jnp.float32)


def dot_t(a, b):
    return lax.dot_general(a, b, (((0,), (0,)), ((), ())), preferred_element_type=jnp.float32)


def call(kernel, out_shape, in_specs, out_specs, scratch, flops, moved, vmem, aliases=None):
    return pl.pallas_call(
        kernel,
        out_shape=out_shape,
        in_specs=in_specs,
        out_specs=out_specs,
        scratch_shapes=scratch,
        cost_estimate=pl.CostEstimate(flops=flops, bytes_accessed=moved, transcendentals=0),
        compiler_params=pltpu.CompilerParams(vmem_limit_bytes=vmem),
        input_output_aliases=aliases or {},
    )


def up_kernel(x_ref, basis_ref, leaf_map_ref, mid_map_ref, out_ref, low, high, relay, x, basis, leaf_map, mid_map, skeleton, sems, piece_sems):
    leaves, rank, rows = basis.shape
    cut = low.shape[0]
    parts = []
    for leaf in range(leaves):
        here = slice(leaf * rows, (leaf + 1) * rows)
        parts.append(pltpu.make_async_copy(x_ref.at[here], x.at[here], sems.at[leaf]))
        parts.append(pltpu.make_async_copy(basis_ref.at[leaf], basis.at[leaf], sems.at[leaves + leaf]))
    maps = [pltpu.make_async_copy(leaf_map_ref, leaf_map, sems.at[2 * leaves]), pltpu.make_async_copy(mid_map_ref, mid_map, sems.at[2 * leaves + 1])]
    edge = pl.multiple_of(jnp.where(lax.axis_index("inner") == 0, cut, 0), rows)
    sources = (x_ref.at[:cut], x_ref.at[cut:], x_ref.at[pl.ds(edge, cut)])
    copies = [pltpu.make_async_copy(source, piece, piece_sems.at[i]) for i, (source, piece) in enumerate(zip(sources, (low, high, relay)))]
    for copy in parts + maps + copies:
        copy.start()
    for leaf in range(leaves):
        parts[2 * leaf].wait()
        parts[2 * leaf + 1].wait()
        skeleton[leaf * rank : (leaf + 1) * rank, :] = dot(basis[leaf], x[leaf * rows : (leaf + 1) * rows, :]).astype(jnp.bfloat16)
    for copy in maps:
        copy.wait()
    mid = dot_t(leaf_map[...], skeleton[...]).astype(jnp.bfloat16)
    out_ref[:rank, :] = mid
    out_ref[rank:, :] = dot_t(mid_map[...], mid).astype(jnp.bfloat16)
    for copy in copies:
        copy.wait()


def group_kernel(count, *refs):
    parts, out_ref, top_ref = refs[:count], refs[count], refs[count + 1]
    rank = top_ref.shape[0]
    top = jnp.zeros(top_ref.shape, jnp.float32)
    for i, part in enumerate(parts):
        out_ref[i * rank : (i + 1) * rank, :] = part[:rank, :]
        top += part[rank:, :].astype(jnp.float32)
    top = top.astype(jnp.bfloat16)
    out_ref[count * rank :, :] = top
    top_ref[...] = top


def down_kernel(leaf_size, inner_size, *refs):
    far_ids, far_count, own, before, after = refs[:5]
    tops = dict(zip(range(2, leaf_size - 1), refs[5:]))
    couple, mid_couple, mid_map, leaf_map, out_ref, window = refs[5 + len(tops) :]
    rank = mid_map.shape[1]
    group = lax.axis_index("leaf")
    inner = lax.axis_index("inner")
    last = inner_size * rank
    top_down = jnp.zeros((rank, own.shape[1]), jnp.float32)
    for shift in range(1, leaf_size):
        source = lax.rem(group - shift + leaf_size, leaf_size)
        if shift == 1:
            top = before[last:, :]
        elif shift == leaf_size - 1:
            top = after[last:, :]
        else:
            top = tops[shift][...]
        term = dot(couple[0, source], top)
        top_down += jnp.where(jnp.abs(source - group) >= 2, term, 0.0)
    for i, part in enumerate((before, own, after)):
        window[i * last : (i + 1) * last, :] = part[:last, :]
    total = dot(mid_map[0], top_down.astype(jnp.bfloat16))
    for slot in range(mid_couple.shape[1]):
        live = slot < far_count[0]
        partner = jnp.where(live, far_ids[0, slot], group * inner_size)
        side = partner // inner_size - group + 1
        place = inner ^ lax.rem(partner, inner_size)
        at = pl.multiple_of((side * inner_size + place) * rank, rank)
        term = dot(mid_couple[0, slot], window[pl.ds(at, rank), :])
        total += jnp.where(live, term, 0.0)
    total = total.astype(jnp.bfloat16)
    for leaf in range(leaf_map.shape[0]):
        out_ref[leaf * rank : (leaf + 1) * rank, :] = dot(leaf_map[leaf], total).astype(jnp.bfloat16)


def listed(ids_ref, lists, kind_of):
    leaves, near = ids_ref.shape
    first = (lax.axis_index("leaf") * lax.axis_size("inner") + lax.axis_index("inner")) * leaves

    def one(leaf, counts):
        for k in range(near):
            offset = ids_ref[leaf, k] - first
            grown = []
            for (slots, places), count, (member, place) in zip(lists, counts, kind_of(offset)):
                slots[count] = leaf * near + k
                places[count] = place
                grown.append(count + member.astype(jnp.int32))
            counts = tuple(grown)
        return counts

    return lax.fori_loop(0, leaves, one, (jnp.int32(0),) * len(lists))


def add_products(near, kind, count, blocks, partner, total, arrived=lambda slot: None):
    slots, places = kind
    rows = blocks.shape[1]

    def product(i):
        slot = slots[i]
        arrived(slot)
        at = pl.ds(pl.multiple_of(places[i] * rows, rows), rows)
        here = pl.ds(pl.multiple_of(slot // near * rows, rows), rows)
        return here, dot(blocks[slot], partner(at))

    def pair(j, carry):
        one, first = product(2 * j)
        two, second = product(2 * j + 1)
        total[one, :] += first
        total[two, :] += second
        return carry

    lax.fori_loop(0, count // 2, pair, 0)

    @pl.when(lax.rem(count, 2) == 1)
    def _():
        here, term = product(count - 1)
        total[here, :] += term


def own_kernel(ids_ref, x_any, blocks_ref, total, blocks, own_slots, own_places, other_slots, other_places, x_ref, x_sem, sems):
    leaves, near = ids_ref.shape
    load = pltpu.make_async_copy(x_any, x_ref, x_sem)
    load.start()

    def kind_of(offset):
        own = (offset >= 0) & (offset < leaves)
        return (own, offset), (jnp.logical_not(own), 0)

    kinds = ((own_slots, own_places), (other_slots, other_places))
    own_count, other_count = listed(ids_ref, kinds, kind_of)

    def copy(slot):
        return pltpu.make_async_copy(blocks_ref.at[slot], blocks.at[slot], sems.at[slot])

    def begin(slots):
        def one(i, carry):
            copy(slots[i]).start()
            return carry

        return one

    lax.fori_loop(0, own_count, begin(own_slots), 0)
    lax.fori_loop(0, other_count, begin(other_slots), 0)
    total[...] = jnp.zeros_like(total)
    load.wait()
    add_products(near, kinds[0], own_count, blocks, lambda at: x_ref[at, :], total, lambda slot: copy(slot).wait())

    def finish(i, carry):
        copy(other_slots[i]).wait()
        return carry

    lax.fori_loop(0, other_count, finish, 0)


def close_kernel(half, ids_ref, before, after, blocks, sum_ref, down_ref, basis_ref, total, *lists):
    leaves, near = ids_ref.shape
    rank, rows = basis_ref.shape[1:]

    def kind_of(offset):
        return ((offset < 0) & (offset >= -half), offset + half), ((offset >= leaves) & (offset < leaves + half), offset - leaves)

    kinds = (lists[:2], lists[2:])
    counts = listed(ids_ref, kinds, kind_of)
    for leaf in range(leaves):
        here = slice(leaf * rows, (leaf + 1) * rows)
        total[here, :] = sum_ref[here, :] + dot_t(basis_ref[leaf], down_ref[leaf * rank : (leaf + 1) * rank, :])
    for kind, count, x_ref in zip(kinds, counts, (before, after)):
        add_products(near, kind, count, blocks, lambda at, x_ref=x_ref: x_ref[at, :], total)


def last_kernel(half, ids_ref, before, after, blocks, sum_ref, out_ref, *refs):
    lists, (total, result, sems) = refs[:4], refs[4:]
    leaves, near = ids_ref.shape
    rows = blocks.shape[1]

    def kind_of(offset):
        return (offset < -half, offset + leaves), (offset >= leaves + half, offset - leaves - half)

    kinds = (lists[:2], lists[2:])
    counts = listed(ids_ref, kinds, kind_of)
    total[...] = sum_ref[...]
    for kind, count, x_ref in zip(kinds, counts, (before, after)):
        add_products(near, kind, count, blocks, lambda at, x_ref=x_ref: x_ref[at, :], total)
    stores = []
    for leaf in range(leaves):
        here = slice(leaf * rows, (leaf + 1) * rows)
        result[here, :] = total[here, :].astype(result.dtype)
        stores.append(pltpu.make_async_copy(result.at[here], out_ref.at[here], sems.at[leaf]))
        stores[-1].start()
    for store in stores:
        store.wait()


def local(anomalies, leaf_basis, near_blocks, near_ids, transfer_leaf, transfer_mid, far_ids, far_count, mid_couple, top_couple):
    leaves, rank, rows = leaf_basis.shape
    near = near_blocks.shape[1]
    columns = anomalies.shape[1]
    inner_size = lax.axis_size("inner")
    leaf_size = lax.axis_size("leaf")
    bf16 = jnp.bfloat16
    half = leaves // 2
    cut = half * rows
    inner = lax.axis_index("inner")

    def shaped(*shape, dtype=bf16):
        return jax.ShapeDtypeStruct(shape, dtype)

    def shifted(x, axis, size, shift):
        return lax.ppermute(x, axis, [(i, (i + shift) % size) for i in range(size)])

    first, last = 0, inner_size - 1
    line = [(leaf * inner_size + i, leaf * inner_size + i + 1) for leaf in range(leaf_size) for i in range(last)]
    groups = range(leaf_size)

    def place(leaf, i):
        return leaf * inner_size + i

    def passed(x, pairs):
        return lax.ppermute(x, ("leaf", "inner"), pairs)

    hop_first = [(place(g, last), place(g + 1, last)) for g in groups[:-1]] + [(place(g, first), place(g - 1, first)) for g in groups[1:]]

    x_hbm = held(anomalies, pltpu.HBM)
    part, low, high, relay = call(
        up_kernel,
        [resident(2 * rank, columns)] + [resident(cut, columns)] * 3,
        [ANY] * 4,
        [VMEM] + [ANY] * 3,
        [
            pltpu.VMEM(anomalies.shape, bf16),
            pltpu.VMEM(leaf_basis.shape, bf16),
            pltpu.VMEM((leaves * rank, rank), bf16),
            pltpu.VMEM((rank, rank), bf16),
            pltpu.VMEM((leaves * rank, columns), bf16),
            pltpu.SemaphoreType.DMA((2 * leaves + 2,)),
            pltpu.SemaphoreType.DMA((3,)),
        ],
        1000,
        1000,
        8 * MIB,
    )(x_hbm, *[held(x, pltpu.HBM) for x in (leaf_basis, transfer_leaf.reshape(leaves * rank, rank), transfer_mid.reshape(rank, rank))])

    parts = [part] + [lax.ppermute(part, "inner", [(i, i ^ s) for i in range(inner_size)]) for s in range(1, inner_size)]
    parts, low, high, relay = lax.optimization_barrier((parts, low, high, relay))
    chain = [(i, i + 1) for i in range(leaf_size * inner_size - 1)]
    ahead = passed(high, chain)
    back = passed(low, [(j, i) for i, j in chain])

    group, top = call(functools.partial(group_kernel, inner_size), (resident((inner_size + 1) * rank, columns), resident(rank, columns)), [VMEM] * inner_size, (VMEM, VMEM), [], 1000, 1000, 8 * MIB)(*parts)
    relayed = passed(relay, hop_first)
    before_group = shifted(group, "leaf", leaf_size, 1)
    after_group = shifted(group, "leaf", leaf_size, leaf_size - 1)
    tops = [shifted(top, "leaf", leaf_size, s) for s in range(2, leaf_size - 1)]
    far_low, far_high = jnp.where(inner == last, relayed, low), jnp.where(inner == first, relayed, high)
    far_low, far_high, x_own = lax.optimization_barrier((far_low, far_high, anomalies))
    far_ahead = passed(far_low, line + [(place(g, last), place(g, first)) for g in groups[1:]])
    far_back = passed(far_high, [(j, i) for i, j in line] + [(place(g, first), place(g, last)) for g in groups[:-1]])

    leaf_down = call(
        functools.partial(down_kernel, leaf_size, inner_size),
        shaped(leaves * rank, columns),
        [SMEM, SMEM] + [VMEM] * (7 + len(tops)),
        VMEM,
        [pltpu.VMEM((3 * inner_size * rank, columns), bf16)],
        1000,
        1000,
        8 * MIB,
    )(far_ids, far_count, group, before_group, after_group, *tops, top_couple, mid_couple, transfer_mid, transfer_leaf)

    x_own, leaf_down = lax.optimization_barrier((x_own, leaf_down))
    ids = near_ids
    slots = leaves * near
    lists = [pltpu.SMEM((slots + 1,), jnp.int32)] * 4
    wide = shaped(leaves * rows, columns, dtype=jnp.float32)
    own_sum, blocks = call(
        own_kernel,
        (wide, resident(slots, rows, rows)),
        [SMEM, ANY, ANY],
        (VMEM, VMEM),
        lists + [pltpu.VMEM(anomalies.shape, bf16), pltpu.SemaphoreType.DMA, pltpu.SemaphoreType.DMA((slots,))],
        1000,
        1000,
        12 * MIB,
    )(ids, held(x_own, pltpu.HBM), held(near_blocks.reshape(slots, rows, rows), pltpu.HBM))

    blocks = held(blocks, pltpu.VMEM)
    ahead, back, own_sum = lax.optimization_barrier((ahead, back, own_sum))
    close_sum = call(functools.partial(close_kernel, half), wide, [SMEM] + [VMEM] * 6, VMEM, lists, 1000, 1000, 8 * MIB)(
        ids, ahead, back, blocks, own_sum, leaf_down, leaf_basis
    )
    last_scratch = lists + [
        pltpu.VMEM((leaves * rows, columns), jnp.float32),
        pltpu.VMEM((leaves * rows, columns), bf16),
        pltpu.SemaphoreType.DMA((leaves,)),
    ]
    return call(functools.partial(last_kernel, half), shaped(leaves * rows, columns), [SMEM] + [VMEM] * 4, ANY, last_scratch, 1000, 1000, 8 * MIB)(
        ids, far_ahead, far_back, blocks, close_sum
    )


def solution(mesh):
    return jax.shard_map(
        local,
        mesh=mesh,
        in_specs=(
            P(("leaf", "inner"), "groups"),
            P(("leaf", "inner"), None, None),
            P(("leaf", "inner"), None, None, None),
            P(("leaf", "inner"), None),
            P(("leaf", "inner"), None, None),
            P(("leaf", "inner"), None, None),
            P(("leaf", "inner"), None),
            P(("leaf", "inner")),
            P(("leaf", "inner"), None, None, None),
            P("leaf", None, None, None),
        ),
        out_specs=P(("leaf", "inner"), "groups"),
        check_vma=False,
    )
```

```python
import functools

import jax
import jax.numpy as jnp
from jax import lax
from jax.experimental import pallas as pl
from jax.experimental.pallas import tpu as pltpu
from jax.sharding import PartitionSpec as P

MIB = 1 << 20
VMEM = pl.BlockSpec(memory_space=pltpu.VMEM)
SMEM = pl.BlockSpec(memory_space=pltpu.SMEM)
ANY = pl.BlockSpec(memory_space=pl.ANY)


def held(x, space):
    return pltpu.with_memory_space_constraint(x, space)


def resident(*shape):
    return pltpu.VMEM(shape, jnp.bfloat16)


def dot(a, b):
    return lax.dot_general(a, b, (((1,), (0,)), ((), ())), preferred_element_type=jnp.float32)


def dot_t(a, b):
    return lax.dot_general(a, b, (((0,), (0,)), ((), ())), preferred_element_type=jnp.float32)


def call(kernel, out_shape, in_specs, out_specs, scratch, flops, moved, vmem, aliases=None):
    return pl.pallas_call(
        kernel,
        out_shape=out_shape,
        in_specs=in_specs,
        out_specs=out_specs,
        scratch_shapes=scratch,
        cost_estimate=pl.CostEstimate(flops=flops, bytes_accessed=moved, transcendentals=0),
        compiler_params=pltpu.CompilerParams(vmem_limit_bytes=vmem),
        input_output_aliases=aliases or {},
    )


def up_kernel(
    x_ref, basis_ref, leaf_map_ref, mid_map_ref, mid_couple_ref, couple_ref, out_ref, low, high, relay, basis, leaf_map, mid_map, mid_couple, couple, x, skeleton, sems, piece_sems
):
    leaves, rank, rows = basis.shape
    cut = low.shape[0]
    parts = []
    for leaf in range(leaves):
        here = slice(leaf * rows, (leaf + 1) * rows)
        parts.append(pltpu.make_async_copy(x_ref.at[here], x.at[here], sems.at[leaf]))
        parts.append(pltpu.make_async_copy(basis_ref.at[leaf], basis.at[leaf], sems.at[leaves + leaf]))
    maps = [pltpu.make_async_copy(leaf_map_ref, leaf_map, sems.at[2 * leaves]), pltpu.make_async_copy(mid_map_ref, mid_map, sems.at[2 * leaves + 1])]
    edge = pl.multiple_of(jnp.where(lax.axis_index("inner") == 0, cut, 0), rows)
    moves = ((x_ref.at[:cut], low), (x_ref.at[cut:], high), (x_ref.at[pl.ds(edge, cut)], relay), (mid_couple_ref, mid_couple), (couple_ref, couple))
    copies = [pltpu.make_async_copy(source, piece, piece_sems.at[i]) for i, (source, piece) in enumerate(moves)]
    for copy in parts + maps + copies:
        copy.start()
    for leaf in range(leaves):
        parts[2 * leaf].wait()
        parts[2 * leaf + 1].wait()
        skeleton[leaf * rank : (leaf + 1) * rank, :] = dot(basis[leaf], x[leaf * rows : (leaf + 1) * rows, :]).astype(jnp.bfloat16)
    for copy in maps:
        copy.wait()
    mid = dot_t(leaf_map[...], skeleton[...]).astype(jnp.bfloat16)
    out_ref[:rank, :] = mid
    out_ref[rank:, :] = dot_t(mid_map[...], mid).astype(jnp.bfloat16)
    for copy in copies:
        copy.wait()


def group_kernel(count, parts_ref, out_ref):
    rank = parts_ref.shape[0] // (2 * count)
    top = jnp.zeros((rank, parts_ref.shape[1]), jnp.float32)
    for i in range(count):
        at = 2 * i * rank
        out_ref[i * rank : (i + 1) * rank, :] = parts_ref[at : at + rank, :]
        top += parts_ref[at + rank : at + 2 * rank, :].astype(jnp.float32)
    out_ref[count * rank :, :] = top.astype(jnp.bfloat16)


def down_kernel(inner_size, far_ids, far_count, groups, couple, mid_couple, mid_map, leaf_map, out_ref):
    rank = mid_map.shape[0]
    group = lax.axis_index("leaf")
    inner = lax.axis_index("inner")
    size = (inner_size + 1) * rank
    top_down = jnp.zeros((rank, groups.shape[1]), jnp.float32)
    for i in range(1, couple.shape[0]):
        other = group ^ i
        term = dot(couple[other], groups[(i + 1) * size - rank : (i + 1) * size, :])
        top_down += jnp.where(jnp.abs(other - group) >= 2, term, 0.0)
    total = dot(mid_map[...], top_down.astype(jnp.bfloat16))
    for slot in range(mid_couple.shape[0]):
        live = slot < far_count[0]
        partner = jnp.where(live, far_ids[0, slot], group * inner_size)
        place = (partner // inner_size) ^ group
        at = pl.multiple_of(place * size + (inner ^ lax.rem(partner, inner_size)) * rank, rank)
        term = dot(mid_couple[slot], groups[pl.ds(at, rank), :])
        total += jnp.where(live, term, 0.0)
    total = total.astype(jnp.bfloat16)
    out_ref[...] = dot(leaf_map[...], total).astype(jnp.bfloat16)


def listed(ids_ref, lists, kind_of):
    leaves, near = ids_ref.shape
    first = (lax.axis_index("leaf") * lax.axis_size("inner") + lax.axis_index("inner")) * leaves

    def one(leaf, counts):
        for k in range(near):
            offset = ids_ref[leaf, k] - first
            grown = []
            for (slots, places), count, (member, place) in zip(lists, counts, kind_of(offset)):
                slots[count] = leaf * near + k
                places[count] = place
                grown.append(count + member.astype(jnp.int32))
            counts = tuple(grown)
        return counts

    return lax.fori_loop(0, leaves, one, (jnp.int32(0),) * len(lists))


def add_products(near, kind, count, blocks, partner, total, arrived=lambda slot: None):
    slots, places = kind
    rows = blocks.shape[1]
    cut = rows // 2

    def product(i):
        slot = slots[i]
        arrived(slot)
        at = pl.ds(pl.multiple_of(places[i] * rows, rows), rows)
        here = pl.ds(pl.multiple_of(slot // near * rows, rows), rows)
        return here, dot(blocks[slot, :, :cut], partner(at)[:cut]) + dot(blocks[slot, :, cut:], partner(at)[cut:])

    def pair(j, carry):
        one, first = product(2 * j)
        two, second = product(2 * j + 1)
        total[one, :] += first
        total[two, :] += second
        return carry

    lax.fori_loop(0, count // 2, pair, 0)

    @pl.when(lax.rem(count, 2) == 1)
    def _():
        here, term = product(count - 1)
        total[here, :] += term


def own_kernel(ids_ref, x_any, blocks_ref, total, blocks, own_slots, own_places, other_slots, other_places, x_ref, x_sem, sems):
    leaves, near = ids_ref.shape
    load = pltpu.make_async_copy(x_any, x_ref, x_sem)
    load.start()

    def kind_of(offset):
        own = (offset >= 0) & (offset < leaves)
        return (own, offset), (jnp.logical_not(own), 0)

    kinds = ((own_slots, own_places), (other_slots, other_places))
    own_count, other_count = listed(ids_ref, kinds, kind_of)

    def copy(slot):
        return pltpu.make_async_copy(blocks_ref.at[slot], blocks.at[slot], sems.at[slot])

    def begin(slots):
        def one(i, carry):
            copy(slots[i]).start()
            return carry

        return one

    lax.fori_loop(0, own_count, begin(own_slots), 0)
    lax.fori_loop(0, other_count, begin(other_slots), 0)
    total[...] = jnp.zeros_like(total)
    load.wait()
    add_products(near, kinds[0], own_count, blocks, lambda at: x_ref[at, :], total, lambda slot: copy(slot).wait())

    def finish(i, carry):
        copy(other_slots[i]).wait()
        return carry

    lax.fori_loop(0, other_count, finish, 0)


def close_kernel(half, ids_ref, before, after, blocks, sum_ref, down_ref, basis_ref, total, *lists):
    leaves, near = ids_ref.shape
    rank, rows = basis_ref.shape[1:]

    def kind_of(offset):
        return ((offset < 0) & (offset >= -half), offset + half), ((offset >= leaves) & (offset < leaves + half), offset - leaves)

    kinds = (lists[:2], lists[2:])
    counts = listed(ids_ref, kinds, kind_of)
    for leaf in range(leaves):
        here = slice(leaf * rows, (leaf + 1) * rows)
        total[here, :] = sum_ref[here, :] + dot_t(basis_ref[leaf], down_ref[leaf * rank : (leaf + 1) * rank, :])
    for kind, count, x_ref in zip(kinds, counts, (before, after)):
        add_products(near, kind, count, blocks, lambda at, x_ref=x_ref: x_ref[at, :], total)


def last_kernel(half, ids_ref, before, after, blocks, sum_ref, out_ref, *refs):
    lists, (total, result, sems) = refs[:4], refs[4:]
    leaves, near = ids_ref.shape
    rows = blocks.shape[1]

    def kind_of(offset):
        return (offset < -half, offset + leaves), (offset >= leaves + half, offset - leaves - half)

    kinds = (lists[:2], lists[2:])
    counts = listed(ids_ref, kinds, kind_of)
    total[...] = sum_ref[...]
    for kind, count, x_ref in zip(kinds, counts, (before, after)):
        add_products(near, kind, count, blocks, lambda at, x_ref=x_ref: x_ref[at, :], total)
    stores = []
    for leaf in range(leaves):
        here = slice(leaf * rows, (leaf + 1) * rows)
        result[here, :] = total[here, :].astype(result.dtype)
        stores.append(pltpu.make_async_copy(result.at[here], out_ref.at[here], sems.at[leaf]))
        stores[-1].start()
    for store in stores:
        store.wait()


def local(anomalies, leaf_basis, near_blocks, near_ids, transfer_leaf, transfer_mid, far_ids, far_count, mid_couple, top_couple):
    leaves, rank, rows = leaf_basis.shape
    near = near_blocks.shape[1]
    columns = anomalies.shape[1]
    inner_size = lax.axis_size("inner")
    leaf_size = lax.axis_size("leaf")
    bf16 = jnp.bfloat16
    half = leaves // 2
    cut = half * rows
    inner = lax.axis_index("inner")

    def shaped(*shape, dtype=bf16):
        return jax.ShapeDtypeStruct(shape, dtype)

    first, last = 0, inner_size - 1
    line = [(leaf * inner_size + i, leaf * inner_size + i + 1) for leaf in range(leaf_size) for i in range(last)]
    groups = range(leaf_size)

    def place(leaf, i):
        return leaf * inner_size + i

    def passed(x, pairs):
        return lax.ppermute(x, ("leaf", "inner"), pairs)

    hop_first = [(place(g, last), place(g + 1, last)) for g in groups[:-1]] + [(place(g, first), place(g - 1, first)) for g in groups[1:]]

    x_hbm = held(anomalies, pltpu.HBM)
    part, low, high, relay, basis, leaf_map, mid_map, mid_links, group_links = call(
        up_kernel,
        [
            resident(2 * rank, columns),
            resident(cut, columns),
            resident(cut, columns),
            resident(cut, columns),
            resident(leaves, rank, rows),
            resident(leaves * rank, rank),
            resident(rank, rank),
            resident(*mid_couple.shape[1:]),
            resident(*top_couple.shape[1:]),
        ],
        [ANY] * 6,
        [VMEM] + [ANY] * 3 + [VMEM] * 5,
        [
            pltpu.VMEM(anomalies.shape, bf16),
            pltpu.VMEM((leaves * rank, columns), bf16),
            pltpu.SemaphoreType.DMA((2 * leaves + 2,)),
            pltpu.SemaphoreType.DMA((5,)),
        ],
        1000,
        1000,
        8 * MIB,
    )(
        x_hbm,
        *[
            held(x, pltpu.HBM)
            for x in (leaf_basis, transfer_leaf.reshape(leaves * rank, rank), transfer_mid.reshape(rank, rank), mid_couple[0], top_couple[0])
        ],
    )

    def doubled(x, axis, reach):
        partner = lax.ppermute(x, axis, [(i, i ^ reach) for i in range(lax.axis_size(axis))])
        return jnp.concatenate([x, partner])

    parts = doubled(part, "inner", 1)
    parts, low, high = lax.optimization_barrier((parts, low, high))
    chain = [(i, i + 1) for i in range(leaf_size * inner_size - 1)]
    ahead = passed(high, chain)
    back = passed(low, [(j, i) for i, j in chain])
    reach = 2
    while reach < inner_size:
        parts = doubled(parts, "inner", reach)
        reach *= 2

    group = call(functools.partial(group_kernel, inner_size), resident((inner_size + 1) * rank, columns), [VMEM], VMEM, [], 1000, 1000, 8 * MIB)(parts)
    relayed = passed(relay, hop_first)
    reach = 1
    while reach < leaf_size:
        group = doubled(group, "leaf", reach)
        reach *= 2
    far_low, far_high = jnp.where(inner == last, relayed, low), jnp.where(inner == first, relayed, high)
    far_low, far_high, x_own = lax.optimization_barrier((far_low, far_high, anomalies))
    far_ahead = passed(far_low, line + [(place(g, last), place(g, first)) for g in groups[1:]])
    far_back = passed(far_high, [(j, i) for i, j in line] + [(place(g, first), place(g, last)) for g in groups[:-1]])

    leaf_down = call(functools.partial(down_kernel, inner_size), shaped(leaves * rank, columns), [SMEM, SMEM] + [VMEM] * 5, VMEM, [], 1000, 1000, 8 * MIB)(
        far_ids, far_count, group, group_links, mid_links, mid_map, leaf_map
    )

    x_own, leaf_down = lax.optimization_barrier((x_own, leaf_down))
    ids = near_ids
    slots = leaves * near
    lists = [pltpu.SMEM((slots + 1,), jnp.int32)] * 4
    wide = shaped(leaves * rows, columns, dtype=jnp.float32)
    own_sum, blocks = call(
        own_kernel,
        (wide, resident(slots, rows, rows)),
        [SMEM, ANY, ANY],
        (VMEM, VMEM),
        lists + [pltpu.VMEM(anomalies.shape, bf16), pltpu.SemaphoreType.DMA, pltpu.SemaphoreType.DMA((slots,))],
        1000,
        1000,
        12 * MIB,
    )(ids, held(x_own, pltpu.HBM), held(near_blocks.reshape(slots, rows, rows), pltpu.HBM))

    blocks = held(blocks, pltpu.VMEM)
    ahead, back, own_sum = lax.optimization_barrier((ahead, back, own_sum))
    close_sum = call(functools.partial(close_kernel, half), wide, [SMEM] + [VMEM] * 6, VMEM, lists, 1000, 1000, 8 * MIB)(
        ids, ahead, back, blocks, own_sum, leaf_down, basis
    )
    last_scratch = lists + [
        pltpu.VMEM((leaves * rows, columns), jnp.float32),
        pltpu.VMEM((leaves * rows, columns), bf16),
        pltpu.SemaphoreType.DMA((leaves,)),
    ]
    return call(functools.partial(last_kernel, half), shaped(leaves * rows, columns), [SMEM] + [VMEM] * 4, ANY, last_scratch, 1000, 1000, 8 * MIB)(
        ids, far_ahead, far_back, blocks, close_sum
    )


def solution(mesh):
    return jax.shard_map(
        local,
        mesh=mesh,
        in_specs=(
            P(("leaf", "inner"), "groups"),
            P(("leaf", "inner"), None, None),
            P(("leaf", "inner"), None, None, None),
            P(("leaf", "inner"), None),
            P(("leaf", "inner"), None, None),
            P(("leaf", "inner"), None, None),
            P(("leaf", "inner"), None),
            P(("leaf", "inner")),
            P(("leaf", "inner"), None, None, None),
            P("leaf", None, None, None),
        ),
        out_specs=P(("leaf", "inner"), "groups"),
        check_vma=False,
    )
```

```python
import functools

import jax
import jax.numpy as jnp
from jax import lax
from jax.experimental import pallas as pl
from jax.experimental.pallas import tpu as pltpu
from jax.sharding import PartitionSpec as P

MIB = 1 << 20
VMEM = pl.BlockSpec(memory_space=pltpu.VMEM)
SMEM = pl.BlockSpec(memory_space=pltpu.SMEM)
ANY = pl.BlockSpec(memory_space=pl.ANY)


def held(x, space):
    return pltpu.with_memory_space_constraint(x, space)


def resident(*shape, dtype=jnp.bfloat16):
    return pltpu.VMEM(shape, dtype)


def dot(a, b):
    return lax.dot_general(a, b, (((1,), (0,)), ((), ())), preferred_element_type=jnp.float32)


def dot_t(a, b):
    return lax.dot_general(a, b, (((0,), (0,)), ((), ())), preferred_element_type=jnp.float32)


def call(kernel, out_shape, in_specs, out_specs, scratch, flops, moved, vmem, aliases=None):
    return pl.pallas_call(
        kernel,
        out_shape=out_shape,
        in_specs=in_specs,
        out_specs=out_specs,
        scratch_shapes=scratch,
        cost_estimate=pl.CostEstimate(flops=flops, bytes_accessed=moved, transcendentals=0),
        compiler_params=pltpu.CompilerParams(vmem_limit_bytes=vmem),
        input_output_aliases=aliases or {},
    )


def cut_kernel(cuts, x_ref, *refs):
    pieces, relay, sems = refs[:-2], refs[-2], refs[-1]
    rows = x_ref.shape[0] // cuts[-1]
    edge = jnp.where(lax.axis_index("inner") == 0, (cuts[-1] - relay.shape[0] // rows) * rows, 0)
    sources = [x_ref.at[a * rows : b * rows] for a, b in cuts[:-1]] + [x_ref.at[pl.ds(pl.multiple_of(edge, rows), relay.shape[0])]]
    copies = [pltpu.make_async_copy(source, piece, sems.at[i]) for i, (source, piece) in enumerate(zip(sources, (*pieces, relay)))]
    for copy in copies:
        copy.start()
    for copy in copies:
        copy.wait()


def up_kernel(
    cuts, x_ref, basis_ref, leaf_map_ref, mid_map_ref, mid_couple_ref, couple_ref, out_ref, x, basis, leaf_map, mid_map, mid_couple, couple, *refs
):
    pieces, (skeleton, sems, piece_sems) = refs[:-3], refs[-3:]
    leaves, rank, rows = basis.shape
    parts = []
    for leaf in range(leaves):
        here = slice(leaf * rows, (leaf + 1) * rows)
        parts.append(pltpu.make_async_copy(x_ref.at[here], x.at[here], sems.at[leaf]))
        parts.append(pltpu.make_async_copy(basis_ref.at[leaf], basis.at[leaf], sems.at[leaves + leaf]))
    maps = [pltpu.make_async_copy(leaf_map_ref, leaf_map, sems.at[2 * leaves]), pltpu.make_async_copy(mid_map_ref, mid_map, sems.at[2 * leaves + 1])]
    moves = [(x_ref.at[a * rows : b * rows], piece) for (a, b), piece in zip(cuts, pieces)] + [(mid_couple_ref, mid_couple), (couple_ref, couple)]
    copies = [pltpu.make_async_copy(source, target, piece_sems.at[i]) for i, (source, target) in enumerate(moves)]
    for copy in parts + maps + copies:
        copy.start()
    for leaf in range(leaves):
        parts[2 * leaf].wait()
        parts[2 * leaf + 1].wait()
        skeleton[leaf * rank : (leaf + 1) * rank, :] = dot(basis[leaf], x[leaf * rows : (leaf + 1) * rows, :]).astype(jnp.bfloat16)
    for copy in maps:
        copy.wait()
    mid = dot_t(leaf_map[...], skeleton[...]).astype(jnp.bfloat16)
    out_ref[:rank, :] = mid
    out_ref[rank:, :] = dot_t(mid_map[...], mid).astype(jnp.bfloat16)
    for copy in copies:
        copy.wait()


def group_kernel(count, parts_ref, out_ref, top_ref):
    rank = top_ref.shape[0]
    top = jnp.zeros(top_ref.shape, jnp.float32)
    for i in range(count):
        at = 2 * i * rank
        out_ref[i * rank : (i + 1) * rank, :] = parts_ref[at : at + rank, :]
        top += parts_ref[at + rank : at + 2 * rank, :].astype(jnp.float32)
    top = top.astype(jnp.bfloat16)
    out_ref[count * rank :, :] = top
    top_ref[...] = top


def down_kernel(leaf_size, inner_size, far_ids, far_count, own, before, after, *refs):
    tops = dict(zip(range(2, leaf_size - 1), refs))
    couple, mid_couple, mid_map, leaf_map, basis, _, out_ref, window = refs[len(tops) :]
    rank = mid_map.shape[0]
    group = lax.axis_index("leaf")
    inner = lax.axis_index("inner")
    last = inner_size * rank
    top_down = jnp.zeros((rank, own.shape[1]), jnp.float32)
    for shift in range(1, leaf_size):
        source = lax.rem(group - shift + leaf_size, leaf_size)
        if shift == 1:
            top = before[last:, :]
        elif shift == leaf_size - 1:
            top = after[last:, :]
        else:
            top = tops[shift][...]
        term = dot(couple[source], top)
        top_down += jnp.where(jnp.abs(source - group) >= 2, term, 0.0)
    for i, part in enumerate((before, own, after)):
        window[i * last : (i + 1) * last, :] = part[:last, :]
    total = dot(mid_map[...], top_down.astype(jnp.bfloat16))
    for slot in range(mid_couple.shape[0]):
        live = slot < far_count[0]
        partner = jnp.where(live, far_ids[0, slot], group * inner_size)
        side = partner // inner_size - group + 1
        at = pl.multiple_of((side * inner_size + (inner ^ lax.rem(partner, inner_size))) * rank, rank)
        term = dot(mid_couple[slot], window[pl.ds(at, rank), :])
        total += jnp.where(live, term, 0.0)
    leaf_down = dot(leaf_map[...], total.astype(jnp.bfloat16)).astype(jnp.bfloat16)
    leaves, _, rows = basis.shape
    for leaf in range(leaves):
        out_ref[leaf * rows : (leaf + 1) * rows, :] += dot_t(basis[leaf], leaf_down[leaf * rank : (leaf + 1) * rank, :])


def listed(ids_ref, lists, kind_of):
    leaves, near = ids_ref.shape
    first = (lax.axis_index("leaf") * lax.axis_size("inner") + lax.axis_index("inner")) * leaves

    def one(leaf, counts):
        for k in range(near):
            offset = ids_ref[leaf, k] - first
            grown = []
            for (slots, places), count, (member, place) in zip(lists, counts, kind_of(leaf, offset)):
                slots[count] = leaf * near + k
                places[count] = place
                grown.append(count + member.astype(jnp.int32))
            counts = tuple(grown)
        return counts

    return lax.fori_loop(0, leaves, one, (jnp.int32(0),) * len(lists))


def add_products(near, kind, count, blocks, x_ref, total, arrived=lambda slot: None):
    slots, places = kind
    rows = blocks.shape[1]

    def product(i):
        slot = slots[i]
        arrived(slot)
        at = pl.ds(pl.multiple_of(places[i] * rows, rows), rows)
        here = pl.ds(pl.multiple_of(slot // near * rows, rows), rows)
        return here, dot(blocks[slot], x_ref[at, :])

    def pair(j, carry):
        one, first = product(2 * j)
        two, second = product(2 * j + 1)
        total[one, :] += first
        total[two, :] += second
        return carry

    lax.fori_loop(0, count // 2, pair, 0)

    @pl.when(lax.rem(count, 2) == 1)
    def _():
        here, term = product(count - 1)
        total[here, :] += term


def own_kernel(stop, ids_ref, x_ref, blocks_ref, total, blocks, own_slots, own_places, other_slots, other_places, sems):
    leaves, near = ids_ref.shape

    def kind_of(leaf, offset):
        own = (offset >= 0) & (offset < leaves) & (leaf < stop)
        return (own, offset), (jnp.logical_not(own), 0)

    kinds = ((own_slots, own_places), (other_slots, other_places))
    own_count, other_count = listed(ids_ref, kinds, kind_of)

    def copy(slot):
        return pltpu.make_async_copy(blocks_ref.at[slot], blocks.at[slot], sems.at[slot])

    def begin(slots):
        def one(i, carry):
            copy(slots[i]).start()
            return carry

        return one

    lax.fori_loop(0, own_count, begin(own_slots), 0)
    lax.fori_loop(0, other_count, begin(other_slots), 0)
    total[...] = jnp.zeros_like(total)
    add_products(near, kinds[0], own_count, blocks, x_ref, total, lambda slot: copy(slot).wait())

    def finish(i, carry):
        copy(other_slots[i]).wait()
        return carry

    lax.fori_loop(0, other_count, finish, 0)


def wave_kernel(near_by, far_off, stop, ids_ref, first_before, first_after, before, after, x_ref, blocks, _, total, *lists):
    leaves, near = ids_ref.shape

    def kind_of(leaf, offset):
        return (
            ((offset < 0) & (offset >= -near_by), offset + near_by),
            ((offset >= leaves) & (offset < leaves + near_by), offset - leaves),
            ((offset < -near_by) & (offset >= -far_off), offset + far_off),
            ((offset >= leaves + near_by) & (offset < leaves + far_off), offset - leaves - near_by),
            ((offset >= 0) & (offset < leaves) & (leaf >= stop), offset),
        )

    kinds = [lists[i : i + 2] for i in range(0, len(lists), 2)]
    counts = listed(ids_ref, kinds, kind_of)
    for kind, count, partner in zip(kinds, counts, (first_before, first_after, before, after, x_ref)):
        add_products(near, kind, count, blocks, partner, total)


def last_kernel(near_by, ids_ref, before, after, blocks, _, out_ref, total, *refs):
    lists, (result, sems) = refs[:4], refs[4:]
    leaves, near = ids_ref.shape
    rows = blocks.shape[1]

    def kind_of(leaf, offset):
        return (offset < -near_by, offset + leaves), (offset >= leaves + near_by, offset - leaves - near_by)

    kinds = (lists[:2], lists[2:])
    counts = listed(ids_ref, kinds, kind_of)
    for kind, count, x_ref in zip(kinds, counts, (before, after)):
        add_products(near, kind, count, blocks, x_ref, total)
    stores = []
    for leaf in range(leaves):
        here = slice(leaf * rows, (leaf + 1) * rows)
        result[here, :] = total[here, :].astype(result.dtype)
        stores.append(pltpu.make_async_copy(result.at[here], out_ref.at[here], sems.at[leaf]))
        stores[-1].start()
    for store in stores:
        store.wait()


def local(anomalies, leaf_basis, near_blocks, near_ids, transfer_leaf, transfer_mid, far_ids, far_count, mid_couple, top_couple):
    leaves, rank, rows = leaf_basis.shape
    near = near_blocks.shape[1]
    columns = anomalies.shape[1]
    inner_size = lax.axis_size("inner")
    leaf_size = lax.axis_size("leaf")
    bf16 = jnp.bfloat16
    inner = lax.axis_index("inner")
    first, last = 0, inner_size - 1
    groups = range(leaf_size)

    def place(leaf, i):
        return leaf * inner_size + i

    def passed(x, pairs):
        return lax.ppermute(x, ("leaf", "inner"), pairs)

    def doubled(x, axis, reach):
        partner = lax.ppermute(x, axis, [(i, i ^ reach) for i in range(lax.axis_size(axis))])
        return jnp.concatenate([x, partner])

    chain = [(i, i + 1) for i in range(leaf_size * inner_size - 1)]
    line = [(place(g, i), place(g, i + 1)) for g in groups for i in range(last)]
    hop = [(place(g, last), place(g + 1, last)) for g in groups[:-1]] + [(place(g, first), place(g - 1, first)) for g in groups[1:]]

    one = leaves // 4
    two = one + leaves * 3 // 8
    sizes = [one, one, two - one, two - one, leaves - two, leaves - two]
    cuts = [(leaves - one, leaves), (0, one), (leaves - two, leaves - one), (one, two), (0, leaves - two), (two, leaves)]

    def kernel(body, out_shape, in_specs, out_specs, scratch, aliases=None, flops=1000):
        return call(body, out_shape, in_specs, out_specs, scratch, flops, 1000, 8 * MIB, aliases)

    pieces = [resident(size * rows, columns) for size in sizes]
    ahead, back, relay = kernel(
        functools.partial(cut_kernel, (*cuts[:2], leaves)), [*pieces[:2], pieces[4]], [ANY], [ANY] * 3, [pltpu.SemaphoreType.DMA((3,))]
    )(held(anomalies, pltpu.HBM))
    relayed = passed(relay, hop)
    x_up, ahead, back = lax.optimization_barrier((anomalies, ahead, back))
    halo = [(passed(ahead, chain), passed(back, [(j, i) for i, j in chain]))]

    operands = (x_up, leaf_basis, transfer_leaf.reshape(leaves * rank, rank), transfer_mid.reshape(rank, rank), mid_couple[0], top_couple[0])
    part, x_own, basis, leaf_map, mid_map, mid_links, group_links, *later = kernel(
        functools.partial(up_kernel, cuts[2:]),
        [resident(2 * rank, columns)] + [resident(*x.shape) for x in operands] + pieces[2:],
        [ANY] * 6,
        [VMEM] * 7 + [ANY] * 4,
        [pltpu.VMEM((leaves * rank, columns), bf16), pltpu.SemaphoreType.DMA((2 * leaves + 2,)), pltpu.SemaphoreType.DMA((6,))],
    )(*[held(x, pltpu.HBM) for x in operands])
    low, high = jnp.where(inner == last, relayed, later[2]), jnp.where(inner == first, relayed, later[3])
    part, x_own, ahead, back, low, high = lax.optimization_barrier((part, x_own, *later[:2], low, high))
    parts = doubled(part, "inner", 1)
    halo.append((passed(ahead, chain), passed(back, [(j, i) for i, j in chain])))

    slots = leaves * near
    lists = [pltpu.SMEM((slots + 1,), jnp.int32)] * 2
    wide = resident(leaves * rows, columns, dtype=jnp.float32)
    total, blocks = kernel(
        functools.partial(own_kernel, leaves // 2),
        (wide, resident(slots, rows, rows)),
        [SMEM, VMEM, ANY],
        (VMEM, VMEM),
        lists * 2 + [pltpu.SemaphoreType.DMA((slots,))],
        flops=4 * 10**9,
    )(near_ids, held(x_own, pltpu.VMEM), held(near_blocks.reshape(slots, rows, rows), pltpu.HBM))
    blocks = held(blocks, pltpu.VMEM)

    parts, total, halo[0] = lax.optimization_barrier((parts, total, halo[0]))
    reach = 2
    while reach < inner_size:
        parts = doubled(parts, "inner", reach)
        reach *= 2
    low, high, total = lax.optimization_barrier((low, high, total))
    halo.append(
        (
            passed(low, line + [(place(g, last), place(g, first)) for g in groups[1:]]),
            passed(high, [(j, i) for i, j in line] + [(place(g, first), place(g, last)) for g in groups[:-1]]),
        )
    )

    parts, halo[1] = lax.optimization_barrier((parts, halo[1]))
    group, top = kernel(
        functools.partial(group_kernel, inner_size), (resident((inner_size + 1) * rank, columns), resident(rank, columns)), [VMEM], (VMEM, VMEM), []
    )(parts)

    def shifted(x, shift):
        return lax.ppermute(x, "leaf", [(i, (i + shift) % leaf_size) for i in groups])

    found = [shifted(group, 1), shifted(group, leaf_size - 1)] + [shifted(top, s) for s in range(2, leaf_size - 1)]
    group, total = lax.optimization_barrier((group, total))
    total = kernel(functools.partial(wave_kernel, one, two, leaves // 2), wide, [SMEM] + [VMEM] * 7, VMEM, lists * 5, aliases={7: 0}, flops=10**10)(
        near_ids, *halo[0], *halo[1], x_own, blocks, held(total, pltpu.VMEM)
    )
    found, total = lax.optimization_barrier((found, total))
    total = kernel(
        functools.partial(down_kernel, leaf_size, inner_size),
        wide,
        [SMEM, SMEM] + [VMEM] * (7 + len(found)),
        VMEM,
        [pltpu.VMEM((3 * inner_size * rank, columns), bf16)],
        aliases={8 + len(found): 0},
    )(far_ids, far_count, group, *found, group_links, mid_links, mid_map, leaf_map, basis, held(total, pltpu.VMEM))
    out, _ = kernel(
        functools.partial(last_kernel, two),
        (jax.ShapeDtypeStruct(anomalies.shape, bf16), wide),
        [SMEM] + [VMEM] * 4,
        (ANY, VMEM),
        lists * 2 + [pltpu.VMEM(anomalies.shape, bf16), pltpu.SemaphoreType.DMA((leaves,))],
        aliases={4: 1},
    )(near_ids, *halo[2], blocks, held(total, pltpu.VMEM))
    return out


def solution(mesh):
    return jax.shard_map(
        local,
        mesh=mesh,
        in_specs=(
            P(("leaf", "inner"), "groups"),
            P(("leaf", "inner"), None, None),
            P(("leaf", "inner"), None, None, None),
            P(("leaf", "inner"), None),
            P(("leaf", "inner"), None, None),
            P(("leaf", "inner"), None, None),
            P(("leaf", "inner"), None),
            P(("leaf", "inner")),
            P(("leaf", "inner"), None, None, None),
            P("leaf", None, None, None),
        ),
        out_specs=P(("leaf", "inner"), "groups"),
        check_vma=False,
    )
```

```python
import functools

import jax
import jax.numpy as jnp
from jax import lax
from jax.experimental import pallas as pl
from jax.experimental.pallas import tpu as pltpu
from jax.sharding import PartitionSpec as P

MIB = 1 << 20
VMEM = pl.BlockSpec(memory_space=pltpu.VMEM)
SMEM = pl.BlockSpec(memory_space=pltpu.SMEM)
ANY = pl.BlockSpec(memory_space=pl.ANY)


def held(x, space):
    return pltpu.with_memory_space_constraint(x, space)


def resident(*shape, dtype=jnp.bfloat16):
    return pltpu.VMEM(shape, dtype)


def turn_of(leaf, inner_size):
    return (3 * leaf + 2) % inner_size


def carrier(turn, inner_size):
    return lax.rem((turn + inner_size - 2 % inner_size) * pow(3, -1, inner_size), inner_size)


def dot(a, b):
    return lax.dot_general(a, b, (((1,), (0,)), ((), ())), preferred_element_type=jnp.float32)


def dot_t(a, b):
    return lax.dot_general(a, b, (((0,), (0,)), ((), ())), preferred_element_type=jnp.float32)


def call(kernel, out_shape, in_specs, out_specs, scratch, flops, moved, vmem, aliases=None):
    return pl.pallas_call(
        kernel,
        out_shape=out_shape,
        in_specs=in_specs,
        out_specs=out_specs,
        scratch_shapes=scratch,
        cost_estimate=pl.CostEstimate(flops=flops, bytes_accessed=moved, transcendentals=0),
        compiler_params=pltpu.CompilerParams(vmem_limit_bytes=vmem),
        input_output_aliases=aliases or {},
    )


def cut_kernel(cuts, x_ref, *refs):
    pieces, relay, sems = refs[:-2], refs[-2], refs[-1]
    rows = x_ref.shape[0] // cuts[-1]
    edge = jnp.where(lax.axis_index("inner") == 0, (cuts[-1] - relay.shape[0] // rows) * rows, 0)
    sources = [x_ref.at[a * rows : b * rows] for a, b in cuts[:-1]] + [x_ref.at[pl.ds(pl.multiple_of(edge, rows), relay.shape[0])]]
    copies = [pltpu.make_async_copy(source, piece, sems.at[i]) for i, (source, piece) in enumerate(zip(sources, (*pieces, relay)))]
    for copy in copies:
        copy.start()
    for copy in copies:
        copy.wait()


def up_kernel(
    cuts, x_ref, basis_ref, leaf_map_ref, mid_map_ref, mid_couple_ref, couple_ref, out_ref, x, basis, leaf_map, mid_map, mid_couple, couple, *refs
):
    pieces, (skeleton, sems, piece_sems) = refs[:-3], refs[-3:]
    leaves, rank, rows = basis.shape
    parts = []
    for leaf in range(leaves):
        here = slice(leaf * rows, (leaf + 1) * rows)
        parts.append(pltpu.make_async_copy(x_ref.at[here], x.at[here], sems.at[leaf]))
        parts.append(pltpu.make_async_copy(basis_ref.at[leaf], basis.at[leaf], sems.at[leaves + leaf]))
    maps = [pltpu.make_async_copy(leaf_map_ref, leaf_map, sems.at[2 * leaves]), pltpu.make_async_copy(mid_map_ref, mid_map, sems.at[2 * leaves + 1])]
    moves = [(x_ref.at[a * rows : b * rows], piece) for (a, b), piece in zip(cuts, pieces)] + [(mid_couple_ref, mid_couple), (couple_ref, couple)]
    copies = [pltpu.make_async_copy(source, target, piece_sems.at[i]) for i, (source, target) in enumerate(moves)]
    for copy in parts + maps + copies:
        copy.start()
    for leaf in range(leaves):
        parts[2 * leaf].wait()
        parts[2 * leaf + 1].wait()
        skeleton[leaf * rank : (leaf + 1) * rank, :] = dot(basis[leaf], x[leaf * rows : (leaf + 1) * rows, :]).astype(jnp.bfloat16)
    for copy in maps:
        copy.wait()
    mid = dot_t(leaf_map[...], skeleton[...]).astype(jnp.bfloat16)
    out_ref[:rank, :] = mid
    out_ref[rank:, :] = dot_t(mid_map[...], mid).astype(jnp.bfloat16)
    for copy in copies:
        copy.wait()


def down_kernel(leaf_size, inner_size, far_ids, far_count, plane, planes, couple, mid_couple, mid_map, leaf_map, basis, _, out_ref):
    rank = mid_map.shape[0]
    size = 2 * rank
    group = lax.axis_index("leaf")
    inner = lax.axis_index("inner")

    def at_of(step, leaf, offset=0):
        return pl.ds(pl.multiple_of((step * leaf_size + leaf) * size + offset, rank), rank)

    top_down = jnp.zeros((rank, plane.shape[1]), jnp.float32)
    for distance in range(1, leaf_size):
        other = group ^ distance
        top = plane[at_of(0, other, rank), :].astype(jnp.float32)
        for step in range(inner_size):
            top += planes[at_of(step, other, rank), :].astype(jnp.float32)
        term = dot(couple[other], top.astype(jnp.bfloat16))
        top_down += jnp.where(jnp.abs(other - group) >= 2, term, 0.0)
    total = dot(mid_map[...], top_down.astype(jnp.bfloat16))
    for slot in range(mid_couple.shape[0]):
        live = slot < far_count[0]
        partner = jnp.where(live, far_ids[0, slot], group * inner_size)
        other, turn = partner // inner_size, inner ^ lax.rem(partner, inner_size)
        step = (group & (inner_size - 1)) ^ carrier(turn, inner_size)
        near, far = plane[at_of(0, other), :], planes[at_of(step, other), :]
        term = dot(mid_couple[slot], jnp.where(turn == 0, near, far))
        total += jnp.where(live, term, 0.0)
    leaf_down = dot(leaf_map[...], total.astype(jnp.bfloat16)).astype(jnp.bfloat16)
    leaves, _, rows = basis.shape
    for leaf in range(leaves):
        out_ref[leaf * rows : (leaf + 1) * rows, :] += dot_t(basis[leaf], leaf_down[leaf * rank : (leaf + 1) * rank, :])


def listed(ids_ref, lists, kind_of):
    leaves, near = ids_ref.shape
    first = (lax.axis_index("leaf") * lax.axis_size("inner") + lax.axis_index("inner")) * leaves

    def one(leaf, counts):
        for k in range(near):
            offset = ids_ref[leaf, k] - first
            grown = []
            for (slots, places), count, (member, place) in zip(lists, counts, kind_of(leaf, offset)):
                slots[count] = leaf * near + k
                places[count] = place
                grown.append(count + member.astype(jnp.int32))
            counts = tuple(grown)
        return counts

    return lax.fori_loop(0, leaves, one, (jnp.int32(0),) * len(lists))


def add_products(near, kind, count, blocks, x_ref, total, arrived=lambda slot: None):
    slots, places = kind
    rows = blocks.shape[1]

    def product(i):
        slot = slots[i]
        arrived(slot)
        at = pl.ds(pl.multiple_of(places[i] * rows, rows), rows)
        here = pl.ds(pl.multiple_of(slot // near * rows, rows), rows)
        return here, dot(blocks[slot], x_ref[at, :])

    def pair(j, carry):
        one, first = product(2 * j)
        two, second = product(2 * j + 1)
        total[one, :] += first
        total[two, :] += second
        return carry

    lax.fori_loop(0, count // 2, pair, 0)

    @pl.when(lax.rem(count, 2) == 1)
    def _():
        here, term = product(count - 1)
        total[here, :] += term


def own_kernel(stop, ids_ref, x_ref, blocks_ref, total, blocks, own_slots, own_places, other_slots, other_places, sems):
    leaves, near = ids_ref.shape

    def kind_of(leaf, offset):
        own = (offset >= 0) & (offset < leaves) & (leaf < stop)
        return (own, offset), (jnp.logical_not(own), 0)

    kinds = ((own_slots, own_places), (other_slots, other_places))
    own_count, other_count = listed(ids_ref, kinds, kind_of)

    def copy(slot):
        return pltpu.make_async_copy(blocks_ref.at[slot], blocks.at[slot], sems.at[slot])

    def begin(slots):
        def one(i, carry):
            copy(slots[i]).start()
            return carry

        return one

    lax.fori_loop(0, own_count, begin(own_slots), 0)
    lax.fori_loop(0, other_count, begin(other_slots), 0)
    total[...] = jnp.zeros_like(total)
    add_products(near, kinds[0], own_count, blocks, x_ref, total, lambda slot: copy(slot).wait())

    def finish(i, carry):
        copy(other_slots[i]).wait()
        return carry

    lax.fori_loop(0, other_count, finish, 0)


def wave_kernel(near_by, ids_ref, before, after, blocks, _, total, *lists):
    leaves, near = ids_ref.shape

    def kind_of(leaf, offset):
        return ((offset < 0) & (offset >= -near_by), offset + near_by), ((offset >= leaves) & (offset < leaves + near_by), offset - leaves)

    kinds = (lists[:2], lists[2:])
    counts = listed(ids_ref, kinds, kind_of)
    for kind, count, x_ref in zip(kinds, counts, (before, after)):
        add_products(near, kind, count, blocks, x_ref, total)


def last_kernel(near_by, ids_ref, before, after, blocks, _, out_ref, total, *refs):
    lists, (result, sems) = refs[:4], refs[4:]
    leaves, near = ids_ref.shape
    rows = blocks.shape[1]

    def kind_of(leaf, offset):
        return (offset < -near_by, offset + leaves), (offset >= leaves + near_by, offset - leaves - near_by)

    kinds = (lists[:2], lists[2:])
    counts = listed(ids_ref, kinds, kind_of)
    for kind, count, x_ref in zip(kinds, counts, (before, after)):
        add_products(near, kind, count, blocks, x_ref, total)
    stores = []
    for leaf in range(leaves):
        here = slice(leaf * rows, (leaf + 1) * rows)
        result[here, :] = total[here, :].astype(result.dtype)
        stores.append(pltpu.make_async_copy(result.at[here], out_ref.at[here], sems.at[leaf]))
        stores[-1].start()
    for store in stores:
        store.wait()


def local(anomalies, leaf_basis, near_blocks, near_ids, transfer_leaf, transfer_mid, far_ids, far_count, mid_couple, top_couple):
    leaves, rank, rows = leaf_basis.shape
    near = near_blocks.shape[1]
    columns = anomalies.shape[1]
    inner_size = lax.axis_size("inner")
    leaf_size = lax.axis_size("leaf")
    bf16 = jnp.bfloat16
    inner = lax.axis_index("inner")
    first, last = 0, inner_size - 1
    groups = range(leaf_size)

    def place(leaf, i):
        return leaf * inner_size + i

    def passed(x, pairs):
        return lax.ppermute(x, ("leaf", "inner"), pairs)

    def swapped(x, reach):
        return lax.ppermute(x, "leaf", [(i, i ^ reach) for i in groups])

    chain = [(i, i + 1) for i in range(leaf_size * inner_size - 1)]
    line = [(place(g, i), place(g, i + 1)) for g in groups for i in range(last)]
    hop = [(place(g, last), place(g + 1, last)) for g in groups[:-1]] + [(place(g, first), place(g - 1, first)) for g in groups[1:]]

    one = leaves * 5 // 8
    rest = leaves - one
    sizes = [one, one, rest, rest]
    cuts = [(rest, leaves), (0, one), (0, rest), (one, leaves)]

    def kernel(body, out_shape, in_specs, out_specs, scratch, aliases=None, flops=1000):
        return call(body, out_shape, in_specs, out_specs, scratch, flops, 1000, 8 * MIB, aliases)

    pieces = [resident(size * rows, columns) for size in sizes]
    ahead, back, relay = kernel(
        functools.partial(cut_kernel, (*cuts[:2], leaves)), [*pieces[:2], pieces[2]], [ANY], [VMEM] * 3, [pltpu.SemaphoreType.DMA((3,))]
    )(held(anomalies, pltpu.HBM))
    relayed = passed(relay, hop)
    x_up, ahead, back = lax.optimization_barrier((anomalies, ahead, back))
    halo = [(passed(ahead, chain), passed(back, [(j, i) for i, j in chain]))]

    operands = (x_up, leaf_basis, transfer_leaf.reshape(leaves * rank, rank), transfer_mid.reshape(rank, rank), mid_couple[0], top_couple[0])
    plane, x_own, basis, leaf_map, mid_map, mid_links, group_links, *later = kernel(
        functools.partial(up_kernel, cuts[2:]),
        [resident(2 * rank, columns)] + [resident(*x.shape) for x in operands] + pieces[2:],
        [ANY] * 6,
        [VMEM] * 9,
        [pltpu.VMEM((leaves * rank, columns), bf16), pltpu.SemaphoreType.DMA((2 * leaves + 2,)), pltpu.SemaphoreType.DMA((4,))],
    )(*[held(x, pltpu.HBM) for x in operands])
    slots = leaves * near
    lists = [pltpu.SMEM((slots + 1,), jnp.int32)] * 2
    wide = resident(leaves * rows, columns, dtype=jnp.float32)
    total, blocks = kernel(
        functools.partial(own_kernel, leaves),
        (wide, resident(slots, rows, rows)),
        [SMEM, VMEM, ANY],
        (VMEM, VMEM),
        lists * 2 + [pltpu.SemaphoreType.DMA((slots,))],
        flops=1000,
    )(near_ids, held(x_own, pltpu.VMEM), held(near_blocks.reshape(slots, rows, rows), pltpu.HBM))
    blocks = held(blocks, pltpu.VMEM)
    plane = lax.all_gather(plane, "leaf", axis=0, tiled=True)
    low, high = jnp.where(inner == last, relayed, later[0]), jnp.where(inner == first, relayed, later[1])
    plane, low, high, total = lax.optimization_barrier((plane, low, high, total))
    turns = [(place(g, i), place(g, i ^ turn_of(g, inner_size))) for g in groups for i in range(inner_size)]
    planes = passed(plane, [(i, j) for i, j in turns if i != j])
    halo.append(
        (
            passed(low, line + [(place(g, last), place(g, first)) for g in groups[1:]]),
            passed(high, [(j, i) for i, j in line] + [(place(g, first), place(g, last)) for g in groups[:-1]]),
        )
    )

    planes, halo[0] = lax.optimization_barrier((planes, halo[0]))

    others = [swapped(planes, reach) for reach in range(1, inner_size)]
    total, planes = lax.optimization_barrier((total, planes))
    total = kernel(functools.partial(wave_kernel, one), wide, [SMEM] + [VMEM] * 4, VMEM, lists * 2, aliases={4: 0}, flops=10**9)(
        near_ids, *halo[0], blocks, held(total, pltpu.VMEM)
    )
    others, total = lax.optimization_barrier((others, total))
    planes = jnp.concatenate([planes, *others])
    total = kernel(
        functools.partial(down_kernel, leaf_size, inner_size), wide, [SMEM, SMEM] + [VMEM] * 8, VMEM, [], aliases={9: 0}
    )(far_ids, far_count, plane, planes, group_links, mid_links, mid_map, leaf_map, basis, held(total, pltpu.VMEM))
    out, _ = kernel(
        functools.partial(last_kernel, one),
        (jax.ShapeDtypeStruct(anomalies.shape, bf16), wide),
        [SMEM] + [VMEM] * 4,
        (ANY, VMEM),
        lists * 2 + [pltpu.VMEM(anomalies.shape, bf16), pltpu.SemaphoreType.DMA((leaves,))],
        aliases={4: 1},
    )(near_ids, *halo[1], blocks, held(total, pltpu.VMEM))
    return out


def solution(mesh):
    return jax.shard_map(
        local,
        mesh=mesh,
        in_specs=(
            P(("leaf", "inner"), "groups"),
            P(("leaf", "inner"), None, None),
            P(("leaf", "inner"), None, None, None),
            P(("leaf", "inner"), None),
            P(("leaf", "inner"), None, None),
            P(("leaf", "inner"), None, None),
            P(("leaf", "inner"), None),
            P(("leaf", "inner")),
            P(("leaf", "inner"), None, None, None),
            P("leaf", None, None, None),
        ),
        out_specs=P(("leaf", "inner"), "groups"),
        check_vma=False,
    )
```

```python
import functools

import jax
import jax.numpy as jnp
from jax import lax
from jax.experimental import pallas as pl
from jax.experimental.pallas import tpu as pltpu
from jax.sharding import PartitionSpec as P

MIB = 1 << 20
VMEM = pl.BlockSpec(memory_space=pltpu.VMEM)
SMEM = pl.BlockSpec(memory_space=pltpu.SMEM)
ANY = pl.BlockSpec(memory_space=pl.ANY)


def held(x, space):
    return pltpu.with_memory_space_constraint(x, space)


def resident(*shape, dtype=jnp.bfloat16):
    return pltpu.VMEM(shape, dtype)


def turn_of(leaf, inner_size):
    return (3 * leaf + 2) % inner_size


def carrier(turn, inner_size):
    return lax.rem((turn + inner_size - 2 % inner_size) * pow(3, -1, inner_size), inner_size)


def dot(a, b):
    return lax.dot_general(a, b, (((1,), (0,)), ((), ())), preferred_element_type=jnp.float32)


def dot_t(a, b):
    return lax.dot_general(a, b, (((0,), (0,)), ((), ())), preferred_element_type=jnp.float32)


def call(kernel, out_shape, in_specs, out_specs, scratch, flops, moved, vmem, aliases=None):
    return pl.pallas_call(
        kernel,
        out_shape=out_shape,
        in_specs=in_specs,
        out_specs=out_specs,
        scratch_shapes=scratch,
        cost_estimate=pl.CostEstimate(flops=flops, bytes_accessed=moved, transcendentals=0),
        compiler_params=pltpu.CompilerParams(vmem_limit_bytes=vmem),
        input_output_aliases=aliases or {},
    )


def up_kernel(x_ref, basis_ref, leaf_map_ref, mid_map_ref, out_ref, x, basis, leaf_map, mid_map, skeleton, sems):
    leaves, rank, rows = basis.shape
    parts = []
    for leaf in range(leaves):
        here = slice(leaf * rows, (leaf + 1) * rows)
        parts.append(pltpu.make_async_copy(x_ref.at[here], x.at[here], sems.at[leaf]))
        parts.append(pltpu.make_async_copy(basis_ref.at[leaf], basis.at[leaf], sems.at[leaves + leaf]))
    maps = [pltpu.make_async_copy(leaf_map_ref, leaf_map, sems.at[2 * leaves]), pltpu.make_async_copy(mid_map_ref, mid_map, sems.at[2 * leaves + 1])]
    for copy in parts + maps:
        copy.start()
    for leaf in range(leaves):
        parts[2 * leaf].wait()
        parts[2 * leaf + 1].wait()
        skeleton[leaf * rank : (leaf + 1) * rank, :] = dot(basis[leaf], x[leaf * rows : (leaf + 1) * rows, :]).astype(jnp.bfloat16)
    for copy in maps:
        copy.wait()
    mid = dot_t(leaf_map[...], skeleton[...]).astype(jnp.bfloat16)
    out_ref[:rank, :] = mid
    out_ref[rank:, :] = dot_t(mid_map[...], mid).astype(jnp.bfloat16)


def pieces_kernel(x_ref, relayed, low, high, sems):
    inner = lax.axis_index("inner")
    size = low.shape[0]
    ends = (inner == lax.axis_size("inner") - 1, inner == 0)
    for i, (piece, at_end, first) in enumerate(zip((low, high), ends, (0, x_ref.shape[0] - size))):

        @pl.when(at_end)
        def _():
            pltpu.make_async_copy(relayed, piece, sems.at[i]).start()

        @pl.when(jnp.logical_not(at_end))
        def _():
            pltpu.make_async_copy(x_ref.at[first : first + size], piece, sems.at[i]).start()

    for i, piece in enumerate((low, high)):
        pltpu.make_async_copy(relayed, piece, sems.at[i]).wait()


def down_kernel(leaf_size, inner_size, far_ids, far_count, plane, *refs):
    found, (couple, mid_couple, mid_map, leaf_map, basis, _, out_ref, planes) = refs[:inner_size], refs[inner_size:]
    rank = mid_map.shape[0]
    size = 2 * rank
    for step, part in enumerate(found):
        planes[step * leaf_size * size : (step + 1) * leaf_size * size, :] = part[...]
    group = lax.axis_index("leaf")
    inner = lax.axis_index("inner")

    def at_of(step, leaf, offset=0):
        return pl.ds(pl.multiple_of((step * leaf_size + leaf) * size + offset, rank), rank)

    top_down = jnp.zeros((rank, plane.shape[1]), jnp.float32)
    for distance in range(1, leaf_size):
        other = group ^ distance
        top = plane[at_of(0, other, rank), :].astype(jnp.float32)
        for step in range(inner_size):
            top += planes[at_of(step, other, rank), :].astype(jnp.float32)
        term = dot(couple[other], top.astype(jnp.bfloat16))
        top_down += jnp.where(jnp.abs(other - group) >= 2, term, 0.0)
    total = dot(mid_map[...], top_down.astype(jnp.bfloat16))
    for slot in range(mid_couple.shape[0]):
        live = slot < far_count[0]
        partner = jnp.where(live, far_ids[0, slot], group * inner_size)
        other, turn = partner // inner_size, inner ^ lax.rem(partner, inner_size)
        step = (group & (inner_size - 1)) ^ carrier(turn, inner_size)
        near, far = plane[at_of(0, other), :], planes[at_of(step, other), :]
        term = dot(mid_couple[slot], jnp.where(turn == 0, near, far))
        total += jnp.where(live, term, 0.0)
    leaf_down = dot(leaf_map[...], total.astype(jnp.bfloat16)).astype(jnp.bfloat16)
    leaves, _, rows = basis.shape
    for leaf in range(leaves):
        out_ref[leaf * rows : (leaf + 1) * rows, :] += dot_t(basis[leaf], leaf_down[leaf * rank : (leaf + 1) * rank, :])


def listed(ids_ref, lists, kind_of):
    leaves, near = ids_ref.shape
    first = (lax.axis_index("leaf") * lax.axis_size("inner") + lax.axis_index("inner")) * leaves

    def one(leaf, counts):
        for k in range(near):
            offset = ids_ref[leaf, k] - first
            grown = []
            for (slots, places), count, (member, place) in zip(lists, counts, kind_of(leaf, offset)):
                slots[count] = leaf * near + k
                places[count] = place
                grown.append(count + member.astype(jnp.int32))
            counts = tuple(grown)
        return counts

    return lax.fori_loop(0, leaves, one, (jnp.int32(0),) * len(lists))


def add_products(near, kind, count, blocks, x_ref, total, arrived=lambda slot: None):
    slots, places = kind
    rows = blocks.shape[1]

    def product(i):
        slot = slots[i]
        arrived(slot)
        at = pl.ds(pl.multiple_of(places[i] * rows, rows), rows)
        here = pl.ds(pl.multiple_of(slot // near * rows, rows), rows)
        return here, dot(blocks[slot], x_ref[at, :])

    def pair(j, carry):
        one, first = product(2 * j)
        two, second = product(2 * j + 1)
        total[one, :] += first
        total[two, :] += second
        return carry

    lax.fori_loop(0, count // 2, pair, 0)

    @pl.when(lax.rem(count, 2) == 1)
    def _():
        here, term = product(count - 1)
        total[here, :] += term


def own_kernel(ids_ref, x_hbm, blocks_ref, *refs):
    count = (len(refs) - 8) // 2
    sources, total, blocks, targets = refs[:count], refs[count], refs[count + 1], refs[count + 2 : 2 * count + 2]
    own_slots, own_places, other_slots, other_places, x_ref, sems = refs[2 * count + 2 :]
    leaves, near = ids_ref.shape
    slots = leaves * near
    load = pltpu.make_async_copy(x_hbm, x_ref, sems.at[slots])
    load.start()

    def kind_of(leaf, offset):
        own = (offset >= 0) & (offset < leaves)
        return (own, offset), (jnp.logical_not(own), 0)

    kinds = ((own_slots, own_places), (other_slots, other_places))
    own_count, other_count = listed(ids_ref, kinds, kind_of)

    def copy(slot):
        return pltpu.make_async_copy(blocks_ref.at[slot], blocks.at[slot], sems.at[slot])

    def begin(slots):
        def one(i, carry):
            copy(slots[i]).start()
            return carry

        return one

    lax.fori_loop(0, own_count, begin(own_slots), 0)
    lax.fori_loop(0, other_count, begin(other_slots), 0)
    others = [pltpu.make_async_copy(source, target, sems.at[slots + 1 + i]) for i, (source, target) in enumerate(zip(sources, targets))]
    for other in others:
        other.start()
    total[...] = jnp.zeros_like(total)
    load.wait()
    add_products(near, kinds[0], own_count, blocks, x_ref, total, lambda slot: copy(slot).wait())

    def finish(i, carry):
        copy(other_slots[i]).wait()
        return carry

    lax.fori_loop(0, other_count, finish, 0)
    for other in others:
        other.wait()


def wave_kernel(near_by, ids_ref, before, after, blocks, _, total, *lists):
    leaves, near = ids_ref.shape

    def kind_of(leaf, offset):
        return ((offset < 0) & (offset >= -near_by), offset + near_by), ((offset >= leaves) & (offset < leaves + near_by), offset - leaves)

    kinds = (lists[:2], lists[2:])
    counts = listed(ids_ref, kinds, kind_of)
    for kind, count, x_ref in zip(kinds, counts, (before, after)):
        add_products(near, kind, count, blocks, x_ref, total)


def last_kernel(near_by, ids_ref, before, after, blocks, _, out_ref, total, *refs):
    lists, (result, sems) = refs[:4], refs[4:]
    leaves, near = ids_ref.shape
    rows = blocks.shape[1]

    def kind_of(leaf, offset):
        return (offset < -near_by, offset + leaves), (offset >= leaves + near_by, offset - leaves - near_by)

    kinds = (lists[:2], lists[2:])
    counts = listed(ids_ref, kinds, kind_of)
    for kind, count, x_ref in zip(kinds, counts, (before, after)):
        add_products(near, kind, count, blocks, x_ref, total)
    stores = []
    for leaf in range(leaves):
        here = slice(leaf * rows, (leaf + 1) * rows)
        result[here, :] = total[here, :].astype(result.dtype)
        stores.append(pltpu.make_async_copy(result.at[here], out_ref.at[here], sems.at[leaf]))
        stores[-1].start()
    for store in stores:
        store.wait()


def local(anomalies, leaf_basis, near_blocks, near_ids, transfer_leaf, transfer_mid, far_ids, far_count, mid_couple, top_couple):
    leaves, rank, rows = leaf_basis.shape
    near = near_blocks.shape[1]
    columns = anomalies.shape[1]
    inner_size = lax.axis_size("inner")
    leaf_size = lax.axis_size("leaf")
    bf16 = jnp.bfloat16
    inner = lax.axis_index("inner")
    first, last = 0, inner_size - 1
    groups = range(leaf_size)

    def place(leaf, i):
        return leaf * inner_size + i

    def passed(x, pairs):
        return lax.ppermute(x, ("leaf", "inner"), pairs)

    def swapped(x, reach):
        return lax.ppermute(x, "leaf", [(i, i ^ reach) for i in groups])

    chain = [(i, i + 1) for i in range(leaf_size * inner_size - 1)]
    line = [(place(g, i), place(g, i + 1)) for g in groups for i in range(last)]
    hop = [(place(g, last), place(g + 1, last)) for g in groups[:-1]] + [(place(g, first), place(g - 1, first)) for g in groups[1:]]

    one = leaves * 5 // 8
    rest = leaves - one
    def kernel(body, out_shape, in_specs, out_specs, scratch, aliases=None, flops=1000):
        return call(body, out_shape, in_specs, out_specs, scratch, flops, 1000, 8 * MIB, aliases)

    ahead, back = lax.slice_in_dim(anomalies, rest * rows, leaves * rows), lax.slice_in_dim(anomalies, 0, one * rows)
    edge = jnp.where(inner == first, one * rows, 0)
    relayed = passed(lax.dynamic_slice_in_dim(anomalies, edge, rest * rows), hop)
    x_up, ahead, back = lax.optimization_barrier((anomalies, ahead, back))
    halo = [(passed(ahead, chain), passed(back, [(j, i) for i, j in chain]))]

    maps = (transfer_leaf.reshape(leaves * rank, rank), transfer_mid.reshape(rank, rank))
    operands = (x_up, leaf_basis, *maps)
    part = kernel(
        up_kernel,
        jax.ShapeDtypeStruct((2 * rank, columns), bf16),
        [ANY] * 4,
        VMEM,
        [pltpu.VMEM(x.shape, bf16) for x in operands] + [pltpu.VMEM((leaves * rank, columns), bf16), pltpu.SemaphoreType.DMA((2 * leaves + 2,))],
    )(*[held(x, pltpu.HBM) for x in operands])
    plane = lax.all_gather(part, "leaf", axis=0, tiled=True)
    plane, x_late, relayed = lax.optimization_barrier((plane, x_up, relayed))
    piece = jax.ShapeDtypeStruct((rest * rows, columns), bf16)
    low, high = kernel(pieces_kernel, (piece, piece), [ANY] * 2, (VMEM, VMEM), [pltpu.SemaphoreType.DMA((2,))])(held(x_late, pltpu.HBM), relayed)
    plane, x_late, low, high = lax.optimization_barrier((plane, x_late, low, high))
    turns = [(place(g, i), place(g, i ^ turn_of(g, inner_size))) for g in groups for i in range(inner_size)]
    planes = passed(plane, [(i, j) for i, j in turns if i != j])
    halo.append(
        (
            passed(low, line + [(place(g, last), place(g, first)) for g in groups[1:]]),
            passed(high, [(j, i) for i, j in line] + [(place(g, first), place(g, last)) for g in groups[:-1]]),
        )
    )

    slots = leaves * near
    lists = [pltpu.SMEM((slots + 1,), jnp.int32)] * 2
    wide = resident(leaves * rows, columns, dtype=jnp.float32)
    later = (top_couple[0], mid_couple[0], maps[1], maps[0], leaf_basis)
    total, blocks, *later = kernel(
        own_kernel,
        [wide, resident(slots, rows, rows)] + [resident(*x.shape) for x in later],
        [SMEM] + [ANY] * (2 + len(later)),
        [VMEM] * (2 + len(later)),
        lists * 2 + [pltpu.VMEM(anomalies.shape, bf16), pltpu.SemaphoreType.DMA((slots + 1 + len(later),))],
    )(near_ids, *[held(x, pltpu.HBM) for x in (x_late, near_blocks.reshape(slots, rows, rows), *later)])
    blocks = held(blocks, pltpu.VMEM)
    planes, halo[0], total = lax.optimization_barrier((planes, halo[0], total))
    others = [swapped(planes, reach) for reach in range(1, inner_size)]
    total, planes = lax.optimization_barrier((total, planes))
    total = kernel(functools.partial(wave_kernel, one), wide, [SMEM] + [VMEM] * 4, VMEM, lists * 2, aliases={4: 0}, flops=10**10)(
        near_ids, *halo[0], blocks, held(total, pltpu.VMEM)
    )
    others, total = lax.optimization_barrier((others, total))
    total = kernel(
        functools.partial(down_kernel, leaf_size, inner_size),
        wide,
        [SMEM, SMEM] + [VMEM] * (7 + inner_size),
        VMEM,
        [pltpu.VMEM((inner_size * leaf_size * 2 * rank, columns), bf16)],
        aliases={8 + inner_size: 0},
    )(far_ids, far_count, plane, planes, *others, *later, held(total, pltpu.VMEM))
    out, _ = kernel(
        functools.partial(last_kernel, one),
        (jax.ShapeDtypeStruct(anomalies.shape, bf16), wide),
        [SMEM] + [VMEM] * 4,
        (ANY, VMEM),
        lists * 2 + [pltpu.VMEM(anomalies.shape, bf16), pltpu.SemaphoreType.DMA((leaves,))],
        aliases={4: 1},
    )(near_ids, *halo[1], blocks, held(total, pltpu.VMEM))
    return out


def solution(mesh):
    return jax.shard_map(
        local,
        mesh=mesh,
        in_specs=(
            P(("leaf", "inner"), "groups"),
            P(("leaf", "inner"), None, None),
            P(("leaf", "inner"), None, None, None),
            P(("leaf", "inner"), None),
            P(("leaf", "inner"), None, None),
            P(("leaf", "inner"), None, None),
            P(("leaf", "inner"), None),
            P(("leaf", "inner")),
            P(("leaf", "inner"), None, None, None),
            P("leaf", None, None, None),
        ),
        out_specs=P(("leaf", "inner"), "groups"),
        check_vma=False,
    )
```

```python
import functools

import jax
import jax.numpy as jnp
from jax import lax
from jax.experimental import pallas as pl
from jax.experimental.pallas import tpu as pltpu
from jax.sharding import PartitionSpec as P

MIB = 1 << 20
VMEM = pl.BlockSpec(memory_space=pltpu.VMEM)
SMEM = pl.BlockSpec(memory_space=pltpu.SMEM)
ANY = pl.BlockSpec(memory_space=pl.ANY)


def held(x, space):
    return pltpu.with_memory_space_constraint(x, space)


def resident(*shape, dtype=jnp.bfloat16):
    return pltpu.VMEM(shape, dtype)


def turn_of(leaf, inner_size):
    return (3 * leaf + 2) % inner_size


def carrier(turn, inner_size):
    return lax.rem((turn + inner_size - 2 % inner_size) * pow(3, -1, inner_size), inner_size)


def dot(a, b):
    return lax.dot_general(a, b, (((1,), (0,)), ((), ())), preferred_element_type=jnp.float32)


def dot_t(a, b):
    return lax.dot_general(a, b, (((0,), (0,)), ((), ())), preferred_element_type=jnp.float32)


def call(kernel, out_shape, in_specs, out_specs, scratch, flops, moved, vmem, aliases=None):
    return pl.pallas_call(
        kernel,
        out_shape=out_shape,
        in_specs=in_specs,
        out_specs=out_specs,
        scratch_shapes=scratch,
        cost_estimate=pl.CostEstimate(flops=flops, bytes_accessed=moved, transcendentals=0),
        compiler_params=pltpu.CompilerParams(vmem_limit_bytes=vmem),
        input_output_aliases=aliases or {},
    )


def up_kernel(x_ref, basis_ref, leaf_map_ref, mid_map_ref, out_ref, relay, x, basis, leaf_map, mid_map, skeleton, sems):
    leaves, rank, rows = basis.shape
    parts = []
    for leaf in range(leaves):
        here = slice(leaf * rows, (leaf + 1) * rows)
        parts.append(pltpu.make_async_copy(x_ref.at[here], x.at[here], sems.at[leaf]))
        parts.append(pltpu.make_async_copy(basis_ref.at[leaf], basis.at[leaf], sems.at[leaves + leaf]))
    maps = [pltpu.make_async_copy(leaf_map_ref, leaf_map, sems.at[2 * leaves]), pltpu.make_async_copy(mid_map_ref, mid_map, sems.at[2 * leaves + 1])]
    edge = jnp.where(lax.axis_index("inner") == 0, x.shape[0] - relay.shape[0], 0)
    handed = pltpu.make_async_copy(x_ref.at[pl.ds(pl.multiple_of(edge, rows), relay.shape[0])], relay, sems.at[2 * leaves + 2])
    for copy in [*parts, *maps, handed]:
        copy.start()
    for leaf in range(leaves):
        parts[2 * leaf].wait()
        parts[2 * leaf + 1].wait()
        skeleton[leaf * rank : (leaf + 1) * rank, :] = dot(basis[leaf], x[leaf * rows : (leaf + 1) * rows, :]).astype(jnp.bfloat16)
    for copy in maps:
        copy.wait()
    mid = dot_t(leaf_map[...], skeleton[...]).astype(jnp.bfloat16)
    out_ref[:rank, :] = mid
    out_ref[rank:, :] = dot_t(mid_map[...], mid).astype(jnp.bfloat16)
    handed.wait()


def pieces_kernel(x_ref, relayed, *refs):
    parts, (low, high, plane, sems) = refs[:-4], refs[-4:]
    inner = lax.axis_index("inner")
    size = low.shape[0]
    ends = (inner == lax.axis_size("inner") - 1, inner == 0)
    for i, (piece, at_end, first) in enumerate(zip((low, high), ends, (0, x_ref.shape[0] - size))):

        @pl.when(at_end)
        def _():
            pltpu.make_async_copy(relayed, piece, sems.at[i]).start()

        @pl.when(jnp.logical_not(at_end))
        def _():
            pltpu.make_async_copy(x_ref.at[first : first + size], piece, sems.at[i]).start()

    height = parts[0].shape[0]
    for i, part in enumerate(parts):
        plane[i * height : (i + 1) * height, :] = part[...]
    for i, piece in enumerate((low, high)):
        pltpu.make_async_copy(relayed, piece, sems.at[i]).wait()


def down_kernel(leaf_size, inner_size, far_ids, far_count, plane, *refs):
    found, (couple, mid_couple, mid_map, leaf_map, basis, _, out_ref, planes) = refs[:inner_size], refs[inner_size:]
    rank = mid_map.shape[0]
    size = 2 * rank
    for step, part in enumerate(found):
        planes[step * leaf_size * size : (step + 1) * leaf_size * size, :] = part[...]
    group = lax.axis_index("leaf")
    inner = lax.axis_index("inner")

    def at_of(step, distance, offset=0):
        return pl.ds(pl.multiple_of((step * leaf_size + distance) * size + offset, rank), rank)

    top_down = jnp.zeros((rank, plane.shape[1]), jnp.float32)
    for distance in range(1, leaf_size):
        other = group ^ distance
        top = plane[at_of(0, distance, rank), :].astype(jnp.float32)
        for step in range(inner_size):
            top += planes[at_of(step, step ^ distance, rank), :].astype(jnp.float32)
        term = dot(couple[other], top.astype(jnp.bfloat16))
        top_down += jnp.where(jnp.abs(other - group) >= 2, term, 0.0)
    total = dot(mid_map[...], top_down.astype(jnp.bfloat16))
    for slot in range(mid_couple.shape[0]):
        live = slot < far_count[0]
        partner = jnp.where(live, far_ids[0, slot], group * inner_size)
        other, turn = partner // inner_size, inner ^ lax.rem(partner, inner_size)
        step = (group & (inner_size - 1)) ^ carrier(turn, inner_size)
        near, far = plane[at_of(0, group ^ other), :], planes[at_of(step, group ^ step ^ other), :]
        term = dot(mid_couple[slot], jnp.where(turn == 0, near, far))
        total += jnp.where(live, term, 0.0)
    leaf_down = dot(leaf_map[...], total.astype(jnp.bfloat16)).astype(jnp.bfloat16)
    leaves, _, rows = basis.shape
    for leaf in range(leaves):
        out_ref[leaf * rows : (leaf + 1) * rows, :] += dot_t(basis[leaf], leaf_down[leaf * rank : (leaf + 1) * rank, :])


def listed(ids_ref, lists, kind_of):
    leaves, near = ids_ref.shape
    first = (lax.axis_index("leaf") * lax.axis_size("inner") + lax.axis_index("inner")) * leaves

    def one(leaf, counts):
        for k in range(near):
            offset = ids_ref[leaf, k] - first
            grown = []
            for (slots, places), count, (member, place) in zip(lists, counts, kind_of(leaf, offset)):
                slots[count] = leaf * near + k
                places[count] = place
                grown.append(count + member.astype(jnp.int32))
            counts = tuple(grown)
        return counts

    return lax.fori_loop(0, leaves, one, (jnp.int32(0),) * len(lists))


def add_products(near, kind, count, blocks, x_ref, total, arrived=lambda slot: None):
    slots, places = kind
    rows = blocks.shape[1]

    def product(i):
        slot = slots[i]
        arrived(slot)
        at = pl.ds(pl.multiple_of(places[i] * rows, rows), rows)
        here = pl.ds(pl.multiple_of(slot // near * rows, rows), rows)
        return here, dot(blocks[slot], x_ref[at, :])

    def pair(j, carry):
        one, first = product(2 * j)
        two, second = product(2 * j + 1)
        total[one, :] += first
        total[two, :] += second
        return carry

    lax.fori_loop(0, count // 2, pair, 0)

    @pl.when(lax.rem(count, 2) == 1)
    def _():
        here, term = product(count - 1)
        total[here, :] += term


def own_kernel(ids_ref, x_hbm, blocks_ref, *refs):
    count = (len(refs) - 8) // 2
    sources, total, blocks, targets = refs[:count], refs[count], refs[count + 1], refs[count + 2 : 2 * count + 2]
    own_slots, own_places, other_slots, other_places, x_ref, sems = refs[2 * count + 2 :]
    leaves, near = ids_ref.shape
    slots = leaves * near
    load = pltpu.make_async_copy(x_hbm, x_ref, sems.at[slots])
    load.start()

    def kind_of(leaf, offset):
        own = (offset >= 0) & (offset < leaves)
        return (own, offset), (jnp.logical_not(own), 0)

    kinds = ((own_slots, own_places), (other_slots, other_places))
    own_count, other_count = listed(ids_ref, kinds, kind_of)

    def copy(slot):
        return pltpu.make_async_copy(blocks_ref.at[slot], blocks.at[slot], sems.at[slot])

    def begin(slots):
        def one(i, carry):
            copy(slots[i]).start()
            return carry

        return one

    lax.fori_loop(0, own_count, begin(own_slots), 0)
    lax.fori_loop(0, other_count, begin(other_slots), 0)
    others = [pltpu.make_async_copy(source, target, sems.at[slots + 1 + i]) for i, (source, target) in enumerate(zip(sources, targets))]
    for other in others:
        other.start()
    total[...] = jnp.zeros_like(total)
    load.wait()
    add_products(near, kinds[0], own_count, blocks, x_ref, total, lambda slot: copy(slot).wait())

    def finish(i, carry):
        copy(other_slots[i]).wait()
        return carry

    lax.fori_loop(0, other_count, finish, 0)
    for other in others:
        other.wait()


def wave_kernel(near_by, ids_ref, before, after, blocks, _, total, *lists):
    leaves, near = ids_ref.shape

    def kind_of(leaf, offset):
        return ((offset < 0) & (offset >= -near_by), offset + near_by), ((offset >= leaves) & (offset < leaves + near_by), offset - leaves)

    kinds = (lists[:2], lists[2:])
    counts = listed(ids_ref, kinds, kind_of)
    for kind, count, x_ref in zip(kinds, counts, (before, after)):
        add_products(near, kind, count, blocks, x_ref, total)


def last_kernel(near_by, ids_ref, before, after, blocks, _, out_ref, total, *refs):
    lists, (result, sems) = refs[:4], refs[4:]
    leaves, near = ids_ref.shape
    rows = blocks.shape[1]

    def kind_of(leaf, offset):
        return (offset < -near_by, offset + leaves), (offset >= leaves + near_by, offset - leaves - near_by)

    kinds = (lists[:2], lists[2:])
    counts = listed(ids_ref, kinds, kind_of)
    for kind, count, x_ref in zip(kinds, counts, (before, after)):
        add_products(near, kind, count, blocks, x_ref, total)
    stores = []
    for leaf in range(leaves):
        here = slice(leaf * rows, (leaf + 1) * rows)
        result[here, :] = total[here, :].astype(result.dtype)
        stores.append(pltpu.make_async_copy(result.at[here], out_ref.at[here], sems.at[leaf]))
        stores[-1].start()
    for store in stores:
        store.wait()


def local(anomalies, leaf_basis, near_blocks, near_ids, transfer_leaf, transfer_mid, far_ids, far_count, mid_couple, top_couple):
    leaves, rank, rows = leaf_basis.shape
    near = near_blocks.shape[1]
    columns = anomalies.shape[1]
    inner_size = lax.axis_size("inner")
    leaf_size = lax.axis_size("leaf")
    bf16 = jnp.bfloat16
    inner = lax.axis_index("inner")
    first, last = 0, inner_size - 1
    groups = range(leaf_size)

    def place(leaf, i):
        return leaf * inner_size + i

    def passed(x, pairs):
        return lax.ppermute(x, ("leaf", "inner"), pairs)

    def swapped(x, reach):
        return lax.ppermute(x, "leaf", [(i, i ^ reach) for i in groups])

    chain = [(i, i + 1) for i in range(leaf_size * inner_size - 1)]
    line = [(place(g, i), place(g, i + 1)) for g in groups for i in range(last)]
    hop = [(place(g, last), place(g + 1, last)) for g in groups[:-1]] + [(place(g, first), place(g - 1, first)) for g in groups[1:]]

    one = leaves * 3 // 4
    rest = leaves - one
    def kernel(body, out_shape, in_specs, out_specs, scratch, aliases=None, flops=1000):
        return call(body, out_shape, in_specs, out_specs, scratch, flops, 1000, 8 * MIB, aliases)

    ahead, back = lax.slice_in_dim(anomalies, rest * rows, leaves * rows), lax.slice_in_dim(anomalies, 0, one * rows)
    x_up, ahead, back = lax.optimization_barrier((anomalies, ahead, back))
    halo = [(passed(ahead, chain), passed(back, [(j, i) for i, j in chain]))]

    maps = (transfer_leaf.reshape(leaves * rank, rank), transfer_mid.reshape(rank, rank))
    operands = (x_up, leaf_basis, *maps)
    piece = jax.ShapeDtypeStruct((rest * rows, columns), bf16)
    part, relay = kernel(
        up_kernel,
        (jax.ShapeDtypeStruct((2 * rank, columns), bf16), piece),
        [ANY] * 4,
        (VMEM, VMEM),
        [pltpu.VMEM(x.shape, bf16) for x in operands] + [pltpu.VMEM((leaves * rank, columns), bf16), pltpu.SemaphoreType.DMA((2 * leaves + 3,))],
    )(*[held(x, pltpu.HBM) for x in operands])
    relayed = passed(relay, hop)
    parts = [part] + [swapped(part, reach) for reach in groups[1:]]
    x_late, part = lax.optimization_barrier((x_up, part))

    slots = leaves * near
    lists = [pltpu.SMEM((slots + 1,), jnp.int32)] * 2
    wide = resident(leaves * rows, columns, dtype=jnp.float32)
    later = (top_couple[0], mid_couple[0], maps[1], maps[0], leaf_basis)
    total, blocks, *later = kernel(
        own_kernel,
        [wide, resident(slots, rows, rows)] + [resident(*x.shape) for x in later],
        [SMEM] + [ANY] * (2 + len(later)),
        [VMEM] * (2 + len(later)),
        lists * 2 + [pltpu.VMEM(anomalies.shape, bf16), pltpu.SemaphoreType.DMA((slots + 1 + len(later),))],
        flops=1000,
    )(near_ids, *[held(x, pltpu.HBM) for x in (x_late, near_blocks.reshape(slots, rows, rows), *later)])
    blocks = held(blocks, pltpu.VMEM)
    parts, x_late, relayed, total = lax.optimization_barrier((parts, x_late, relayed, total))
    low, high, plane = kernel(
        pieces_kernel,
        (piece, piece, jax.ShapeDtypeStruct((leaf_size * 2 * rank, columns), bf16)),
        [ANY] * 2 + [VMEM] * leaf_size,
        [VMEM] * 3,
        [pltpu.SemaphoreType.DMA((2,))],
    )(held(x_late, pltpu.HBM), relayed, *parts)
    turns = [(place(g, i), place(g, i ^ turn_of(g, inner_size))) for g in groups for i in range(inner_size)]
    planes = passed(plane, [(i, j) for i, j in turns if i != j])
    halo.append(
        (
            passed(low, line + [(place(g, last), place(g, first)) for g in groups[1:]]),
            passed(high, [(j, i) for i, j in line] + [(place(g, first), place(g, last)) for g in groups[:-1]]),
        )
    )
    planes, halo[0], total = lax.optimization_barrier((planes, halo[0], total))
    others = [swapped(planes, reach) for reach in range(1, inner_size)]
    total, planes = lax.optimization_barrier((total, planes))
    total = kernel(functools.partial(wave_kernel, one), wide, [SMEM] + [VMEM] * 4, VMEM, lists * 2, aliases={4: 0}, flops=10**10)(
        near_ids, *halo[0], blocks, held(total, pltpu.VMEM)
    )
    others, total = lax.optimization_barrier((others, total))
    total = kernel(
        functools.partial(down_kernel, leaf_size, inner_size),
        wide,
        [SMEM, SMEM] + [VMEM] * (7 + inner_size),
        VMEM,
        [pltpu.VMEM((inner_size * leaf_size * 2 * rank, columns), bf16)],
        aliases={8 + inner_size: 0},
    )(far_ids, far_count, plane, planes, *others, *later, held(total, pltpu.VMEM))
    out, _ = kernel(
        functools.partial(last_kernel, one),
        (jax.ShapeDtypeStruct(anomalies.shape, bf16), wide),
        [SMEM] + [VMEM] * 4,
        (ANY, VMEM),
        lists * 2 + [pltpu.VMEM(anomalies.shape, bf16), pltpu.SemaphoreType.DMA((leaves,))],
        aliases={4: 1},
    )(near_ids, *halo[1], blocks, held(total, pltpu.VMEM))
    return out


def solution(mesh):
    return jax.shard_map(
        local,
        mesh=mesh,
        in_specs=(
            P(("leaf", "inner"), "groups"),
            P(("leaf", "inner"), None, None),
            P(("leaf", "inner"), None, None, None),
            P(("leaf", "inner"), None),
            P(("leaf", "inner"), None, None),
            P(("leaf", "inner"), None, None),
            P(("leaf", "inner"), None),
            P(("leaf", "inner")),
            P(("leaf", "inner"), None, None, None),
            P("leaf", None, None, None),
        ),
        out_specs=P(("leaf", "inner"), "groups"),
        check_vma=False,
    )
```

```python
import functools

import jax
import jax.numpy as jnp
from jax import lax
from jax.experimental import pallas as pl
from jax.experimental.pallas import tpu as pltpu
from jax.sharding import PartitionSpec as P

MIB = 1 << 20
VMEM = pl.BlockSpec(memory_space=pltpu.VMEM)
SMEM = pl.BlockSpec(memory_space=pltpu.SMEM)
ANY = pl.BlockSpec(memory_space=pl.ANY)


def held(x, space):
    return pltpu.with_memory_space_constraint(x, space)


def resident(*shape, dtype=jnp.bfloat16):
    return pltpu.VMEM(shape, dtype)


def turn_of(leaf, inner_size):
    return (3 * leaf + 2) % inner_size


def carrier(turn, inner_size):
    return lax.rem((turn + inner_size - 2 % inner_size) * pow(3, -1, inner_size), inner_size)


def dot(a, b):
    return lax.dot_general(a, b, (((1,), (0,)), ((), ())), preferred_element_type=jnp.float32)


def dot_t(a, b):
    return lax.dot_general(a, b, (((0,), (0,)), ((), ())), preferred_element_type=jnp.float32)


def call(kernel, out_shape, in_specs, out_specs, scratch, flops, moved, vmem, aliases=None):
    return pl.pallas_call(
        kernel,
        out_shape=out_shape,
        in_specs=in_specs,
        out_specs=out_specs,
        scratch_shapes=scratch,
        cost_estimate=pl.CostEstimate(flops=flops, bytes_accessed=moved, transcendentals=0),
        compiler_params=pltpu.CompilerParams(vmem_limit_bytes=vmem),
        input_output_aliases=aliases or {},
    )


def up_kernel(x_ref, basis_ref, leaf_map_ref, mid_map_ref, out_ref, relay, x, basis, leaf_map, mid_map, skeleton, sems):
    leaves, rank, rows = basis.shape
    parts = []
    for leaf in range(leaves):
        here = slice(leaf * rows, (leaf + 1) * rows)
        parts.append(pltpu.make_async_copy(x_ref.at[here], x.at[here], sems.at[leaf]))
        parts.append(pltpu.make_async_copy(basis_ref.at[leaf], basis.at[leaf], sems.at[leaves + leaf]))
    maps = [pltpu.make_async_copy(leaf_map_ref, leaf_map, sems.at[2 * leaves]), pltpu.make_async_copy(mid_map_ref, mid_map, sems.at[2 * leaves + 1])]
    edge = jnp.where(lax.axis_index("inner") == 0, x.shape[0] - relay.shape[0], 0)
    handed = pltpu.make_async_copy(x_ref.at[pl.ds(pl.multiple_of(edge, rows), relay.shape[0])], relay, sems.at[2 * leaves + 2])
    for copy in [*parts, *maps, handed]:
        copy.start()
    for leaf in range(leaves):
        parts[2 * leaf].wait()
        parts[2 * leaf + 1].wait()
        skeleton[leaf * rank : (leaf + 1) * rank, :] = dot(basis[leaf], x[leaf * rows : (leaf + 1) * rows, :]).astype(jnp.bfloat16)
    for copy in maps:
        copy.wait()
    mid = dot_t(leaf_map[...], skeleton[...]).astype(jnp.bfloat16)
    out_ref[:rank, :] = mid
    out_ref[rank:, :] = dot_t(mid_map[...], mid).astype(jnp.bfloat16)
    handed.wait()


def pieces_kernel(x_ref, relayed, *refs):
    parts, (low, high, plane, sems) = refs[:-4], refs[-4:]
    inner = lax.axis_index("inner")
    size = low.shape[0]
    ends = (inner == lax.axis_size("inner") - 1, inner == 0)
    for i, (piece, at_end, first) in enumerate(zip((low, high), ends, (0, x_ref.shape[0] - size))):

        @pl.when(at_end)
        def _():
            pltpu.make_async_copy(relayed, piece, sems.at[i]).start()

        @pl.when(jnp.logical_not(at_end))
        def _():
            pltpu.make_async_copy(x_ref.at[first : first + size], piece, sems.at[i]).start()

    height = parts[0].shape[0]
    for i, part in enumerate(parts):
        plane[i * height : (i + 1) * height, :] = part[...]
    for i, piece in enumerate((low, high)):
        pltpu.make_async_copy(relayed, piece, sems.at[i]).wait()


def down_kernel(leaf_size, inner_size, far_ids, far_count, plane, *refs):
    found, (couple, mid_couple, mid_map, leaf_map, basis, _, out_ref, planes) = refs[:inner_size], refs[inner_size:]
    rank = mid_map.shape[0]
    size = 2 * rank
    for step, part in enumerate(found):
        planes[step * leaf_size * size : (step + 1) * leaf_size * size, :] = part[...]
    group = lax.axis_index("leaf")
    inner = lax.axis_index("inner")

    def at_of(step, distance, offset=0):
        return pl.ds(pl.multiple_of((step * leaf_size + distance) * size + offset, rank), rank)

    top_down = jnp.zeros((rank, plane.shape[1]), jnp.float32)
    for distance in range(1, leaf_size):
        other = group ^ distance
        top = plane[at_of(0, distance, rank), :].astype(jnp.float32)
        for step in range(inner_size):
            top += planes[at_of(step, step ^ distance, rank), :].astype(jnp.float32)
        term = dot(couple[other], top.astype(jnp.bfloat16))
        top_down += jnp.where(jnp.abs(other - group) >= 2, term, 0.0)
    total = dot(mid_map[...], top_down.astype(jnp.bfloat16))
    for slot in range(mid_couple.shape[0]):
        live = slot < far_count[0]
        partner = jnp.where(live, far_ids[0, slot], group * inner_size)
        other, turn = partner // inner_size, inner ^ lax.rem(partner, inner_size)
        step = (group & (inner_size - 1)) ^ carrier(turn, inner_size)
        near, far = plane[at_of(0, group ^ other), :], planes[at_of(step, group ^ step ^ other), :]
        term = dot(mid_couple[slot], jnp.where(turn == 0, near, far))
        total += jnp.where(live, term, 0.0)
    leaf_down = dot(leaf_map[...], total.astype(jnp.bfloat16)).astype(jnp.bfloat16)
    leaves, _, rows = basis.shape
    for leaf in range(leaves):
        out_ref[leaf * rows : (leaf + 1) * rows, :] += dot_t(basis[leaf], leaf_down[leaf * rank : (leaf + 1) * rank, :])


def listed(ids_ref, lists, kind_of):
    leaves, near = ids_ref.shape
    first = (lax.axis_index("leaf") * lax.axis_size("inner") + lax.axis_index("inner")) * leaves

    def one(leaf, counts):
        for k in range(near):
            offset = ids_ref[leaf, k] - first
            grown = []
            for (slots, places), count, (member, place) in zip(lists, counts, kind_of(leaf, offset)):
                slots[count] = leaf * near + k
                places[count] = place
                grown.append(count + member.astype(jnp.int32))
            counts = tuple(grown)
        return counts

    return lax.fori_loop(0, leaves, one, (jnp.int32(0),) * len(lists))


def add_products(near, kind, count, blocks, x_ref, total, arrived=lambda slot: None):
    slots, places = kind
    rows = blocks.shape[1]

    def product(i):
        slot = slots[i]
        arrived(slot)
        at = pl.ds(pl.multiple_of(places[i] * rows, rows), rows)
        here = pl.ds(pl.multiple_of(slot // near * rows, rows), rows)
        return here, dot(blocks[slot], x_ref[at, :])

    def pair(j, carry):
        one, first = product(2 * j)
        two, second = product(2 * j + 1)
        total[one, :] += first
        total[two, :] += second
        return carry

    lax.fori_loop(0, count // 2, pair, 0)

    @pl.when(lax.rem(count, 2) == 1)
    def _():
        here, term = product(count - 1)
        total[here, :] += term


def own_kernel(ids_ref, x_hbm, blocks_ref, *refs):
    count = (len(refs) - 8) // 2
    sources, total, blocks, targets = refs[:count], refs[count], refs[count + 1], refs[count + 2 : 2 * count + 2]
    own_slots, own_places, other_slots, other_places, x_ref, sems = refs[2 * count + 2 :]
    leaves, near = ids_ref.shape
    slots = leaves * near
    load = pltpu.make_async_copy(x_hbm, x_ref, sems.at[slots])
    load.start()

    def kind_of(leaf, offset):
        own = (offset >= 0) & (offset < leaves)
        return (own, offset), (jnp.logical_not(own), 0)

    kinds = ((own_slots, own_places), (other_slots, other_places))
    own_count, other_count = listed(ids_ref, kinds, kind_of)

    def copy(slot):
        return pltpu.make_async_copy(blocks_ref.at[slot], blocks.at[slot], sems.at[slot])

    def begin(slots):
        def one(i, carry):
            copy(slots[i]).start()
            return carry

        return one

    lax.fori_loop(0, own_count, begin(own_slots), 0)
    lax.fori_loop(0, other_count, begin(other_slots), 0)
    others = [pltpu.make_async_copy(source, target, sems.at[slots + 1 + i]) for i, (source, target) in enumerate(zip(sources, targets))]
    for other in others:
        other.start()
    total[...] = jnp.zeros_like(total)
    load.wait()
    add_products(near, kinds[0], own_count, blocks, x_ref, total, lambda slot: copy(slot).wait())

    def finish(i, carry):
        copy(other_slots[i]).wait()
        return carry

    lax.fori_loop(0, other_count, finish, 0)
    for other in others:
        other.wait()


def wave_kernel(near_by, ids_ref, before, after, blocks, _, total, *lists):
    leaves, near = ids_ref.shape

    def kind_of(leaf, offset):
        return ((offset < 0) & (offset >= -near_by), offset + near_by), ((offset >= leaves) & (offset < leaves + near_by), offset - leaves)

    kinds = (lists[:2], lists[2:])
    counts = listed(ids_ref, kinds, kind_of)
    for kind, count, x_ref in zip(kinds, counts, (before, after)):
        add_products(near, kind, count, blocks, x_ref, total)


def last_kernel(near_by, ids_ref, before, after, blocks, _, out_ref, total, *refs):
    lists, (result, sems) = refs[:4], refs[4:]
    leaves, near = ids_ref.shape
    rows = blocks.shape[1]

    def kind_of(leaf, offset):
        return (offset < -near_by, offset + leaves), (offset >= leaves + near_by, offset - leaves - near_by)

    kinds = (lists[:2], lists[2:])
    counts = listed(ids_ref, kinds, kind_of)
    for kind, count, x_ref in zip(kinds, counts, (before, after)):
        add_products(near, kind, count, blocks, x_ref, total)
    stores = []
    for leaf in range(leaves):
        here = slice(leaf * rows, (leaf + 1) * rows)
        result[here, :] = total[here, :].astype(result.dtype)
        stores.append(pltpu.make_async_copy(result.at[here], out_ref.at[here], sems.at[leaf]))
        stores[-1].start()
    for store in stores:
        store.wait()


def local(anomalies, leaf_basis, near_blocks, near_ids, transfer_leaf, transfer_mid, far_ids, far_count, mid_couple, top_couple):
    leaves, rank, rows = leaf_basis.shape
    near = near_blocks.shape[1]
    columns = anomalies.shape[1]
    inner_size = lax.axis_size("inner")
    leaf_size = lax.axis_size("leaf")
    bf16 = jnp.bfloat16
    inner = lax.axis_index("inner")
    first, last = 0, inner_size - 1
    groups = range(leaf_size)

    def place(leaf, i):
        return leaf * inner_size + i

    def passed(x, pairs):
        return lax.ppermute(x, ("leaf", "inner"), pairs)

    def swapped(x, reach):
        return lax.ppermute(x, "leaf", [(i, i ^ reach) for i in groups])

    chain = [(i, i + 1) for i in range(leaf_size * inner_size - 1)]
    line = [(place(g, i), place(g, i + 1)) for g in groups for i in range(last)]
    hop = [(place(g, last), place(g + 1, last)) for g in groups[:-1]] + [(place(g, first), place(g - 1, first)) for g in groups[1:]]

    one = leaves * 5 // 8
    rest = leaves - one
    def kernel(body, out_shape, in_specs, out_specs, scratch, aliases=None, flops=1000):
        return call(body, out_shape, in_specs, out_specs, scratch, flops, 1000, 8 * MIB, aliases)

    ahead, back = lax.slice_in_dim(anomalies, rest * rows, leaves * rows), lax.slice_in_dim(anomalies, 0, one * rows)
    x_up, ahead, back = lax.optimization_barrier((anomalies, ahead, back))
    halo = [(passed(ahead, chain), passed(back, [(j, i) for i, j in chain]))]

    maps = (transfer_leaf.reshape(leaves * rank, rank), transfer_mid.reshape(rank, rank))
    operands = (x_up, leaf_basis, *maps)
    piece = jax.ShapeDtypeStruct((rest * rows, columns), bf16)
    part, relay = kernel(
        up_kernel,
        (jax.ShapeDtypeStruct((2 * rank, columns), bf16), piece),
        [ANY] * 4,
        (VMEM, VMEM),
        [pltpu.VMEM(x.shape, bf16) for x in operands] + [pltpu.VMEM((leaves * rank, columns), bf16), pltpu.SemaphoreType.DMA((2 * leaves + 3,))],
    )(*[held(x, pltpu.HBM) for x in operands])
    relayed = passed(relay, hop)
    parts = [part] + [swapped(part, reach) for reach in groups[1:]]
    slots = leaves * near
    parts, x_late, relayed = lax.optimization_barrier((parts, x_up, relayed))
    low, high, plane = kernel(
        pieces_kernel,
        (piece, piece, jax.ShapeDtypeStruct((leaf_size * 2 * rank, columns), bf16)),
        [ANY] * 2 + [VMEM] * leaf_size,
        [VMEM] * 3,
        [pltpu.SemaphoreType.DMA((2,))],
    )(held(x_late, pltpu.HBM), relayed, *parts)
    low, high, plane, x_late = lax.optimization_barrier((low, high, plane, x_late))
    turns = [(place(g, i), place(g, i ^ turn_of(g, inner_size))) for g in groups for i in range(inner_size)]
    planes = passed(plane, [(i, j) for i, j in turns if i != j])
    halo.append(
        (
            passed(low, line + [(place(g, last), place(g, first)) for g in groups[1:]]),
            passed(high, [(j, i) for i, j in line] + [(place(g, first), place(g, last)) for g in groups[:-1]]),
        )
    )
    lists = [pltpu.SMEM((slots + 1,), jnp.int32)] * 2
    wide = resident(leaves * rows, columns, dtype=jnp.float32)
    later = (top_couple[0], mid_couple[0], maps[1], maps[0], leaf_basis)
    total, blocks, *later = kernel(
        own_kernel,
        [wide, resident(slots, rows, rows)] + [resident(*x.shape) for x in later],
        [SMEM] + [ANY] * (2 + len(later)),
        [VMEM] * (2 + len(later)),
        lists * 2 + [pltpu.VMEM(anomalies.shape, bf16), pltpu.SemaphoreType.DMA((slots + 1 + len(later),))],
        flops=1000,
    )(near_ids, *[held(x, pltpu.HBM) for x in (x_late, near_blocks.reshape(slots, rows, rows), *later)])
    blocks = held(blocks, pltpu.VMEM)
    planes, halo[0], total = lax.optimization_barrier((planes, halo[0], total))
    others = [swapped(planes, reach) for reach in range(1, inner_size)]
    total, planes = lax.optimization_barrier((total, planes))
    total = kernel(functools.partial(wave_kernel, one), wide, [SMEM] + [VMEM] * 4, VMEM, lists * 2, aliases={4: 0}, flops=10**10)(
        near_ids, *halo[0], blocks, held(total, pltpu.VMEM)
    )
    others, total = lax.optimization_barrier((others, total))
    total = kernel(
        functools.partial(down_kernel, leaf_size, inner_size),
        wide,
        [SMEM, SMEM] + [VMEM] * (7 + inner_size),
        VMEM,
        [pltpu.VMEM((inner_size * leaf_size * 2 * rank, columns), bf16)],
        aliases={8 + inner_size: 0},
    )(far_ids, far_count, plane, planes, *others, *later, held(total, pltpu.VMEM))
    out, _ = kernel(
        functools.partial(last_kernel, one),
        (jax.ShapeDtypeStruct(anomalies.shape, bf16), wide),
        [SMEM] + [VMEM] * 4,
        (ANY, VMEM),
        lists * 2 + [pltpu.VMEM(anomalies.shape, bf16), pltpu.SemaphoreType.DMA((leaves,))],
        aliases={4: 1},
    )(near_ids, *halo[1], blocks, held(total, pltpu.VMEM))
    return out


def solution(mesh):
    return jax.shard_map(
        local,
        mesh=mesh,
        in_specs=(
            P(("leaf", "inner"), "groups"),
            P(("leaf", "inner"), None, None),
            P(("leaf", "inner"), None, None, None),
            P(("leaf", "inner"), None),
            P(("leaf", "inner"), None, None),
            P(("leaf", "inner"), None, None),
            P(("leaf", "inner"), None),
            P(("leaf", "inner")),
            P(("leaf", "inner"), None, None, None),
            P("leaf", None, None, None),
        ),
        out_specs=P(("leaf", "inner"), "groups"),
        check_vma=False,
    )
```

```python
import functools

import jax
import jax.numpy as jnp
from jax import lax
from jax.experimental import pallas as pl
from jax.experimental.pallas import tpu as pltpu
from jax.sharding import PartitionSpec as P

MIB = 1 << 20
VMEM = pl.BlockSpec(memory_space=pltpu.VMEM)
SMEM = pl.BlockSpec(memory_space=pltpu.SMEM)
ANY = pl.BlockSpec(memory_space=pl.ANY)


def held(x, space):
    return pltpu.with_memory_space_constraint(x, space)


def resident(*shape, dtype=jnp.bfloat16):
    return pltpu.VMEM(shape, dtype)


def turn_of(leaf, inner_size):
    return (3 * leaf + 2) % inner_size


def carrier(turn, inner_size):
    return lax.rem((turn + inner_size - 2 % inner_size) * pow(3, -1, inner_size), inner_size)


def dot(a, b):
    return lax.dot_general(a, b, (((1,), (0,)), ((), ())), preferred_element_type=jnp.float32)


def dot_t(a, b):
    return lax.dot_general(a, b, (((0,), (0,)), ((), ())), preferred_element_type=jnp.float32)


def call(kernel, out_shape, in_specs, out_specs, scratch, flops, moved, vmem, aliases=None):
    return pl.pallas_call(
        kernel,
        out_shape=out_shape,
        in_specs=in_specs,
        out_specs=out_specs,
        scratch_shapes=scratch,
        cost_estimate=pl.CostEstimate(flops=flops, bytes_accessed=moved, transcendentals=0),
        compiler_params=pltpu.CompilerParams(vmem_limit_bytes=vmem),
        input_output_aliases=aliases or {},
    )


def up_kernel(x_ref, basis_ref, leaf_map_ref, mid_map_ref, out_ref, relay, x, basis, leaf_map, mid_map, skeleton, sems):
    leaves, rank, rows = basis.shape
    parts = []
    for leaf in range(leaves):
        here = slice(leaf * rows, (leaf + 1) * rows)
        parts.append(pltpu.make_async_copy(x_ref.at[here], x.at[here], sems.at[leaf]))
        parts.append(pltpu.make_async_copy(basis_ref.at[leaf], basis.at[leaf], sems.at[leaves + leaf]))
    maps = [pltpu.make_async_copy(leaf_map_ref, leaf_map, sems.at[2 * leaves]), pltpu.make_async_copy(mid_map_ref, mid_map, sems.at[2 * leaves + 1])]
    edge = jnp.where(lax.axis_index("inner") == 0, x.shape[0] - relay.shape[0], 0)
    handed = pltpu.make_async_copy(x_ref.at[pl.ds(pl.multiple_of(edge, rows), relay.shape[0])], relay, sems.at[2 * leaves + 2])
    for copy in [*parts, *maps, handed]:
        copy.start()
    for leaf in range(leaves):
        parts[2 * leaf].wait()
        parts[2 * leaf + 1].wait()
        skeleton[leaf * rank : (leaf + 1) * rank, :] = dot(basis[leaf], x[leaf * rows : (leaf + 1) * rows, :]).astype(jnp.bfloat16)
    for copy in maps:
        copy.wait()
    mid = dot_t(leaf_map[...], skeleton[...]).astype(jnp.bfloat16)
    out_ref[:rank, :] = mid
    out_ref[rank:, :] = dot_t(mid_map[...], mid).astype(jnp.bfloat16)
    handed.wait()


def join_kernel(*refs):
    parts, plane = refs[:-1], refs[-1]
    height = parts[0].shape[0]
    for i, part in enumerate(parts):
        plane[i * height : (i + 1) * height, :] = part[...]


def pieces_kernel(x_ref, relayed, low, high, sems):
    inner = lax.axis_index("inner")
    size = low.shape[0]
    ends = (inner == lax.axis_size("inner") - 1, inner == 0)
    for i, (piece, at_end, first) in enumerate(zip((low, high), ends, (0, x_ref.shape[0] - size))):

        @pl.when(at_end)
        def _():
            pltpu.make_async_copy(relayed, piece, sems.at[i]).start()

        @pl.when(jnp.logical_not(at_end))
        def _():
            pltpu.make_async_copy(x_ref.at[first : first + size], piece, sems.at[i]).start()

    for i, piece in enumerate((low, high)):
        pltpu.make_async_copy(relayed, piece, sems.at[i]).wait()


def down_kernel(leaf_size, inner_size, far_ids, far_count, plane, *refs):
    found, (couple, mid_couple, mid_map, leaf_map, basis, _, out_ref, planes) = refs[:inner_size], refs[inner_size:]
    rank = mid_map.shape[0]
    size = 2 * rank
    for step, part in enumerate(found):
        planes[step * leaf_size * size : (step + 1) * leaf_size * size, :] = part[...]
    group = lax.axis_index("leaf")
    inner = lax.axis_index("inner")

    def at_of(step, distance, offset=0):
        return pl.ds(pl.multiple_of((step * leaf_size + distance) * size + offset, rank), rank)

    top_down = jnp.zeros((rank, plane.shape[1]), jnp.float32)
    for distance in range(1, leaf_size):
        other = group ^ distance
        top = plane[at_of(0, distance, rank), :].astype(jnp.float32)
        for step in range(inner_size):
            top += planes[at_of(step, step ^ distance, rank), :].astype(jnp.float32)
        term = dot(couple[other], top.astype(jnp.bfloat16))
        top_down += jnp.where(jnp.abs(other - group) >= 2, term, 0.0)
    total = dot(mid_map[...], top_down.astype(jnp.bfloat16))
    for slot in range(mid_couple.shape[0]):
        live = slot < far_count[0]
        partner = jnp.where(live, far_ids[0, slot], group * inner_size)
        other, turn = partner // inner_size, inner ^ lax.rem(partner, inner_size)
        step = (group & (inner_size - 1)) ^ carrier(turn, inner_size)
        near, far = plane[at_of(0, group ^ other), :], planes[at_of(step, group ^ step ^ other), :]
        term = dot(mid_couple[slot], jnp.where(turn == 0, near, far))
        total += jnp.where(live, term, 0.0)
    leaf_down = dot(leaf_map[...], total.astype(jnp.bfloat16)).astype(jnp.bfloat16)
    leaves, _, rows = basis.shape
    for leaf in range(leaves):
        out_ref[leaf * rows : (leaf + 1) * rows, :] += dot_t(basis[leaf], leaf_down[leaf * rank : (leaf + 1) * rank, :])


def listed(ids_ref, lists, kind_of):
    leaves, near = ids_ref.shape
    first = (lax.axis_index("leaf") * lax.axis_size("inner") + lax.axis_index("inner")) * leaves

    def one(leaf, counts):
        for k in range(near):
            offset = ids_ref[leaf, k] - first
            grown = []
            for (slots, places), count, (member, place) in zip(lists, counts, kind_of(leaf, offset)):
                slots[count] = leaf * near + k
                places[count] = place
                grown.append(count + member.astype(jnp.int32))
            counts = tuple(grown)
        return counts

    return lax.fori_loop(0, leaves, one, (jnp.int32(0),) * len(lists))


def add_products(near, kind, count, blocks, x_ref, total, arrived=lambda slot: None):
    slots, places = kind
    rows = blocks.shape[1]
    half = rows // 2

    def product(i):
        slot = slots[i]
        arrived(slot)
        at = pl.ds(pl.multiple_of(places[i] * rows, rows), rows)
        here = slot // near * rows
        partner = x_ref[at, :]
        return here, [dot(blocks[slot, :half, :], partner), dot(blocks[slot, half:, :], partner)]

    def add(start, terms):
        for i, term in enumerate(terms):
            total[pl.ds(pl.multiple_of(start + i * half, half), half), :] += term

    def pair(j, carry):
        one, first = product(2 * j)
        two, second = product(2 * j + 1)
        add(one, first)
        add(two, second)
        return carry

    lax.fori_loop(0, count // 2, pair, 0)

    @pl.when(lax.rem(count, 2) == 1)
    def _():
        add(*product(count - 1))


def own_kernel(ids_ref, x_hbm, blocks_ref, *refs):
    count = (len(refs) - 8) // 2
    sources, total, blocks, targets = refs[:count], refs[count], refs[count + 1], refs[count + 2 : 2 * count + 2]
    own_slots, own_places, other_slots, other_places, x_ref, sems = refs[2 * count + 2 :]
    leaves, near = ids_ref.shape
    slots = leaves * near
    load = pltpu.make_async_copy(x_hbm, x_ref, sems.at[slots])
    load.start()

    def kind_of(leaf, offset):
        own = (offset >= 0) & (offset < leaves)
        return (own, offset), (jnp.logical_not(own), 0)

    kinds = ((own_slots, own_places), (other_slots, other_places))
    own_count, other_count = listed(ids_ref, kinds, kind_of)

    def copy(slot):
        return pltpu.make_async_copy(blocks_ref.at[slot], blocks.at[slot], sems.at[slot])

    def begin(slots):
        def one(i, carry):
            copy(slots[i]).start()
            return carry

        return one

    lax.fori_loop(0, own_count, begin(own_slots), 0)
    lax.fori_loop(0, other_count, begin(other_slots), 0)
    others = [pltpu.make_async_copy(source, target, sems.at[slots + 1 + i]) for i, (source, target) in enumerate(zip(sources, targets))]
    for other in others:
        other.start()
    total[...] = jnp.zeros_like(total)
    load.wait()
    add_products(near, kinds[0], own_count, blocks, x_ref, total, lambda slot: copy(slot).wait())

    def finish(i, carry):
        copy(other_slots[i]).wait()
        return carry

    lax.fori_loop(0, other_count, finish, 0)
    for other in others:
        other.wait()


def wave_kernel(near_by, ids_ref, before, after, blocks, _, total, *lists):
    leaves, near = ids_ref.shape

    def kind_of(leaf, offset):
        return ((offset < 0) & (offset >= -near_by), offset + near_by), ((offset >= leaves) & (offset < leaves + near_by), offset - leaves)

    kinds = (lists[:2], lists[2:])
    counts = listed(ids_ref, kinds, kind_of)
    for kind, count, x_ref in zip(kinds, counts, (before, after)):
        add_products(near, kind, count, blocks, x_ref, total)


def last_kernel(near_by, ids_ref, before, after, blocks, _, out_ref, total, *refs):
    lists, (result, sems) = refs[:4], refs[4:]
    leaves, near = ids_ref.shape
    rows = blocks.shape[1]

    def kind_of(leaf, offset):
        return (offset < -near_by, offset + leaves), (offset >= leaves + near_by, offset - leaves - near_by)

    kinds = (lists[:2], lists[2:])
    counts = listed(ids_ref, kinds, kind_of)
    for kind, count, x_ref in zip(kinds, counts, (before, after)):
        add_products(near, kind, count, blocks, x_ref, total)
    stores = []
    for leaf in range(leaves):
        here = slice(leaf * rows, (leaf + 1) * rows)
        result[here, :] = total[here, :].astype(result.dtype)
        stores.append(pltpu.make_async_copy(result.at[here], out_ref.at[here], sems.at[leaf]))
        stores[-1].start()
    for store in stores:
        store.wait()


def local(anomalies, leaf_basis, near_blocks, near_ids, transfer_leaf, transfer_mid, far_ids, far_count, mid_couple, top_couple):
    leaves, rank, rows = leaf_basis.shape
    near = near_blocks.shape[1]
    columns = anomalies.shape[1]
    inner_size = lax.axis_size("inner")
    leaf_size = lax.axis_size("leaf")
    bf16 = jnp.bfloat16
    inner = lax.axis_index("inner")
    first, last = 0, inner_size - 1
    groups = range(leaf_size)

    def place(leaf, i):
        return leaf * inner_size + i

    def passed(x, pairs):
        return lax.ppermute(x, ("leaf", "inner"), pairs)

    def swapped(x, reach):
        return lax.ppermute(x, "leaf", [(i, i ^ reach) for i in groups])

    chain = [(i, i + 1) for i in range(leaf_size * inner_size - 1)]
    line = [(place(g, i), place(g, i + 1)) for g in groups for i in range(last)]
    hop = [(place(g, last), place(g + 1, last)) for g in groups[:-1]] + [(place(g, first), place(g - 1, first)) for g in groups[1:]]

    one = leaves * 5 // 8
    rest = leaves - one
    def kernel(body, out_shape, in_specs, out_specs, scratch, aliases=None, flops=1000):
        return call(body, out_shape, in_specs, out_specs, scratch, flops, 1000, 8 * MIB, aliases)

    ahead, back = lax.slice_in_dim(anomalies, rest * rows, leaves * rows), lax.slice_in_dim(anomalies, 0, one * rows)
    x_up, ahead, back = lax.optimization_barrier((anomalies, ahead, back))
    halo = [(passed(ahead, chain), passed(back, [(j, i) for i, j in chain]))]

    maps = (transfer_leaf.reshape(leaves * rank, rank), transfer_mid.reshape(rank, rank))
    operands = (x_up, leaf_basis, *maps)
    piece = jax.ShapeDtypeStruct((rest * rows, columns), bf16)
    part, relay = kernel(
        up_kernel,
        (jax.ShapeDtypeStruct((2 * rank, columns), bf16), piece),
        [ANY] * 4,
        (VMEM, VMEM),
        [pltpu.VMEM(x.shape, bf16) for x in operands] + [pltpu.VMEM((leaves * rank, columns), bf16), pltpu.SemaphoreType.DMA((2 * leaves + 3,))],
    )(*[held(x, pltpu.HBM) for x in operands])
    parts = [part] + [swapped(part, reach) for reach in groups[1:]]
    relay, parts = lax.optimization_barrier((relay, parts))
    relayed = passed(relay, hop)
    slots = leaves * near
    plane = kernel(join_kernel, jax.ShapeDtypeStruct((leaf_size * 2 * rank, columns), bf16), [VMEM] * leaf_size, VMEM, [])(*parts)
    plane, x_late = lax.optimization_barrier((plane, x_up))
    turns = [(place(g, i), place(g, i ^ turn_of(g, inner_size))) for g in groups for i in range(inner_size)]
    planes = passed(plane, [(i, j) for i, j in turns if i != j])
    low, high = kernel(pieces_kernel, (piece, piece), [ANY] * 2, (VMEM, VMEM), [pltpu.SemaphoreType.DMA((2,))])(held(x_late, pltpu.HBM), relayed)
    low, high, x_late = lax.optimization_barrier((low, high, x_late))
    halo.append(
        (
            passed(low, line + [(place(g, last), place(g, first)) for g in groups[1:]]),
            passed(high, [(j, i) for i, j in line] + [(place(g, first), place(g, last)) for g in groups[:-1]]),
        )
    )
    lists = [pltpu.SMEM((slots + 1,), jnp.int32)] * 2
    wide = resident(leaves * rows, columns, dtype=jnp.float32)
    later = (top_couple[0], mid_couple[0], maps[1], maps[0], leaf_basis)
    total, blocks, *later = kernel(
        own_kernel,
        [wide, resident(slots, rows, rows)] + [resident(*x.shape) for x in later],
        [SMEM] + [ANY] * (2 + len(later)),
        [VMEM] * (2 + len(later)),
        lists * 2 + [pltpu.VMEM(anomalies.shape, bf16), pltpu.SemaphoreType.DMA((slots + 1 + len(later),))],
        flops=1000,
    )(near_ids, *[held(x, pltpu.HBM) for x in (x_late, near_blocks.reshape(slots, rows, rows), *later)])
    blocks = held(blocks, pltpu.VMEM)
    planes, halo[0], total = lax.optimization_barrier((planes, halo[0], total))
    others = [swapped(planes, reach) for reach in range(1, inner_size)]
    total, planes = lax.optimization_barrier((total, planes))
    total = kernel(functools.partial(wave_kernel, one), wide, [SMEM] + [VMEM] * 4, VMEM, lists * 2, aliases={4: 0}, flops=10**10)(
        near_ids, *halo[0], blocks, held(total, pltpu.VMEM)
    )
    others, total = lax.optimization_barrier((others, total))
    total = kernel(
        functools.partial(down_kernel, leaf_size, inner_size),
        wide,
        [SMEM, SMEM] + [VMEM] * (7 + inner_size),
        VMEM,
        [pltpu.VMEM((inner_size * leaf_size * 2 * rank, columns), bf16)],
        aliases={8 + inner_size: 0},
    )(far_ids, far_count, plane, planes, *others, *later, held(total, pltpu.VMEM))
    out, _ = kernel(
        functools.partial(last_kernel, one),
        (jax.ShapeDtypeStruct(anomalies.shape, bf16), wide),
        [SMEM] + [VMEM] * 4,
        (ANY, VMEM),
        lists * 2 + [pltpu.VMEM(anomalies.shape, bf16), pltpu.SemaphoreType.DMA((leaves,))],
        aliases={4: 1},
    )(near_ids, *halo[1], blocks, held(total, pltpu.VMEM))
    return out


def solution(mesh):
    return jax.shard_map(
        local,
        mesh=mesh,
        in_specs=(
            P(("leaf", "inner"), "groups"),
            P(("leaf", "inner"), None, None),
            P(("leaf", "inner"), None, None, None),
            P(("leaf", "inner"), None),
            P(("leaf", "inner"), None, None),
            P(("leaf", "inner"), None, None),
            P(("leaf", "inner"), None),
            P(("leaf", "inner")),
            P(("leaf", "inner"), None, None, None),
            P("leaf", None, None, None),
        ),
        out_specs=P(("leaf", "inner"), "groups"),
        check_vma=False,
    )
```

```python
import functools

import jax
import jax.numpy as jnp
from jax import lax
from jax.experimental import pallas as pl
from jax.experimental.pallas import tpu as pltpu
from jax.sharding import PartitionSpec as P

MIB = 1 << 20
VMEM = pl.BlockSpec(memory_space=pltpu.VMEM)
SMEM = pl.BlockSpec(memory_space=pltpu.SMEM)
ANY = pl.BlockSpec(memory_space=pl.ANY)


def held(x, space):
    return pltpu.with_memory_space_constraint(x, space)


def resident(*shape, dtype=jnp.bfloat16):
    return pltpu.VMEM(shape, dtype)


def turn_of(leaf, inner_size):
    return (3 * leaf + 2) % inner_size


def carrier(turn, inner_size):
    return lax.rem((turn + inner_size - 2 % inner_size) * pow(3, -1, inner_size), inner_size)


def dot(a, b):
    return lax.dot_general(a, b, (((1,), (0,)), ((), ())), preferred_element_type=jnp.float32)


def dot_t(a, b):
    return lax.dot_general(a, b, (((0,), (0,)), ((), ())), preferred_element_type=jnp.float32)


def call(kernel, out_shape, in_specs, out_specs, scratch, flops, moved, vmem, aliases=None):
    return pl.pallas_call(
        kernel,
        out_shape=out_shape,
        in_specs=in_specs,
        out_specs=out_specs,
        scratch_shapes=scratch,
        cost_estimate=pl.CostEstimate(flops=flops, bytes_accessed=moved, transcendentals=0),
        compiler_params=pltpu.CompilerParams(vmem_limit_bytes=vmem),
        input_output_aliases=aliases or {},
    )


def up_kernel(x_ref, basis_ref, leaf_map_ref, mid_map_ref, out_ref, relay, x, basis, leaf_map, mid_map, skeleton, sems):
    leaves, rank, rows = basis.shape
    parts = []
    for leaf in range(leaves):
        here = slice(leaf * rows, (leaf + 1) * rows)
        parts.append(pltpu.make_async_copy(x_ref.at[here], x.at[here], sems.at[leaf]))
        parts.append(pltpu.make_async_copy(basis_ref.at[leaf], basis.at[leaf], sems.at[leaves + leaf]))
    maps = [pltpu.make_async_copy(leaf_map_ref, leaf_map, sems.at[2 * leaves]), pltpu.make_async_copy(mid_map_ref, mid_map, sems.at[2 * leaves + 1])]
    edge = jnp.where(lax.axis_index("inner") == 0, x.shape[0] - relay.shape[0], 0)
    handed = pltpu.make_async_copy(x_ref.at[pl.ds(pl.multiple_of(edge, rows), relay.shape[0])], relay, sems.at[2 * leaves + 2])
    for copy in [*parts, *maps, handed]:
        copy.start()
    for leaf in range(leaves):
        parts[2 * leaf].wait()
        parts[2 * leaf + 1].wait()
        skeleton[leaf * rank : (leaf + 1) * rank, :] = dot(basis[leaf], x[leaf * rows : (leaf + 1) * rows, :]).astype(jnp.bfloat16)
    for copy in maps:
        copy.wait()
    mid = dot_t(leaf_map[...], skeleton[...]).astype(jnp.bfloat16)
    out_ref[:rank, :] = mid
    out_ref[rank:, :] = dot_t(mid_map[...], mid).astype(jnp.bfloat16)
    handed.wait()


def join_kernel(*refs):
    parts, plane = refs[:-1], refs[-1]
    height = parts[0].shape[0]
    for i, part in enumerate(parts):
        plane[i * height : (i + 1) * height, :] = part[...]


def pieces_kernel(x_ref, relayed, low, high, sems):
    inner = lax.axis_index("inner")
    size = low.shape[0]
    ends = (inner == lax.axis_size("inner") - 1, inner == 0)
    for i, (piece, at_end, first) in enumerate(zip((low, high), ends, (0, x_ref.shape[0] - size))):

        @pl.when(at_end)
        def _():
            pltpu.make_async_copy(relayed, piece, sems.at[i]).start()

        @pl.when(jnp.logical_not(at_end))
        def _():
            pltpu.make_async_copy(x_ref.at[first : first + size], piece, sems.at[i]).start()

    for i, piece in enumerate((low, high)):
        pltpu.make_async_copy(relayed, piece, sems.at[i]).wait()


def close_kernel(near_by, leaf_size, inner_size, ids_ref, far_ids, far_count, before, after, blocks, plane, *refs):
    found, refs = refs[:inner_size], refs[inner_size:]
    couple, mid_couple, mid_map, leaf_map, basis, _, out_ref, total_ref, planes, *lists, result, sems = refs
    leaves, near = ids_ref.shape

    def kind_of(leaf, offset):
        return (offset < -near_by, offset + leaves), (offset >= leaves + near_by, offset - leaves - near_by)

    kinds = (lists[:2], lists[2:])
    counts = listed(ids_ref, kinds, kind_of)
    for kind, count, x_ref in zip(kinds, counts, (before, after)):
        add_products(near, kind, count, blocks, x_ref, total_ref)
    rank = mid_map.shape[0]
    size = 2 * rank
    for step, part in enumerate(found):
        planes[step * leaf_size * size : (step + 1) * leaf_size * size, :] = part[...]
    group = lax.axis_index("leaf")
    inner = lax.axis_index("inner")

    def at_of(step, distance, offset=0):
        return pl.ds(pl.multiple_of((step * leaf_size + distance) * size + offset, rank), rank)

    top_down = jnp.zeros((rank, plane.shape[1]), jnp.float32)
    for distance in range(1, leaf_size):
        other = group ^ distance
        top = plane[at_of(0, distance, rank), :].astype(jnp.float32)
        for step in range(inner_size):
            top += planes[at_of(step, step ^ distance, rank), :].astype(jnp.float32)
        term = dot(couple[other], top.astype(jnp.bfloat16))
        top_down += jnp.where(jnp.abs(other - group) >= 2, term, 0.0)
    total = dot(mid_map[...], top_down.astype(jnp.bfloat16))
    for slot in range(mid_couple.shape[0]):
        live = slot < far_count[0]
        partner = jnp.where(live, far_ids[0, slot], group * inner_size)
        other, turn = partner // inner_size, inner ^ lax.rem(partner, inner_size)
        step = (group & (inner_size - 1)) ^ carrier(turn, inner_size)
        here, there = plane[at_of(0, group ^ other), :], planes[at_of(step, group ^ step ^ other), :]
        term = dot(mid_couple[slot], jnp.where(turn == 0, here, there))
        total += jnp.where(live, term, 0.0)
    leaf_down = dot(leaf_map[...], total.astype(jnp.bfloat16)).astype(jnp.bfloat16)
    rows = basis.shape[2]
    stores = []
    for leaf in range(leaves):
        here = slice(leaf * rows, (leaf + 1) * rows)
        far = dot_t(basis[leaf], leaf_down[leaf * rank : (leaf + 1) * rank, :])
        result[here, :] = (total_ref[here, :] + far).astype(result.dtype)
        stores.append(pltpu.make_async_copy(result.at[here], out_ref.at[here], sems.at[leaf]))
        stores[-1].start()
    for store in stores:
        store.wait()


def listed(ids_ref, lists, kind_of):
    leaves, near = ids_ref.shape
    first = (lax.axis_index("leaf") * lax.axis_size("inner") + lax.axis_index("inner")) * leaves

    def one(leaf, counts):
        for k in range(near):
            offset = ids_ref[leaf, k] - first
            grown = []
            for (slots, places), count, (member, place) in zip(lists, counts, kind_of(leaf, offset)):
                slots[count] = leaf * near + k
                places[count] = place
                grown.append(count + member.astype(jnp.int32))
            counts = tuple(grown)
        return counts

    return lax.fori_loop(0, leaves, one, (jnp.int32(0),) * len(lists))


def add_products(near, kind, count, blocks, x_ref, total, arrived=lambda slot: None):
    slots, places = kind
    rows = blocks.shape[1]
    half = rows // 2

    def product(i):
        slot = slots[i]
        arrived(slot)
        at = pl.ds(pl.multiple_of(places[i] * rows, rows), rows)
        here = slot // near * rows
        partner = x_ref[at, :]
        return here, [dot(blocks[slot, :half, :], partner), dot(blocks[slot, half:, :], partner)]

    def add(start, terms):
        for i, term in enumerate(terms):
            total[pl.ds(pl.multiple_of(start + i * half, half), half), :] += term

    def pair(j, carry):
        one, first = product(2 * j)
        two, second = product(2 * j + 1)
        add(one, first)
        add(two, second)
        return carry

    lax.fori_loop(0, count // 2, pair, 0)

    @pl.when(lax.rem(count, 2) == 1)
    def _():
        add(*product(count - 1))


def own_kernel(ids_ref, x_hbm, blocks_ref, *refs):
    count = (len(refs) - 8) // 2
    sources, total, blocks, targets = refs[:count], refs[count], refs[count + 1], refs[count + 2 : 2 * count + 2]
    own_slots, own_places, other_slots, other_places, x_ref, sems = refs[2 * count + 2 :]
    leaves, near = ids_ref.shape
    slots = leaves * near
    load = pltpu.make_async_copy(x_hbm, x_ref, sems.at[slots])
    load.start()

    def kind_of(leaf, offset):
        own = (offset >= 0) & (offset < leaves)
        return (own, offset), (jnp.logical_not(own), 0)

    kinds = ((own_slots, own_places), (other_slots, other_places))
    own_count, other_count = listed(ids_ref, kinds, kind_of)

    def copy(slot):
        return pltpu.make_async_copy(blocks_ref.at[slot], blocks.at[slot], sems.at[slot])

    def begin(slots):
        def one(i, carry):
            copy(slots[i]).start()
            return carry

        return one

    lax.fori_loop(0, own_count, begin(own_slots), 0)
    lax.fori_loop(0, other_count, begin(other_slots), 0)
    others = [pltpu.make_async_copy(source, target, sems.at[slots + 1 + i]) for i, (source, target) in enumerate(zip(sources, targets))]
    for other in others:
        other.start()
    total[...] = jnp.zeros_like(total)
    load.wait()
    add_products(near, kinds[0], own_count, blocks, x_ref, total, lambda slot: copy(slot).wait())

    def finish(i, carry):
        copy(other_slots[i]).wait()
        return carry

    lax.fori_loop(0, other_count, finish, 0)
    for other in others:
        other.wait()


def wave_kernel(near_by, ids_ref, before, after, blocks, _, total, *lists):
    leaves, near = ids_ref.shape

    def kind_of(leaf, offset):
        return ((offset < 0) & (offset >= -near_by), offset + near_by), ((offset >= leaves) & (offset < leaves + near_by), offset - leaves)

    kinds = (lists[:2], lists[2:])
    counts = listed(ids_ref, kinds, kind_of)
    for kind, count, x_ref in zip(kinds, counts, (before, after)):
        add_products(near, kind, count, blocks, x_ref, total)


def local(anomalies, leaf_basis, near_blocks, near_ids, transfer_leaf, transfer_mid, far_ids, far_count, mid_couple, top_couple):
    leaves, rank, rows = leaf_basis.shape
    near = near_blocks.shape[1]
    columns = anomalies.shape[1]
    inner_size = lax.axis_size("inner")
    leaf_size = lax.axis_size("leaf")
    bf16 = jnp.bfloat16
    inner = lax.axis_index("inner")
    first, last = 0, inner_size - 1
    groups = range(leaf_size)

    def place(leaf, i):
        return leaf * inner_size + i

    def passed(x, pairs):
        return lax.ppermute(x, ("leaf", "inner"), pairs)

    def swapped(x, reach):
        return lax.ppermute(x, "leaf", [(i, i ^ reach) for i in groups])

    chain = [(i, i + 1) for i in range(leaf_size * inner_size - 1)]
    line = [(place(g, i), place(g, i + 1)) for g in groups for i in range(last)]
    hop = [(place(g, last), place(g + 1, last)) for g in groups[:-1]] + [(place(g, first), place(g - 1, first)) for g in groups[1:]]

    one = leaves * 5 // 8
    rest = leaves - one
    def kernel(body, out_shape, in_specs, out_specs, scratch, aliases=None, flops=1000):
        return call(body, out_shape, in_specs, out_specs, scratch, flops, 1000, 8 * MIB, aliases)

    ahead, back = lax.slice_in_dim(anomalies, rest * rows, leaves * rows), lax.slice_in_dim(anomalies, 0, one * rows)
    x_up, ahead, back = lax.optimization_barrier((anomalies, ahead, back))
    halo = [(passed(ahead, chain), passed(back, [(j, i) for i, j in chain]))]

    maps = (transfer_leaf.reshape(leaves * rank, rank), transfer_mid.reshape(rank, rank))
    operands = (x_up, leaf_basis, *maps)
    piece = jax.ShapeDtypeStruct((rest * rows, columns), bf16)
    part, relay = kernel(
        up_kernel,
        (jax.ShapeDtypeStruct((2 * rank, columns), bf16), piece),
        [ANY] * 4,
        (VMEM, VMEM),
        [pltpu.VMEM(x.shape, bf16) for x in operands] + [pltpu.VMEM((leaves * rank, columns), bf16), pltpu.SemaphoreType.DMA((2 * leaves + 3,))],
    )(*[held(x, pltpu.HBM) for x in operands])
    parts = [part] + [swapped(part, reach) for reach in groups[1:]]
    relay, parts = lax.optimization_barrier((relay, parts))
    relayed = passed(relay, hop)
    slots = leaves * near
    plane = kernel(join_kernel, jax.ShapeDtypeStruct((leaf_size * 2 * rank, columns), bf16), [VMEM] * leaf_size, VMEM, [])(*parts)
    plane, x_late = lax.optimization_barrier((plane, x_up))
    turns = [(place(g, i), place(g, i ^ turn_of(g, inner_size))) for g in groups for i in range(inner_size)]
    planes = passed(plane, [(i, j) for i, j in turns if i != j])
    low, high = kernel(pieces_kernel, (piece, piece), [ANY] * 2, (VMEM, VMEM), [pltpu.SemaphoreType.DMA((2,))])(held(x_late, pltpu.HBM), relayed)
    low, high, x_late = lax.optimization_barrier((low, high, x_late))
    halo.append(
        (
            passed(low, line + [(place(g, last), place(g, first)) for g in groups[1:]]),
            passed(high, [(j, i) for i, j in line] + [(place(g, first), place(g, last)) for g in groups[:-1]]),
        )
    )
    lists = [pltpu.SMEM((slots + 1,), jnp.int32)] * 2
    wide = resident(leaves * rows, columns, dtype=jnp.float32)
    later = (top_couple[0], mid_couple[0], maps[1], maps[0], leaf_basis)
    total, blocks, *later = kernel(
        own_kernel,
        [wide, resident(slots, rows, rows)] + [resident(*x.shape) for x in later],
        [SMEM] + [ANY] * (2 + len(later)),
        [VMEM] * (2 + len(later)),
        lists * 2 + [pltpu.VMEM(anomalies.shape, bf16), pltpu.SemaphoreType.DMA((slots + 1 + len(later),))],
        flops=1000,
    )(near_ids, *[held(x, pltpu.HBM) for x in (x_late, near_blocks.reshape(slots, rows, rows), *later)])
    blocks = held(blocks, pltpu.VMEM)
    halo[0], total = lax.optimization_barrier((halo[0], total))
    total = kernel(functools.partial(wave_kernel, one), wide, [SMEM] + [VMEM] * 4, VMEM, lists * 2, aliases={4: 0}, flops=10**10)(
        near_ids, *halo[0], blocks, held(total, pltpu.VMEM)
    )
    planes, total = lax.optimization_barrier((planes, total))
    found = [planes] + [swapped(planes, reach) for reach in range(1, inner_size)]
    out, _ = kernel(
        functools.partial(close_kernel, one, leaf_size, inner_size),
        (jax.ShapeDtypeStruct(anomalies.shape, bf16), wide),
        [SMEM] * 3 + [VMEM] * (10 + inner_size),
        (ANY, VMEM),
        [
            pltpu.VMEM((inner_size * leaf_size * 2 * rank, columns), bf16),
            *lists * 2,
            pltpu.VMEM(anomalies.shape, bf16),
            pltpu.SemaphoreType.DMA((leaves,)),
        ],
        aliases={12 + inner_size: 1},
    )(near_ids, far_ids, far_count, *halo[1], blocks, plane, *found, *later, held(total, pltpu.VMEM))
    return out


def solution(mesh):
    return jax.shard_map(
        local,
        mesh=mesh,
        in_specs=(
            P(("leaf", "inner"), "groups"),
            P(("leaf", "inner"), None, None),
            P(("leaf", "inner"), None, None, None),
            P(("leaf", "inner"), None),
            P(("leaf", "inner"), None, None),
            P(("leaf", "inner"), None, None),
            P(("leaf", "inner"), None),
            P(("leaf", "inner")),
            P(("leaf", "inner"), None, None, None),
            P("leaf", None, None, None),
        ),
        out_specs=P(("leaf", "inner"), "groups"),
        check_vma=False,
    )
```

```python
import functools

import jax
import jax.numpy as jnp
from jax import lax
from jax.experimental import pallas as pl
from jax.experimental.pallas import tpu as pltpu
from jax.sharding import PartitionSpec as P

MIB = 1 << 20
VMEM = pl.BlockSpec(memory_space=pltpu.VMEM)
SMEM = pl.BlockSpec(memory_space=pltpu.SMEM)
ANY = pl.BlockSpec(memory_space=pl.ANY)


def held(x, space):
    return pltpu.with_memory_space_constraint(x, space)


def resident(*shape, dtype=jnp.bfloat16):
    return pltpu.VMEM(shape, dtype)


def turn_of(leaf, inner_size):
    return (3 * leaf + 2) % inner_size


def carrier(turn, inner_size):
    return lax.rem((turn + inner_size - 2 % inner_size) * pow(3, -1, inner_size), inner_size)


def dot(a, b):
    return lax.dot_general(a, b, (((1,), (0,)), ((), ())), preferred_element_type=jnp.float32)


def dot_t(a, b):
    return lax.dot_general(a, b, (((0,), (0,)), ((), ())), preferred_element_type=jnp.float32)


def call(kernel, out_shape, in_specs, out_specs, scratch, flops, moved, vmem, aliases=None):
    return pl.pallas_call(
        kernel,
        out_shape=out_shape,
        in_specs=in_specs,
        out_specs=out_specs,
        scratch_shapes=scratch,
        cost_estimate=pl.CostEstimate(flops=flops, bytes_accessed=moved, transcendentals=0),
        compiler_params=pltpu.CompilerParams(vmem_limit_bytes=vmem),
        input_output_aliases=aliases or {},
    )


def up_kernel(x_ref, basis_ref, leaf_map_ref, mid_map_ref, out_ref, x, basis, leaf_map, mid_map, skeleton, sems):
    leaves, rank, rows = basis.shape
    parts = []
    for leaf in range(leaves):
        here = slice(leaf * rows, (leaf + 1) * rows)
        parts.append(pltpu.make_async_copy(x_ref.at[here], x.at[here], sems.at[leaf]))
        parts.append(pltpu.make_async_copy(basis_ref.at[leaf], basis.at[leaf], sems.at[leaves + leaf]))
    maps = [pltpu.make_async_copy(leaf_map_ref, leaf_map, sems.at[2 * leaves]), pltpu.make_async_copy(mid_map_ref, mid_map, sems.at[2 * leaves + 1])]
    for copy in parts + maps:
        copy.start()
    for leaf in range(leaves):
        parts[2 * leaf].wait()
        parts[2 * leaf + 1].wait()
        skeleton[leaf * rank : (leaf + 1) * rank, :] = dot(basis[leaf], x[leaf * rows : (leaf + 1) * rows, :]).astype(jnp.bfloat16)
    for copy in maps:
        copy.wait()
    mid = dot_t(leaf_map[...], skeleton[...]).astype(jnp.bfloat16)
    out_ref[:rank, :] = mid
    out_ref[rank:, :] = dot_t(mid_map[...], mid).astype(jnp.bfloat16)


def pieces_kernel(x_ref, relayed, *refs):
    parts, (low, high, plane, sems) = refs[:-4], refs[-4:]
    inner = lax.axis_index("inner")
    size = low.shape[0]
    ends = (inner == lax.axis_size("inner") - 1, inner == 0)
    for i, (piece, at_end, first) in enumerate(zip((low, high), ends, (0, x_ref.shape[0] - size))):

        @pl.when(at_end)
        def _():
            pltpu.make_async_copy(relayed, piece, sems.at[i]).start()

        @pl.when(jnp.logical_not(at_end))
        def _():
            pltpu.make_async_copy(x_ref.at[first : first + size], piece, sems.at[i]).start()

    height = parts[0].shape[0]
    for i, part in enumerate(parts):
        plane[i * height : (i + 1) * height, :] = part[...]
    for i, piece in enumerate((low, high)):
        pltpu.make_async_copy(relayed, piece, sems.at[i]).wait()


def close_kernel(near_by, leaf_size, inner_size, ids_ref, far_ids, far_count, before, after, blocks, plane, *refs):
    found, refs = refs[:inner_size], refs[inner_size:]
    couple, mid_couple, mid_map, leaf_map, basis, _, out_ref, total_ref, planes, *lists, result, sems = refs
    leaves, near = ids_ref.shape

    def kind_of(leaf, offset):
        return (offset < -near_by, offset + leaves), (offset >= leaves + near_by, offset - leaves - near_by)

    kinds = (lists[:2], lists[2:])
    counts = listed(ids_ref, kinds, kind_of)
    for kind, count, x_ref in zip(kinds, counts, (before, after)):
        add_products(near, kind, count, blocks, x_ref, total_ref)
    rank = mid_map.shape[0]
    size = 2 * rank
    for step, part in enumerate(found):
        planes[step * leaf_size * size : (step + 1) * leaf_size * size, :] = part[...]
    group = lax.axis_index("leaf")
    inner = lax.axis_index("inner")

    def at_of(step, distance, offset=0):
        return pl.ds(pl.multiple_of((step * leaf_size + distance) * size + offset, rank), rank)

    top_down = jnp.zeros((rank, plane.shape[1]), jnp.float32)
    for distance in range(1, leaf_size):
        other = group ^ distance
        top = plane[at_of(0, distance, rank), :].astype(jnp.float32)
        for step in range(inner_size):
            top += planes[at_of(step, step ^ distance, rank), :].astype(jnp.float32)
        term = dot(couple[other], top.astype(jnp.bfloat16))
        top_down += jnp.where(jnp.abs(other - group) >= 2, term, 0.0)
    total = dot(mid_map[...], top_down.astype(jnp.bfloat16))
    for slot in range(mid_couple.shape[0]):
        live = slot < far_count[0]
        partner = jnp.where(live, far_ids[0, slot], group * inner_size)
        other, turn = partner // inner_size, inner ^ lax.rem(partner, inner_size)
        step = (group & (inner_size - 1)) ^ carrier(turn, inner_size)
        here, there = plane[at_of(0, group ^ other), :], planes[at_of(step, group ^ step ^ other), :]
        term = dot(mid_couple[slot], jnp.where(turn == 0, here, there))
        total += jnp.where(live, term, 0.0)
    leaf_down = dot(leaf_map[...], total.astype(jnp.bfloat16)).astype(jnp.bfloat16)
    rows = basis.shape[2]
    stores = []
    for leaf in range(leaves):
        here = slice(leaf * rows, (leaf + 1) * rows)
        far = dot_t(basis[leaf], leaf_down[leaf * rank : (leaf + 1) * rank, :])
        result[here, :] = (total_ref[here, :] + far).astype(result.dtype)
        stores.append(pltpu.make_async_copy(result.at[here], out_ref.at[here], sems.at[leaf]))
        stores[-1].start()
    for store in stores:
        store.wait()


def listed(ids_ref, lists, kind_of):
    leaves, near = ids_ref.shape
    first = (lax.axis_index("leaf") * lax.axis_size("inner") + lax.axis_index("inner")) * leaves

    def one(leaf, counts):
        for k in range(near):
            offset = ids_ref[leaf, k] - first
            grown = []
            for (slots, places), count, (member, place) in zip(lists, counts, kind_of(leaf, offset)):
                slots[count] = leaf * near + k
                places[count] = place
                grown.append(count + member.astype(jnp.int32))
            counts = tuple(grown)
        return counts

    return lax.fori_loop(0, leaves, one, (jnp.int32(0),) * len(lists))


def add_products(near, kind, count, blocks, x_ref, total, arrived=lambda slot: None):
    slots, places = kind
    rows = blocks.shape[1]
    half = rows // 2

    def product(i):
        slot = slots[i]
        arrived(slot)
        at = pl.ds(pl.multiple_of(places[i] * rows, rows), rows)
        here = slot // near * rows
        partner = x_ref[at, :]
        return here, [dot(blocks[slot, :half, :], partner), dot(blocks[slot, half:, :], partner)]

    def add(start, terms):
        for i, term in enumerate(terms):
            total[pl.ds(pl.multiple_of(start + i * half, half), half), :] += term

    def pair(j, carry):
        one, first = product(2 * j)
        two, second = product(2 * j + 1)
        add(one, first)
        add(two, second)
        return carry

    lax.fori_loop(0, count // 2, pair, 0)

    @pl.when(lax.rem(count, 2) == 1)
    def _():
        add(*product(count - 1))


def own_kernel(ids_ref, x_hbm, blocks_ref, *refs):
    count = (len(refs) - 8) // 2
    sources, total, blocks, targets = refs[:count], refs[count], refs[count + 1], refs[count + 2 : 2 * count + 2]
    own_slots, own_places, other_slots, other_places, x_ref, sems = refs[2 * count + 2 :]
    leaves, near = ids_ref.shape
    slots = leaves * near
    load = pltpu.make_async_copy(x_hbm, x_ref, sems.at[slots])
    load.start()

    def kind_of(leaf, offset):
        own = (offset >= 0) & (offset < leaves)
        return (own, offset), (jnp.logical_not(own), 0)

    kinds = ((own_slots, own_places), (other_slots, other_places))
    own_count, other_count = listed(ids_ref, kinds, kind_of)

    def copy(slot):
        return pltpu.make_async_copy(blocks_ref.at[slot], blocks.at[slot], sems.at[slot])

    def begin(slots):
        def one(i, carry):
            copy(slots[i]).start()
            return carry

        return one

    lax.fori_loop(0, own_count, begin(own_slots), 0)
    lax.fori_loop(0, other_count, begin(other_slots), 0)
    others = [pltpu.make_async_copy(source, target, sems.at[slots + 1 + i]) for i, (source, target) in enumerate(zip(sources, targets))]
    for other in others:
        other.start()
    total[...] = jnp.zeros_like(total)
    load.wait()
    add_products(near, kinds[0], own_count, blocks, x_ref, total, lambda slot: copy(slot).wait())

    def finish(i, carry):
        copy(other_slots[i]).wait()
        return carry

    lax.fori_loop(0, other_count, finish, 0)
    for other in others:
        other.wait()


def wave_kernel(near_by, ids_ref, before, after, blocks, _, total, *lists):
    leaves, near = ids_ref.shape

    def kind_of(leaf, offset):
        return ((offset < 0) & (offset >= -near_by), offset + near_by), ((offset >= leaves) & (offset < leaves + near_by), offset - leaves)

    kinds = (lists[:2], lists[2:])
    counts = listed(ids_ref, kinds, kind_of)
    for kind, count, x_ref in zip(kinds, counts, (before, after)):
        add_products(near, kind, count, blocks, x_ref, total)


def local(anomalies, leaf_basis, near_blocks, near_ids, transfer_leaf, transfer_mid, far_ids, far_count, mid_couple, top_couple):
    leaves, rank, rows = leaf_basis.shape
    near = near_blocks.shape[1]
    columns = anomalies.shape[1]
    inner_size = lax.axis_size("inner")
    leaf_size = lax.axis_size("leaf")
    bf16 = jnp.bfloat16
    inner = lax.axis_index("inner")
    first, last = 0, inner_size - 1
    groups = range(leaf_size)

    def place(leaf, i):
        return leaf * inner_size + i

    def passed(x, pairs):
        return lax.ppermute(x, ("leaf", "inner"), pairs)

    def swapped(x, reach):
        return lax.ppermute(x, "leaf", [(i, i ^ reach) for i in groups])

    chain = [(i, i + 1) for i in range(leaf_size * inner_size - 1)]
    line = [(place(g, i), place(g, i + 1)) for g in groups for i in range(last)]
    hop = [(place(g, last), place(g + 1, last)) for g in groups[:-1]] + [(place(g, first), place(g - 1, first)) for g in groups[1:]]

    one = leaves // 2
    rest = leaves - one
    def kernel(body, out_shape, in_specs, out_specs, scratch, aliases=None, flops=1000):
        return call(body, out_shape, in_specs, out_specs, scratch, flops, 1000, 8 * MIB, aliases)

    ahead, back = lax.slice_in_dim(anomalies, rest * rows, leaves * rows), lax.slice_in_dim(anomalies, 0, one * rows)
    relay = jnp.where(inner == first, lax.slice_in_dim(anomalies, one * rows, leaves * rows), lax.slice_in_dim(anomalies, 0, rest * rows))
    x_up, ahead, back, relay = lax.optimization_barrier((anomalies, ahead, back, relay))
    relayed = passed(relay, hop)
    halo = [(passed(ahead, chain), passed(back, [(j, i) for i, j in chain]))]

    maps = (transfer_leaf.reshape(leaves * rank, rank), transfer_mid.reshape(rank, rank))
    operands = (x_up, leaf_basis, *maps)
    piece = jax.ShapeDtypeStruct((rest * rows, columns), bf16)
    part = kernel(
        up_kernel,
        jax.ShapeDtypeStruct((2 * rank, columns), bf16),
        [ANY] * 4,
        VMEM,
        [pltpu.VMEM(x.shape, bf16) for x in operands] + [pltpu.VMEM((leaves * rank, columns), bf16), pltpu.SemaphoreType.DMA((2 * leaves + 2,))],
    )(*[held(x, pltpu.HBM) for x in operands])
    parts = [part] + [swapped(part, reach) for reach in groups[1:]]
    slots = leaves * near
    parts, x_late, relayed = lax.optimization_barrier((parts, x_up, relayed))
    low, high, plane = kernel(
        pieces_kernel,
        (piece, piece, jax.ShapeDtypeStruct((leaf_size * 2 * rank, columns), bf16)),
        [ANY] * 2 + [VMEM] * leaf_size,
        [VMEM] * 3,
        [pltpu.SemaphoreType.DMA((2,))],
    )(held(x_late, pltpu.HBM), relayed, *parts)
    low, high, plane, x_late = lax.optimization_barrier((low, high, plane, x_late))
    turns = [(place(g, i), place(g, i ^ turn_of(g, inner_size))) for g in groups for i in range(inner_size)]
    planes = passed(plane, [(i, j) for i, j in turns if i != j])
    halo.append(
        (
            passed(low, line + [(place(g, last), place(g, first)) for g in groups[1:]]),
            passed(high, [(j, i) for i, j in line] + [(place(g, first), place(g, last)) for g in groups[:-1]]),
        )
    )
    lists = [pltpu.SMEM((slots + 1,), jnp.int32)] * 2
    wide = resident(leaves * rows, columns, dtype=jnp.float32)
    later = (top_couple[0], mid_couple[0], maps[1], maps[0], leaf_basis)
    total, blocks, *later = kernel(
        own_kernel,
        [wide, resident(slots, rows, rows)] + [resident(*x.shape) for x in later],
        [SMEM] + [ANY] * (2 + len(later)),
        [VMEM] * (2 + len(later)),
        lists * 2 + [pltpu.VMEM(anomalies.shape, bf16), pltpu.SemaphoreType.DMA((slots + 1 + len(later),))],
        flops=1000,
    )(near_ids, *[held(x, pltpu.HBM) for x in (x_late, near_blocks.reshape(slots, rows, rows), *later)])
    blocks = held(blocks, pltpu.VMEM)
    planes, halo[0], total = lax.optimization_barrier((planes, halo[0], total))
    others = [swapped(planes, reach) for reach in range(1, inner_size)]
    total, planes = lax.optimization_barrier((total, planes))
    total = kernel(functools.partial(wave_kernel, one), wide, [SMEM] + [VMEM] * 4, VMEM, lists * 2, aliases={4: 0}, flops=10**10)(
        near_ids, *halo[0], blocks, held(total, pltpu.VMEM)
    )
    others, total = lax.optimization_barrier((others, total))
    out, _ = kernel(
        functools.partial(close_kernel, one, leaf_size, inner_size),
        (jax.ShapeDtypeStruct(anomalies.shape, bf16), wide),
        [SMEM] * 3 + [VMEM] * (10 + inner_size),
        (ANY, VMEM),
        [
            pltpu.VMEM((inner_size * leaf_size * 2 * rank, columns), bf16),
            *lists * 2,
            pltpu.VMEM(anomalies.shape, bf16),
            pltpu.SemaphoreType.DMA((leaves,)),
        ],
        aliases={12 + inner_size: 1},
    )(near_ids, far_ids, far_count, *halo[1], blocks, plane, planes, *others, *later, held(total, pltpu.VMEM))
    return out


def solution(mesh):
    return jax.shard_map(
        local,
        mesh=mesh,
        in_specs=(
            P(("leaf", "inner"), "groups"),
            P(("leaf", "inner"), None, None),
            P(("leaf", "inner"), None, None, None),
            P(("leaf", "inner"), None),
            P(("leaf", "inner"), None, None),
            P(("leaf", "inner"), None, None),
            P(("leaf", "inner"), None),
            P(("leaf", "inner")),
            P(("leaf", "inner"), None, None, None),
            P("leaf", None, None, None),
        ),
        out_specs=P(("leaf", "inner"), "groups"),
        check_vma=False,
    )
```

```python
import functools

import jax
import jax.numpy as jnp
from jax import lax
from jax.experimental import pallas as pl
from jax.experimental.pallas import tpu as pltpu
from jax.sharding import PartitionSpec as P

MIB = 1 << 20
VMEM = pl.BlockSpec(memory_space=pltpu.VMEM)
SMEM = pl.BlockSpec(memory_space=pltpu.SMEM)
ANY = pl.BlockSpec(memory_space=pl.ANY)


def held(x, space):
    return pltpu.with_memory_space_constraint(x, space)


def resident(*shape, dtype=jnp.bfloat16):
    return pltpu.VMEM(shape, dtype)


def turn_of(leaf, inner_size):
    return (3 * leaf + 2) % inner_size


def carrier(turn, inner_size):
    return lax.rem((turn + inner_size - 2 % inner_size) * pow(3, -1, inner_size), inner_size)


def dot(a, b):
    return lax.dot_general(a, b, (((1,), (0,)), ((), ())), preferred_element_type=jnp.float32)


def dot_t(a, b):
    return lax.dot_general(a, b, (((0,), (0,)), ((), ())), preferred_element_type=jnp.float32)


def call(kernel, out_shape, in_specs, out_specs, scratch, flops, moved, vmem, aliases=None):
    return pl.pallas_call(
        kernel,
        out_shape=out_shape,
        in_specs=in_specs,
        out_specs=out_specs,
        scratch_shapes=scratch,
        cost_estimate=pl.CostEstimate(flops=flops, bytes_accessed=moved, transcendentals=0),
        compiler_params=pltpu.CompilerParams(vmem_limit_bytes=vmem),
        input_output_aliases=aliases or {},
    )


def up_kernel(x_ref, basis_ref, leaf_map_ref, mid_map_ref, out_ref, x, basis, leaf_map, mid_map, skeleton, sems):
    leaves, rank, rows = basis.shape
    parts = []
    for leaf in range(leaves):
        here = slice(leaf * rows, (leaf + 1) * rows)
        parts.append(pltpu.make_async_copy(x_ref.at[here], x.at[here], sems.at[leaf]))
        parts.append(pltpu.make_async_copy(basis_ref.at[leaf], basis.at[leaf], sems.at[leaves + leaf]))
    maps = [pltpu.make_async_copy(leaf_map_ref, leaf_map, sems.at[2 * leaves]), pltpu.make_async_copy(mid_map_ref, mid_map, sems.at[2 * leaves + 1])]
    for copy in parts + maps:
        copy.start()
    for leaf in range(leaves):
        parts[2 * leaf].wait()
        parts[2 * leaf + 1].wait()
        skeleton[leaf * rank : (leaf + 1) * rank, :] = dot(basis[leaf], x[leaf * rows : (leaf + 1) * rows, :]).astype(jnp.bfloat16)
    for copy in maps:
        copy.wait()
    mid = dot_t(leaf_map[...], skeleton[...]).astype(jnp.bfloat16)
    out_ref[:rank, :] = mid
    out_ref[rank:, :] = dot_t(mid_map[...], mid).astype(jnp.bfloat16)


def pieces_kernel(x_ref, relayed, *refs):
    parts, (low, high, plane, sems) = refs[:-4], refs[-4:]
    inner = lax.axis_index("inner")
    size = low.shape[0]
    ends = (inner == lax.axis_size("inner") - 1, inner == 0)
    for i, (piece, at_end, first) in enumerate(zip((low, high), ends, (0, x_ref.shape[0] - size))):

        @pl.when(at_end)
        def _():
            pltpu.make_async_copy(relayed, piece, sems.at[i]).start()

        @pl.when(jnp.logical_not(at_end))
        def _():
            pltpu.make_async_copy(x_ref.at[first : first + size], piece, sems.at[i]).start()

    height = parts[0].shape[0]
    for i, part in enumerate(parts):
        plane[i * height : (i + 1) * height, :] = part[...]
    for i, piece in enumerate((low, high)):
        pltpu.make_async_copy(relayed, piece, sems.at[i]).wait()


def close_kernel(near_by, leaf_size, inner_size, ids_ref, far_ids, far_count, before, after, blocks, plane, *refs):
    found, refs = refs[:inner_size], refs[inner_size:]
    couple, mid_couple, mid_map, leaf_map, basis, _, out_ref, total_ref, planes, *lists, result, sems = refs
    leaves, near = ids_ref.shape

    def kind_of(leaf, offset):
        return (offset < -near_by, offset + leaves), (offset >= leaves + near_by, offset - leaves - near_by)

    kinds = (lists[:2], lists[2:])
    counts = listed(ids_ref, kinds, kind_of)
    for kind, count, x_ref in zip(kinds, counts, (before, after)):
        add_products(near, kind, count, blocks, x_ref, total_ref)
    rank = mid_map.shape[0]
    size = 2 * rank
    for step, part in enumerate(found):
        planes[step * leaf_size * size : (step + 1) * leaf_size * size, :] = part[...]
    group = lax.axis_index("leaf")
    inner = lax.axis_index("inner")

    def at_of(step, distance, offset=0):
        return pl.ds(pl.multiple_of((step * leaf_size + distance) * size + offset, rank), rank)

    top_down = jnp.zeros((rank, plane.shape[1]), jnp.float32)
    for distance in range(1, leaf_size):
        other = group ^ distance
        top = plane[at_of(0, distance, rank), :].astype(jnp.float32)
        for step in range(inner_size):
            top += planes[at_of(step, step ^ distance, rank), :].astype(jnp.float32)
        term = dot(couple[other], top.astype(jnp.bfloat16))
        top_down += jnp.where(jnp.abs(other - group) >= 2, term, 0.0)
    total = dot(mid_map[...], top_down.astype(jnp.bfloat16))
    for slot in range(mid_couple.shape[0]):
        live = slot < far_count[0]
        partner = jnp.where(live, far_ids[0, slot], group * inner_size)
        other, turn = partner // inner_size, inner ^ lax.rem(partner, inner_size)
        step = (group & (inner_size - 1)) ^ carrier(turn, inner_size)
        here, there = plane[at_of(0, group ^ other), :], planes[at_of(step, group ^ step ^ other), :]
        term = dot(mid_couple[slot], jnp.where(turn == 0, here, there))
        total += jnp.where(live, term, 0.0)
    leaf_down = dot(leaf_map[...], total.astype(jnp.bfloat16)).astype(jnp.bfloat16)
    rows = basis.shape[2]
    stores = []
    for leaf in range(leaves):
        here = slice(leaf * rows, (leaf + 1) * rows)
        far = dot_t(basis[leaf], leaf_down[leaf * rank : (leaf + 1) * rank, :])
        result[here, :] = (total_ref[here, :] + far).astype(result.dtype)
        stores.append(pltpu.make_async_copy(result.at[here], out_ref.at[here], sems.at[leaf]))
        stores[-1].start()
    for store in stores:
        store.wait()


def listed(ids_ref, lists, kind_of):
    leaves, near = ids_ref.shape
    first = (lax.axis_index("leaf") * lax.axis_size("inner") + lax.axis_index("inner")) * leaves

    def one(leaf, counts):
        for k in range(near):
            offset = ids_ref[leaf, k] - first
            grown = []
            for (slots, places), count, (member, place) in zip(lists, counts, kind_of(leaf, offset)):
                slots[count] = leaf * near + k
                places[count] = place
                grown.append(count + member.astype(jnp.int32))
            counts = tuple(grown)
        return counts

    return lax.fori_loop(0, leaves, one, (jnp.int32(0),) * len(lists))


def add_products(near, kind, count, blocks, x_ref, total, arrived=lambda slot: None):
    slots, places = kind
    rows = blocks.shape[1]
    half = rows // 2

    def product(i):
        slot = slots[i]
        arrived(slot)
        at = pl.ds(pl.multiple_of(places[i] * rows, rows), rows)
        here = slot // near * rows
        partner = x_ref[at, :]
        return here, [dot(blocks[slot, :half, :], partner), dot(blocks[slot, half:, :], partner)]

    def add(start, terms):
        for i, term in enumerate(terms):
            total[pl.ds(pl.multiple_of(start + i * half, half), half), :] += term

    def pair(j, carry):
        one, first = product(2 * j)
        two, second = product(2 * j + 1)
        add(one, first)
        add(two, second)
        return carry

    lax.fori_loop(0, count // 2, pair, 0)

    @pl.when(lax.rem(count, 2) == 1)
    def _():
        add(*product(count - 1))


def own_kernel(ids_ref, x_hbm, blocks_ref, *refs):
    count = (len(refs) - 8) // 2
    sources, total, blocks, targets = refs[:count], refs[count], refs[count + 1], refs[count + 2 : 2 * count + 2]
    own_slots, own_places, other_slots, other_places, x_ref, sems = refs[2 * count + 2 :]
    leaves, near = ids_ref.shape
    slots = leaves * near
    load = pltpu.make_async_copy(x_hbm, x_ref, sems.at[slots])
    load.start()

    def kind_of(leaf, offset):
        own = (offset >= 0) & (offset < leaves)
        return (own, offset), (jnp.logical_not(own), 0)

    kinds = ((own_slots, own_places), (other_slots, other_places))
    own_count, other_count = listed(ids_ref, kinds, kind_of)

    def copy(slot):
        return pltpu.make_async_copy(blocks_ref.at[slot], blocks.at[slot], sems.at[slot])

    def begin(slots):
        def one(i, carry):
            copy(slots[i]).start()
            return carry

        return one

    lax.fori_loop(0, own_count, begin(own_slots), 0)
    lax.fori_loop(0, other_count, begin(other_slots), 0)
    others = [pltpu.make_async_copy(source, target, sems.at[slots + 1 + i]) for i, (source, target) in enumerate(zip(sources, targets))]
    for other in others:
        other.start()
    total[...] = jnp.zeros_like(total)
    load.wait()
    add_products(near, kinds[0], own_count, blocks, x_ref, total, lambda slot: copy(slot).wait())

    def finish(i, carry):
        copy(other_slots[i]).wait()
        return carry

    lax.fori_loop(0, other_count, finish, 0)
    for other in others:
        other.wait()


def wave_kernel(near_by, ids_ref, before, after, blocks, _, total, *lists):
    leaves, near = ids_ref.shape

    def kind_of(leaf, offset):
        return ((offset < 0) & (offset >= -near_by), offset + near_by), ((offset >= leaves) & (offset < leaves + near_by), offset - leaves)

    kinds = (lists[:2], lists[2:])
    counts = listed(ids_ref, kinds, kind_of)
    for kind, count, x_ref in zip(kinds, counts, (before, after)):
        add_products(near, kind, count, blocks, x_ref, total)


def local(anomalies, leaf_basis, near_blocks, near_ids, transfer_leaf, transfer_mid, far_ids, far_count, mid_couple, top_couple):
    leaves, rank, rows = leaf_basis.shape
    near = near_blocks.shape[1]
    columns = anomalies.shape[1]
    inner_size = lax.axis_size("inner")
    leaf_size = lax.axis_size("leaf")
    bf16 = jnp.bfloat16
    inner = lax.axis_index("inner")
    first, last = 0, inner_size - 1
    groups = range(leaf_size)

    def place(leaf, i):
        return leaf * inner_size + i

    def passed(x, pairs):
        return lax.ppermute(x, ("leaf", "inner"), pairs)

    def swapped(x, reach):
        return lax.ppermute(x, "leaf", [(i, i ^ reach) for i in groups])

    chain = [(i, i + 1) for i in range(leaf_size * inner_size - 1)]
    line = [(place(g, i), place(g, i + 1)) for g in groups for i in range(last)]
    hop = [(place(g, last), place(g + 1, last)) for g in groups[:-1]] + [(place(g, first), place(g - 1, first)) for g in groups[1:]]

    one = leaves * 5 // 8
    rest = leaves - one
    def kernel(body, out_shape, in_specs, out_specs, scratch, aliases=None, flops=1000):
        return call(body, out_shape, in_specs, out_specs, scratch, flops, 1000, 8 * MIB, aliases)

    ahead, back = lax.slice_in_dim(anomalies, rest * rows, leaves * rows), lax.slice_in_dim(anomalies, 0, one * rows)
    relay = jnp.where(inner == first, lax.slice_in_dim(anomalies, one * rows, leaves * rows), lax.slice_in_dim(anomalies, 0, rest * rows))
    x_up, ahead, back = lax.optimization_barrier((anomalies, ahead, back))
    relayed = passed(relay, hop)
    halo = [(passed(ahead, chain), passed(back, [(j, i) for i, j in chain]))]

    maps = (transfer_leaf.reshape(leaves * rank, rank), transfer_mid.reshape(rank, rank))
    operands = (x_up, leaf_basis, *maps)
    piece = jax.ShapeDtypeStruct((rest * rows, columns), bf16)
    part = kernel(
        up_kernel,
        jax.ShapeDtypeStruct((2 * rank, columns), bf16),
        [ANY] * 4,
        VMEM,
        [pltpu.VMEM(x.shape, bf16) for x in operands] + [pltpu.VMEM((leaves * rank, columns), bf16), pltpu.SemaphoreType.DMA((2 * leaves + 2,))],
    )(*[held(x, pltpu.HBM) for x in operands])
    parts = [part] + [swapped(part, reach) for reach in groups[1:]]
    slots = leaves * near
    parts, x_late, relayed = lax.optimization_barrier((parts, x_up, relayed))
    low, high, plane = kernel(
        pieces_kernel,
        (piece, piece, jax.ShapeDtypeStruct((leaf_size * 2 * rank, columns), bf16)),
        [ANY] * 2 + [VMEM] * leaf_size,
        [VMEM] * 3,
        [pltpu.SemaphoreType.DMA((2,))],
    )(held(x_late, pltpu.HBM), relayed, *parts)
    low, high, plane, x_late = lax.optimization_barrier((low, high, plane, x_late))
    turns = [(place(g, i), place(g, i ^ turn_of(g, inner_size))) for g in groups for i in range(inner_size)]
    planes = passed(plane, [(i, j) for i, j in turns if i != j])
    halo.append(
        (
            passed(low, line + [(place(g, last), place(g, first)) for g in groups[1:]]),
            passed(high, [(j, i) for i, j in line] + [(place(g, first), place(g, last)) for g in groups[:-1]]),
        )
    )
    lists = [pltpu.SMEM((slots + 1,), jnp.int32)] * 2
    wide = resident(leaves * rows, columns, dtype=jnp.float32)
    later = (top_couple[0], mid_couple[0], maps[1], maps[0], leaf_basis)
    total, blocks, *later = kernel(
        own_kernel,
        [wide, resident(slots, rows, rows)] + [resident(*x.shape) for x in later],
        [SMEM] + [ANY] * (2 + len(later)),
        [VMEM] * (2 + len(later)),
        lists * 2 + [pltpu.VMEM(anomalies.shape, bf16), pltpu.SemaphoreType.DMA((slots + 1 + len(later),))],
        flops=1000,
    )(near_ids, *[held(x, pltpu.HBM) for x in (x_late, near_blocks.reshape(slots, rows, rows), *later)])
    blocks = held(blocks, pltpu.VMEM)
    planes, halo[0], total = lax.optimization_barrier((planes, halo[0], total))
    others = [swapped(planes, reach) for reach in range(1, inner_size)]
    total, planes = lax.optimization_barrier((total, planes))
    total = kernel(functools.partial(wave_kernel, one), wide, [SMEM] + [VMEM] * 4, VMEM, lists * 2, aliases={4: 0}, flops=10**10)(
        near_ids, *halo[0], blocks, held(total, pltpu.VMEM)
    )
    others, total = lax.optimization_barrier((others, total))
    out, _ = kernel(
        functools.partial(close_kernel, one, leaf_size, inner_size),
        (jax.ShapeDtypeStruct(anomalies.shape, bf16), wide),
        [SMEM] * 3 + [VMEM] * (10 + inner_size),
        (ANY, VMEM),
        [
            pltpu.VMEM((inner_size * leaf_size * 2 * rank, columns), bf16),
            *lists * 2,
            pltpu.VMEM(anomalies.shape, bf16),
            pltpu.SemaphoreType.DMA((leaves,)),
        ],
        aliases={12 + inner_size: 1},
    )(near_ids, far_ids, far_count, *halo[1], blocks, plane, planes, *others, *later, held(total, pltpu.VMEM))
    return out


def solution(mesh):
    return jax.shard_map(
        local,
        mesh=mesh,
        in_specs=(
            P(("leaf", "inner"), "groups"),
            P(("leaf", "inner"), None, None),
            P(("leaf", "inner"), None, None, None),
            P(("leaf", "inner"), None),
            P(("leaf", "inner"), None, None),
            P(("leaf", "inner"), None, None),
            P(("leaf", "inner"), None),
            P(("leaf", "inner")),
            P(("leaf", "inner"), None, None, None),
            P("leaf", None, None, None),
        ),
        out_specs=P(("leaf", "inner"), "groups"),
        check_vma=False,
    )
```

```python
import functools

import jax
import jax.numpy as jnp
from jax import lax
from jax.experimental import pallas as pl
from jax.experimental.pallas import tpu as pltpu
from jax.sharding import PartitionSpec as P

MIB = 1 << 20
VMEM = pl.BlockSpec(memory_space=pltpu.VMEM)
SMEM = pl.BlockSpec(memory_space=pltpu.SMEM)
ANY = pl.BlockSpec(memory_space=pl.ANY)


def held(x, space):
    return pltpu.with_memory_space_constraint(x, space)


def resident(*shape, dtype=jnp.bfloat16):
    return pltpu.VMEM(shape, dtype)


def turn_of(leaf, inner_size):
    return (leaf + inner_size - 1) % inner_size


def carrier(turn, inner_size):
    return lax.rem(turn + 1, inner_size)


def dot(a, b):
    return lax.dot_general(a, b, (((1,), (0,)), ((), ())), preferred_element_type=jnp.float32)


def dot_t(a, b):
    return lax.dot_general(a, b, (((0,), (0,)), ((), ())), preferred_element_type=jnp.float32)


def call(kernel, out_shape, in_specs, out_specs, scratch, flops, moved, vmem, aliases=None):
    return pl.pallas_call(
        kernel,
        out_shape=out_shape,
        in_specs=in_specs,
        out_specs=out_specs,
        scratch_shapes=scratch,
        cost_estimate=pl.CostEstimate(flops=flops, bytes_accessed=moved, transcendentals=0),
        compiler_params=pltpu.CompilerParams(vmem_limit_bytes=vmem),
        input_output_aliases=aliases or {},
    )


def up_kernel(x_ref, basis_ref, leaf_map_ref, mid_map_ref, out_ref, x, basis, leaf_map, mid_map, skeleton, sems):
    leaves, rank, rows = basis.shape
    parts = []
    for leaf in range(leaves):
        here = slice(leaf * rows, (leaf + 1) * rows)
        parts.append(pltpu.make_async_copy(x_ref.at[here], x.at[here], sems.at[leaf]))
        parts.append(pltpu.make_async_copy(basis_ref.at[leaf], basis.at[leaf], sems.at[leaves + leaf]))
    maps = [pltpu.make_async_copy(leaf_map_ref, leaf_map, sems.at[2 * leaves]), pltpu.make_async_copy(mid_map_ref, mid_map, sems.at[2 * leaves + 1])]
    for copy in parts + maps:
        copy.start()
    for leaf in range(leaves):
        parts[2 * leaf].wait()
        parts[2 * leaf + 1].wait()
        skeleton[leaf * rank : (leaf + 1) * rank, :] = dot(basis[leaf], x[leaf * rows : (leaf + 1) * rows, :]).astype(jnp.bfloat16)
    for copy in maps:
        copy.wait()
    mid = dot_t(leaf_map[...], skeleton[...]).astype(jnp.bfloat16)
    out_ref[:rank, :] = mid
    out_ref[rank:, :] = dot_t(mid_map[...], mid).astype(jnp.bfloat16)


def pieces_kernel(x_ref, relayed, *refs):
    parts, (low, high, plane, sems) = refs[:-4], refs[-4:]
    inner = lax.axis_index("inner")
    size = low.shape[0]
    ends = (inner == lax.axis_size("inner") - 1, inner == 0)
    for i, (piece, at_end, first) in enumerate(zip((low, high), ends, (0, x_ref.shape[0] - size))):

        @pl.when(at_end)
        def _():
            pltpu.make_async_copy(relayed, piece, sems.at[i]).start()

        @pl.when(jnp.logical_not(at_end))
        def _():
            pltpu.make_async_copy(x_ref.at[first : first + size], piece, sems.at[i]).start()

    height = parts[0].shape[0]
    for i, part in enumerate(parts):
        plane[i * height : (i + 1) * height, :] = part[...]
    for i, piece in enumerate((low, high)):
        pltpu.make_async_copy(relayed, piece, sems.at[i]).wait()


def down_kernel(leaf_size, inner_size, far_ids, far_count, plane, *refs):
    found, refs = refs[:inner_size], refs[inner_size:]
    couple, mid_couple, mid_map, leaf_map, basis, _, total_ref, planes = refs
    rank = mid_map.shape[0]
    size = 2 * rank
    for step, part in enumerate(found):
        planes[step * leaf_size * size : (step + 1) * leaf_size * size, :] = part[...]
    group = lax.axis_index("leaf")
    inner = lax.axis_index("inner")

    def at_of(step, distance, offset=0):
        return pl.ds(pl.multiple_of((step * leaf_size + distance) * size + offset, rank), rank)

    top_down = jnp.zeros((rank, plane.shape[1]), jnp.float32)
    for distance in range(1, leaf_size):
        other = group ^ distance
        top = plane[at_of(0, distance, rank), :].astype(jnp.float32)
        for step in range(inner_size):
            top += planes[at_of(step, step ^ distance, rank), :].astype(jnp.float32)
        term = dot(couple[other], top.astype(jnp.bfloat16))
        top_down += jnp.where(jnp.abs(other - group) >= 2, term, 0.0)
    total = dot(mid_map[...], top_down.astype(jnp.bfloat16))
    for slot in range(mid_couple.shape[0]):
        live = slot < far_count[0]
        partner = jnp.where(live, far_ids[0, slot], group * inner_size)
        other, turn = partner // inner_size, inner ^ lax.rem(partner, inner_size)
        step = (group & (inner_size - 1)) ^ carrier(turn, inner_size)
        here, there = plane[at_of(0, group ^ other), :], planes[at_of(step, group ^ step ^ other), :]
        term = dot(mid_couple[slot], jnp.where(turn == 0, here, there))
        total += jnp.where(live, term, 0.0)
    leaf_down = dot(leaf_map[...], total.astype(jnp.bfloat16)).astype(jnp.bfloat16)
    leaves, _, rows = basis.shape
    for leaf in range(leaves):
        total_ref[leaf * rows : (leaf + 1) * rows, :] += dot_t(basis[leaf], leaf_down[leaf * rank : (leaf + 1) * rank, :])


def listed(ids_ref, lists, kind_of):
    leaves, near = ids_ref.shape
    first = (lax.axis_index("leaf") * lax.axis_size("inner") + lax.axis_index("inner")) * leaves

    def one(leaf, counts):
        for k in range(near):
            offset = ids_ref[leaf, k] - first
            grown = []
            for (slots, places), count, (member, place) in zip(lists, counts, kind_of(leaf, offset)):
                slots[count] = leaf * near + k
                places[count] = place
                grown.append(count + member.astype(jnp.int32))
            counts = tuple(grown)
        return counts

    return lax.fori_loop(0, leaves, one, (jnp.int32(0),) * len(lists))


def add_products(near, kind, count, blocks, x_ref, total, arrived=lambda slot: None):
    slots, places = kind
    rows = blocks.shape[1]
    half = rows // 2

    def product(i):
        slot = slots[i]
        arrived(slot)
        at = pl.ds(pl.multiple_of(places[i] * rows, rows), rows)
        here = slot // near * rows
        partner = x_ref[at, :]
        return here, [dot(blocks[slot, :half, :], partner), dot(blocks[slot, half:, :], partner)]

    def add(start, terms):
        for i, term in enumerate(terms):
            total[pl.ds(pl.multiple_of(start + i * half, half), half), :] += term

    def pair(j, carry):
        one, first = product(2 * j)
        two, second = product(2 * j + 1)
        add(one, first)
        add(two, second)
        return carry

    lax.fori_loop(0, count // 2, pair, 0)

    @pl.when(lax.rem(count, 2) == 1)
    def _():
        add(*product(count - 1))


def own_kernel(ids_ref, x_hbm, blocks_ref, *refs):
    count = (len(refs) - 8) // 2
    sources, total, blocks, targets = refs[:count], refs[count], refs[count + 1], refs[count + 2 : 2 * count + 2]
    own_slots, own_places, other_slots, other_places, x_ref, sems = refs[2 * count + 2 :]
    leaves, near = ids_ref.shape
    slots = leaves * near
    load = pltpu.make_async_copy(x_hbm, x_ref, sems.at[slots])
    load.start()

    def kind_of(leaf, offset):
        own = (offset >= 0) & (offset < leaves)
        return (own, offset), (jnp.logical_not(own), 0)

    kinds = ((own_slots, own_places), (other_slots, other_places))
    own_count, other_count = listed(ids_ref, kinds, kind_of)

    def copy(slot):
        return pltpu.make_async_copy(blocks_ref.at[slot], blocks.at[slot], sems.at[slot])

    def begin(slots):
        def one(i, carry):
            copy(slots[i]).start()
            return carry

        return one

    lax.fori_loop(0, own_count, begin(own_slots), 0)
    lax.fori_loop(0, other_count, begin(other_slots), 0)
    others = [pltpu.make_async_copy(source, target, sems.at[slots + 1 + i]) for i, (source, target) in enumerate(zip(sources, targets))]
    for other in others:
        other.start()
    total[...] = jnp.zeros_like(total)
    load.wait()
    add_products(near, kinds[0], own_count, blocks, x_ref, total, lambda slot: copy(slot).wait())

    def finish(i, carry):
        copy(other_slots[i]).wait()
        return carry

    lax.fori_loop(0, other_count, finish, 0)
    for other in others:
        other.wait()


def wave_kernel(near_by, ids_ref, before, after, blocks, _, total, *lists):
    leaves, near = ids_ref.shape

    def kind_of(leaf, offset):
        return ((offset < 0) & (offset >= -near_by), offset + near_by), ((offset >= leaves) & (offset < leaves + near_by), offset - leaves)

    kinds = (lists[:2], lists[2:])
    counts = listed(ids_ref, kinds, kind_of)
    for kind, count, x_ref in zip(kinds, counts, (before, after)):
        add_products(near, kind, count, blocks, x_ref, total)


def last_kernel(near_by, ids_ref, before, after, blocks, _, out_ref, total, *refs):
    lists, (result, sems) = refs[:4], refs[4:]
    leaves, near = ids_ref.shape
    rows = blocks.shape[1]

    def kind_of(leaf, offset):
        return (offset < -near_by, offset + leaves), (offset >= leaves + near_by, offset - leaves - near_by)

    kinds = (lists[:2], lists[2:])
    counts = listed(ids_ref, kinds, kind_of)
    for kind, count, x_ref in zip(kinds, counts, (before, after)):
        add_products(near, kind, count, blocks, x_ref, total)
    stores = []
    for leaf in range(leaves):
        here = slice(leaf * rows, (leaf + 1) * rows)
        result[here, :] = total[here, :].astype(result.dtype)
        stores.append(pltpu.make_async_copy(result.at[here], out_ref.at[here], sems.at[leaf]))
        stores[-1].start()
    for store in stores:
        store.wait()


def local(anomalies, leaf_basis, near_blocks, near_ids, transfer_leaf, transfer_mid, far_ids, far_count, mid_couple, top_couple):
    leaves, rank, rows = leaf_basis.shape
    near = near_blocks.shape[1]
    columns = anomalies.shape[1]
    inner_size = lax.axis_size("inner")
    leaf_size = lax.axis_size("leaf")
    bf16 = jnp.bfloat16
    inner = lax.axis_index("inner")
    first, last = 0, inner_size - 1
    groups = range(leaf_size)

    def place(leaf, i):
        return leaf * inner_size + i

    def passed(x, pairs):
        return lax.ppermute(x, ("leaf", "inner"), pairs)

    def swapped(x, reach):
        return lax.ppermute(x, "leaf", [(i, i ^ reach) for i in groups])

    chain = [(i, i + 1) for i in range(leaf_size * inner_size - 1)]
    line = [(place(g, i), place(g, i + 1)) for g in groups for i in range(last)]
    hop = [(place(g, last), place(g + 1, last)) for g in groups[:-1]] + [(place(g, first), place(g - 1, first)) for g in groups[1:]]

    one = leaves * 5 // 8
    rest = leaves - one
    def kernel(body, out_shape, in_specs, out_specs, scratch, aliases=None, flops=1000):
        return call(body, out_shape, in_specs, out_specs, scratch, flops, 1000, 8 * MIB, aliases)

    ahead, back = lax.slice_in_dim(anomalies, rest * rows, leaves * rows), lax.slice_in_dim(anomalies, 0, one * rows)
    x_up, ahead, back = lax.optimization_barrier((anomalies, ahead, back))
    relay = jnp.where(inner == first, lax.slice_in_dim(x_up, one * rows, leaves * rows), lax.slice_in_dim(x_up, 0, rest * rows))
    relayed = passed(relay, hop)
    halo = [(passed(ahead, chain), passed(back, [(j, i) for i, j in chain]))]

    maps = (transfer_leaf.reshape(leaves * rank, rank), transfer_mid.reshape(rank, rank))
    operands = (x_up, leaf_basis, *maps)
    piece = jax.ShapeDtypeStruct((rest * rows, columns), bf16)
    part = kernel(
        up_kernel,
        jax.ShapeDtypeStruct((2 * rank, columns), bf16),
        [ANY] * 4,
        VMEM,
        [pltpu.VMEM(x.shape, bf16) for x in operands] + [pltpu.VMEM((leaves * rank, columns), bf16), pltpu.SemaphoreType.DMA((2 * leaves + 2,))],
    )(*[held(x, pltpu.HBM) for x in operands])
    parts = [part] + [swapped(part, reach) for reach in groups[1:]]
    slots = leaves * near
    parts, x_late, relayed = lax.optimization_barrier((parts, x_up, relayed))
    low, high, plane = kernel(
        pieces_kernel,
        (piece, piece, jax.ShapeDtypeStruct((leaf_size * 2 * rank, columns), bf16)),
        [ANY] * 2 + [VMEM] * leaf_size,
        [VMEM] * 3,
        [pltpu.SemaphoreType.DMA((2,))],
    )(held(x_late, pltpu.HBM), relayed, *parts)
    low, high, plane, x_late = lax.optimization_barrier((low, high, plane, x_late))
    turns = [(place(g, i), place(g, i ^ turn_of(g, inner_size))) for g in groups for i in range(inner_size)]
    planes = passed(plane, [(i, j) for i, j in turns if i != j])
    halo.append(
        (
            passed(low, line + [(place(g, last), place(g, first)) for g in groups[1:]]),
            passed(high, [(j, i) for i, j in line] + [(place(g, first), place(g, last)) for g in groups[:-1]]),
        )
    )
    lists = [pltpu.SMEM((slots + 1,), jnp.int32)] * 2
    wide = resident(leaves * rows, columns, dtype=jnp.float32)
    later = (top_couple[0], mid_couple[0], maps[1], maps[0], leaf_basis)
    total, blocks, *later = kernel(
        own_kernel,
        [wide, resident(slots, rows, rows)] + [resident(*x.shape) for x in later],
        [SMEM] + [ANY] * (2 + len(later)),
        [VMEM] * (2 + len(later)),
        lists * 2 + [pltpu.VMEM(anomalies.shape, bf16), pltpu.SemaphoreType.DMA((slots + 1 + len(later),))],
        flops=1000,
    )(near_ids, *[held(x, pltpu.HBM) for x in (x_late, near_blocks.reshape(slots, rows, rows), *later)])
    blocks = held(blocks, pltpu.VMEM)
    planes, halo[0], total = lax.optimization_barrier((planes, halo[0], total))
    others = [swapped(planes, reach) for reach in range(1, inner_size)]
    total, planes = lax.optimization_barrier((total, planes))
    total = kernel(functools.partial(wave_kernel, one), wide, [SMEM] + [VMEM] * 4, VMEM, lists * 2, aliases={4: 0}, flops=10**10)(
        near_ids, *halo[0], blocks, held(total, pltpu.VMEM)
    )
    others, total = lax.optimization_barrier((others, total))
    total = kernel(
        functools.partial(down_kernel, leaf_size, inner_size),
        wide,
        [SMEM] * 2 + [VMEM] * (7 + inner_size),
        VMEM,
        [pltpu.VMEM((inner_size * leaf_size * 2 * rank, columns), bf16)],
        aliases={8 + inner_size: 0},
    )(far_ids, far_count, plane, planes, *others, *later, held(total, pltpu.VMEM))
    out, _ = kernel(
        functools.partial(last_kernel, one),
        (jax.ShapeDtypeStruct(anomalies.shape, bf16), wide),
        [SMEM] + [VMEM] * 4,
        (ANY, VMEM),
        lists * 2 + [pltpu.VMEM(anomalies.shape, bf16), pltpu.SemaphoreType.DMA((leaves,))],
        aliases={4: 1},
    )(near_ids, *halo[1], blocks, held(total, pltpu.VMEM))
    return out


def solution(mesh):
    return jax.shard_map(
        local,
        mesh=mesh,
        in_specs=(
            P(("leaf", "inner"), "groups"),
            P(("leaf", "inner"), None, None),
            P(("leaf", "inner"), None, None, None),
            P(("leaf", "inner"), None),
            P(("leaf", "inner"), None, None),
            P(("leaf", "inner"), None, None),
            P(("leaf", "inner"), None),
            P(("leaf", "inner")),
            P(("leaf", "inner"), None, None, None),
            P("leaf", None, None, None),
        ),
        out_specs=P(("leaf", "inner"), "groups"),
        check_vma=False,
    )
```

```python
import functools

import jax
import jax.numpy as jnp
from jax import lax
from jax.experimental import pallas as pl
from jax.experimental.pallas import tpu as pltpu
from jax.sharding import PartitionSpec as P

MIB = 1 << 20
VMEM = pl.BlockSpec(memory_space=pltpu.VMEM)
SMEM = pl.BlockSpec(memory_space=pltpu.SMEM)
ANY = pl.BlockSpec(memory_space=pl.ANY)


def held(x, space):
    return pltpu.with_memory_space_constraint(x, space)


def resident(*shape, dtype=jnp.bfloat16):
    return pltpu.VMEM(shape, dtype)


def turn_of(leaf, inner_size):
    return (3 * leaf + 2) % inner_size


def carrier(turn, inner_size):
    return lax.rem((turn + inner_size - 2 % inner_size) * pow(3, -1, inner_size), inner_size)


def dot(a, b):
    return lax.dot_general(a, b, (((1,), (0,)), ((), ())), preferred_element_type=jnp.float32)


def dot_t(a, b):
    return lax.dot_general(a, b, (((0,), (0,)), ((), ())), preferred_element_type=jnp.float32)


def call(kernel, out_shape, in_specs, out_specs, scratch, flops, moved, vmem, aliases=None):
    return pl.pallas_call(
        kernel,
        out_shape=out_shape,
        in_specs=in_specs,
        out_specs=out_specs,
        scratch_shapes=scratch,
        cost_estimate=pl.CostEstimate(flops=flops, bytes_accessed=moved, transcendentals=0),
        compiler_params=pltpu.CompilerParams(vmem_limit_bytes=vmem),
        input_output_aliases=aliases or {},
    )


def up_kernel(x_ref, basis_ref, leaf_map_ref, mid_map_ref, out_ref, x, basis, leaf_map, mid_map, skeleton, sems):
    leaves, rank, rows = basis.shape
    parts = []
    for leaf in range(leaves):
        here = slice(leaf * rows, (leaf + 1) * rows)
        parts.append(pltpu.make_async_copy(x_ref.at[here], x.at[here], sems.at[leaf]))
        parts.append(pltpu.make_async_copy(basis_ref.at[leaf], basis.at[leaf], sems.at[leaves + leaf]))
    maps = [pltpu.make_async_copy(leaf_map_ref, leaf_map, sems.at[2 * leaves]), pltpu.make_async_copy(mid_map_ref, mid_map, sems.at[2 * leaves + 1])]
    for copy in parts + maps:
        copy.start()
    for leaf in range(leaves):
        parts[2 * leaf].wait()
        parts[2 * leaf + 1].wait()
        skeleton[leaf * rank : (leaf + 1) * rank, :] = dot(basis[leaf], x[leaf * rows : (leaf + 1) * rows, :]).astype(jnp.bfloat16)
    for copy in maps:
        copy.wait()
    mid = dot_t(leaf_map[...], skeleton[...]).astype(jnp.bfloat16)
    out_ref[:rank, :] = mid
    out_ref[rank:, :] = dot_t(mid_map[...], mid).astype(jnp.bfloat16)


def pieces_kernel(x_ref, relayed, *refs):
    parts, (low, high, plane, sems) = refs[:-4], refs[-4:]
    inner = lax.axis_index("inner")
    size = low.shape[0]
    ends = (inner == lax.axis_size("inner") - 1, inner == 0)
    for i, (piece, at_end, first) in enumerate(zip((low, high), ends, (0, x_ref.shape[0] - size))):

        @pl.when(at_end)
        def _():
            pltpu.make_async_copy(relayed, piece, sems.at[i]).start()

        @pl.when(jnp.logical_not(at_end))
        def _():
            pltpu.make_async_copy(x_ref.at[first : first + size], piece, sems.at[i]).start()

    height = parts[0].shape[0]
    for i, part in enumerate(parts):
        plane[i * height : (i + 1) * height, :] = part[...]
    for i, piece in enumerate((low, high)):
        pltpu.make_async_copy(relayed, piece, sems.at[i]).wait()


def down_kernel(leaf_size, inner_size, far_ids, far_count, plane, *refs):
    found, refs = refs[:inner_size], refs[inner_size:]
    couple, mid_couple, mid_map, leaf_map, basis, _, total_ref, planes = refs
    rank = mid_map.shape[0]
    size = 2 * rank
    for step, part in enumerate(found):
        planes[step * leaf_size * size : (step + 1) * leaf_size * size, :] = part[...]
    group = lax.axis_index("leaf")
    inner = lax.axis_index("inner")

    def at_of(step, distance, offset=0):
        return pl.ds(pl.multiple_of((step * leaf_size + distance) * size + offset, rank), rank)

    top_down = jnp.zeros((rank, plane.shape[1]), jnp.float32)
    for distance in range(1, leaf_size):
        other = group ^ distance
        top = plane[at_of(0, distance, rank), :].astype(jnp.float32)
        for step in range(inner_size):
            top += planes[at_of(step, step ^ distance, rank), :].astype(jnp.float32)
        term = dot(couple[other], top.astype(jnp.bfloat16))
        top_down += jnp.where(jnp.abs(other - group) >= 2, term, 0.0)
    total = dot(mid_map[...], top_down.astype(jnp.bfloat16))
    for slot in range(mid_couple.shape[0]):
        live = slot < far_count[0]
        partner = jnp.where(live, far_ids[0, slot], group * inner_size)
        other, turn = partner // inner_size, inner ^ lax.rem(partner, inner_size)
        step = (group & (inner_size - 1)) ^ carrier(turn, inner_size)
        here, there = plane[at_of(0, group ^ other), :], planes[at_of(step, group ^ step ^ other), :]
        term = dot(mid_couple[slot], jnp.where(turn == 0, here, there))
        total += jnp.where(live, term, 0.0)
    leaf_down = dot(leaf_map[...], total.astype(jnp.bfloat16)).astype(jnp.bfloat16)
    leaves, _, rows = basis.shape
    for leaf in range(leaves):
        total_ref[leaf * rows : (leaf + 1) * rows, :] += dot_t(basis[leaf], leaf_down[leaf * rank : (leaf + 1) * rank, :])


def listed(ids_ref, lists, kind_of):
    leaves, near = ids_ref.shape
    first = (lax.axis_index("leaf") * lax.axis_size("inner") + lax.axis_index("inner")) * leaves

    def one(leaf, counts):
        for k in range(near):
            offset = ids_ref[leaf, k] - first
            grown = []
            for (slots, places), count, (member, place) in zip(lists, counts, kind_of(leaf, offset)):
                slots[count] = leaf * near + k
                places[count] = place
                grown.append(count + member.astype(jnp.int32))
            counts = tuple(grown)
        return counts

    return lax.fori_loop(0, leaves, one, (jnp.int32(0),) * len(lists))


def add_products(near, kind, count, blocks, x_ref, total, arrived=lambda slot: None):
    slots, places = kind
    rows = blocks.shape[1]
    half = rows // 2

    def product(i):
        slot = slots[i]
        arrived(slot)
        at = pl.ds(pl.multiple_of(places[i] * rows, rows), rows)
        here = slot // near * rows
        partner = x_ref[at, :]
        return here, [dot(blocks[slot, :half, :], partner), dot(blocks[slot, half:, :], partner)]

    def add(start, terms):
        for i, term in enumerate(terms):
            total[pl.ds(pl.multiple_of(start + i * half, half), half), :] += term

    def pair(j, carry):
        one, first = product(2 * j)
        two, second = product(2 * j + 1)
        add(one, first)
        add(two, second)
        return carry

    lax.fori_loop(0, count // 2, pair, 0)

    @pl.when(lax.rem(count, 2) == 1)
    def _():
        add(*product(count - 1))


def own_kernel(ids_ref, x_hbm, blocks_ref, *refs):
    count = (len(refs) - 8) // 2
    sources, total, blocks, targets = refs[:count], refs[count], refs[count + 1], refs[count + 2 : 2 * count + 2]
    own_slots, own_places, other_slots, other_places, x_ref, sems = refs[2 * count + 2 :]
    leaves, near = ids_ref.shape
    slots = leaves * near
    load = pltpu.make_async_copy(x_hbm, x_ref, sems.at[slots])
    load.start()

    def kind_of(leaf, offset):
        own = (offset >= 0) & (offset < leaves)
        return (own, offset), (jnp.logical_not(own), 0)

    kinds = ((own_slots, own_places), (other_slots, other_places))
    own_count, other_count = listed(ids_ref, kinds, kind_of)

    def copy(slot):
        return pltpu.make_async_copy(blocks_ref.at[slot], blocks.at[slot], sems.at[slot])

    def begin(slots):
        def one(i, carry):
            copy(slots[i]).start()
            return carry

        return one

    lax.fori_loop(0, own_count, begin(own_slots), 0)
    lax.fori_loop(0, other_count, begin(other_slots), 0)
    others = [pltpu.make_async_copy(source, target, sems.at[slots + 1 + i]) for i, (source, target) in enumerate(zip(sources, targets))]
    for other in others:
        other.start()
    total[...] = jnp.zeros_like(total)
    load.wait()
    add_products(near, kinds[0], own_count, blocks, x_ref, total, lambda slot: copy(slot).wait())

    def finish(i, carry):
        copy(other_slots[i]).wait()
        return carry

    lax.fori_loop(0, other_count, finish, 0)
    for other in others:
        other.wait()


def wave_kernel(near_by, ids_ref, before, after, blocks, _, total, *lists):
    leaves, near = ids_ref.shape

    def kind_of(leaf, offset):
        return ((offset < 0) & (offset >= -near_by), offset + near_by), ((offset >= leaves) & (offset < leaves + near_by), offset - leaves)

    kinds = (lists[:2], lists[2:])
    counts = listed(ids_ref, kinds, kind_of)
    for kind, count, x_ref in zip(kinds, counts, (before, after)):
        add_products(near, kind, count, blocks, x_ref, total)


def last_kernel(near_by, ids_ref, before, after, blocks, _, out_ref, total, *refs):
    lists, (result, sems) = refs[:4], refs[4:]
    leaves, near = ids_ref.shape
    rows = blocks.shape[1]

    def kind_of(leaf, offset):
        return (offset < -near_by, offset + leaves), (offset >= leaves + near_by, offset - leaves - near_by)

    kinds = (lists[:2], lists[2:])
    counts = listed(ids_ref, kinds, kind_of)
    for kind, count, x_ref in zip(kinds, counts, (before, after)):
        add_products(near, kind, count, blocks, x_ref, total)
    stores = []
    for leaf in range(leaves):
        here = slice(leaf * rows, (leaf + 1) * rows)
        result[here, :] = total[here, :].astype(result.dtype)
        stores.append(pltpu.make_async_copy(result.at[here], out_ref.at[here], sems.at[leaf]))
        stores[-1].start()
    for store in stores:
        store.wait()


def local(anomalies, leaf_basis, near_blocks, near_ids, transfer_leaf, transfer_mid, far_ids, far_count, mid_couple, top_couple):
    leaves, rank, rows = leaf_basis.shape
    near = near_blocks.shape[1]
    columns = anomalies.shape[1]
    inner_size = lax.axis_size("inner")
    leaf_size = lax.axis_size("leaf")
    bf16 = jnp.bfloat16
    inner = lax.axis_index("inner")
    first, last = 0, inner_size - 1
    groups = range(leaf_size)

    def place(leaf, i):
        return leaf * inner_size + i

    def passed(x, pairs):
        return lax.ppermute(x, ("leaf", "inner"), pairs)

    def swapped(x, reach):
        return lax.ppermute(x, "leaf", [(i, i ^ reach) for i in groups])

    chain = [(i, i + 1) for i in range(leaf_size * inner_size - 1)]
    line = [(place(g, i), place(g, i + 1)) for g in groups for i in range(last)]
    hop = [(place(g, last), place(g + 1, last)) for g in groups[:-1]] + [(place(g, first), place(g - 1, first)) for g in groups[1:]]

    one = leaves * 5 // 8
    rest = leaves - one
    def kernel(body, out_shape, in_specs, out_specs, scratch, aliases=None, flops=1000):
        return call(body, out_shape, in_specs, out_specs, scratch, flops, 1000, 8 * MIB, aliases)

    ahead, back = lax.slice_in_dim(anomalies, rest * rows, leaves * rows), lax.slice_in_dim(anomalies, 0, one * rows)
    x_up, ahead, back = lax.optimization_barrier((anomalies, ahead, back))
    relay = lax.dynamic_slice_in_dim(x_up, jnp.where(inner == first, one * rows, 0), rest * rows)
    relayed = passed(relay, hop)
    halo = [(passed(ahead, chain), passed(back, [(j, i) for i, j in chain]))]

    maps = (transfer_leaf.reshape(leaves * rank, rank), transfer_mid.reshape(rank, rank))
    operands = (x_up, leaf_basis, *maps)
    piece = jax.ShapeDtypeStruct((rest * rows, columns), bf16)
    part = kernel(
        up_kernel,
        jax.ShapeDtypeStruct((2 * rank, columns), bf16),
        [ANY] * 4,
        VMEM,
        [pltpu.VMEM(x.shape, bf16) for x in operands] + [pltpu.VMEM((leaves * rank, columns), bf16), pltpu.SemaphoreType.DMA((2 * leaves + 2,))],
    )(*[held(x, pltpu.HBM) for x in operands])
    parts = [part] + [swapped(part, reach) for reach in groups[1:]]
    slots = leaves * near
    parts, x_late, relayed = lax.optimization_barrier((parts, x_up, relayed))
    low, high, plane = kernel(
        pieces_kernel,
        (piece, piece, jax.ShapeDtypeStruct((leaf_size * 2 * rank, columns), bf16)),
        [ANY] * 2 + [VMEM] * leaf_size,
        [VMEM] * 3,
        [pltpu.SemaphoreType.DMA((2,))],
    )(held(x_late, pltpu.HBM), relayed, *parts)
    low, high, plane, x_late = lax.optimization_barrier((low, high, plane, x_late))
    turns = [(place(g, i), place(g, i ^ turn_of(g, inner_size))) for g in groups for i in range(inner_size)]
    planes = passed(plane, [(i, j) for i, j in turns if i != j])
    halo.append(
        (
            passed(low, line + [(place(g, last), place(g, first)) for g in groups[1:]]),
            passed(high, [(j, i) for i, j in line] + [(place(g, first), place(g, last)) for g in groups[:-1]]),
        )
    )
    lists = [pltpu.SMEM((slots + 1,), jnp.int32)] * 2
    wide = resident(leaves * rows, columns, dtype=jnp.float32)
    later = (top_couple[0], mid_couple[0], maps[1], maps[0], leaf_basis)
    total, blocks, *later = kernel(
        own_kernel,
        [wide, resident(slots, rows, rows)] + [resident(*x.shape) for x in later],
        [SMEM] + [ANY] * (2 + len(later)),
        [VMEM] * (2 + len(later)),
        lists * 2 + [pltpu.VMEM(anomalies.shape, bf16), pltpu.SemaphoreType.DMA((slots + 1 + len(later),))],
        flops=1000,
    )(near_ids, *[held(x, pltpu.HBM) for x in (x_late, near_blocks.reshape(slots, rows, rows), *later)])
    blocks = held(blocks, pltpu.VMEM)
    planes, halo[0], total = lax.optimization_barrier((planes, halo[0], total))
    others = [swapped(planes, reach) for reach in range(1, inner_size)]
    total, planes = lax.optimization_barrier((total, planes))
    total = kernel(functools.partial(wave_kernel, one), wide, [SMEM] + [VMEM] * 4, VMEM, lists * 2, aliases={4: 0}, flops=10**10)(
        near_ids, *halo[0], blocks, held(total, pltpu.VMEM)
    )
    others, total = lax.optimization_barrier((others, total))
    total = kernel(
        functools.partial(down_kernel, leaf_size, inner_size),
        wide,
        [SMEM] * 2 + [VMEM] * (7 + inner_size),
        VMEM,
        [pltpu.VMEM((inner_size * leaf_size * 2 * rank, columns), bf16)],
        aliases={8 + inner_size: 0},
    )(far_ids, far_count, plane, planes, *others, *later, held(total, pltpu.VMEM))
    out, _ = kernel(
        functools.partial(last_kernel, one),
        (jax.ShapeDtypeStruct(anomalies.shape, bf16), wide),
        [SMEM] + [VMEM] * 4,
        (ANY, VMEM),
        lists * 2 + [pltpu.VMEM(anomalies.shape, bf16), pltpu.SemaphoreType.DMA((leaves,))],
        aliases={4: 1},
    )(near_ids, *halo[1], blocks, held(total, pltpu.VMEM))
    return out


def solution(mesh):
    return jax.shard_map(
        local,
        mesh=mesh,
        in_specs=(
            P(("leaf", "inner"), "groups"),
            P(("leaf", "inner"), None, None),
            P(("leaf", "inner"), None, None, None),
            P(("leaf", "inner"), None),
            P(("leaf", "inner"), None, None),
            P(("leaf", "inner"), None, None),
            P(("leaf", "inner"), None),
            P(("leaf", "inner")),
            P(("leaf", "inner"), None, None, None),
            P("leaf", None, None, None),
        ),
        out_specs=P(("leaf", "inner"), "groups"),
        check_vma=False,
    )
```

```python
import functools

import jax
import jax.numpy as jnp
from jax import lax
from jax.experimental import pallas as pl
from jax.experimental.pallas import tpu as pltpu
from jax.sharding import PartitionSpec as P

MIB = 1 << 20
VMEM = pl.BlockSpec(memory_space=pltpu.VMEM)
SMEM = pl.BlockSpec(memory_space=pltpu.SMEM)
ANY = pl.BlockSpec(memory_space=pl.ANY)


def held(x, space):
    return pltpu.with_memory_space_constraint(x, space)


def resident(*shape, dtype=jnp.bfloat16):
    return pltpu.VMEM(shape, dtype)


def turn_of(leaf, inner_size):
    return (3 * leaf + 2) % inner_size


def carrier(turn, inner_size):
    return lax.rem((turn + inner_size - 2 % inner_size) * pow(3, -1, inner_size), inner_size)


def dot(a, b):
    return lax.dot_general(a, b, (((1,), (0,)), ((), ())), preferred_element_type=jnp.float32)


def dot_t(a, b):
    return lax.dot_general(a, b, (((0,), (0,)), ((), ())), preferred_element_type=jnp.float32)


def call(kernel, out_shape, in_specs, out_specs, scratch, flops, moved, vmem, aliases=None):
    return pl.pallas_call(
        kernel,
        out_shape=out_shape,
        in_specs=in_specs,
        out_specs=out_specs,
        scratch_shapes=scratch,
        cost_estimate=pl.CostEstimate(flops=flops, bytes_accessed=moved, transcendentals=0),
        compiler_params=pltpu.CompilerParams(vmem_limit_bytes=vmem),
        input_output_aliases=aliases or {},
    )


def up_kernel(x_ref, basis_ref, leaf_map_ref, mid_map_ref, out_ref, x, basis, leaf_map, mid_map, skeleton, sems):
    leaves, rank, rows = basis.shape
    parts = []
    for leaf in range(leaves):
        here = slice(leaf * rows, (leaf + 1) * rows)
        parts.append(pltpu.make_async_copy(x_ref.at[here], x.at[here], sems.at[leaf]))
        parts.append(pltpu.make_async_copy(basis_ref.at[leaf], basis.at[leaf], sems.at[leaves + leaf]))
    maps = [pltpu.make_async_copy(leaf_map_ref, leaf_map, sems.at[2 * leaves]), pltpu.make_async_copy(mid_map_ref, mid_map, sems.at[2 * leaves + 1])]
    for copy in parts + maps:
        copy.start()
    for leaf in range(leaves):
        parts[2 * leaf].wait()
        parts[2 * leaf + 1].wait()
        skeleton[leaf * rank : (leaf + 1) * rank, :] = dot(basis[leaf], x[leaf * rows : (leaf + 1) * rows, :]).astype(jnp.bfloat16)
    for copy in maps:
        copy.wait()
    mid = dot_t(leaf_map[...], skeleton[...]).astype(jnp.bfloat16)
    out_ref[:rank, :] = mid
    out_ref[rank:, :] = dot_t(mid_map[...], mid).astype(jnp.bfloat16)


def pieces_kernel(x_ref, relayed, *refs):
    parts, (low, high, plane, sems) = refs[:-4], refs[-4:]
    inner = lax.axis_index("inner")
    ends = (inner == lax.axis_size("inner") - 1, inner == 0)
    for i, (piece, at_end, first) in enumerate(zip((low, high), ends, (0, x_ref.shape[0] - high.shape[0]))):
        size = piece.shape[0]
        handed = relayed.at[relayed.shape[0] - size :]

        @pl.when(at_end)
        def _():
            pltpu.make_async_copy(handed, piece, sems.at[i]).start()

        @pl.when(jnp.logical_not(at_end))
        def _():
            pltpu.make_async_copy(x_ref.at[first : first + size], piece, sems.at[i]).start()

    height = parts[0].shape[0]
    for i, part in enumerate(parts):
        plane[i * height : (i + 1) * height, :] = part[...]
    for i, piece in enumerate((low, high)):
        pltpu.make_async_copy(relayed.at[: piece.shape[0]], piece, sems.at[i]).wait()


def down_kernel(leaf_size, inner_size, far_ids, far_count, plane, *refs):
    found, refs = refs[:inner_size], refs[inner_size:]
    couple, mid_couple, mid_map, leaf_map, basis, _, total_ref, planes = refs
    rank = mid_map.shape[0]
    size = 2 * rank
    for step, part in enumerate(found):
        planes[step * leaf_size * size : (step + 1) * leaf_size * size, :] = part[...]
    group = lax.axis_index("leaf")
    inner = lax.axis_index("inner")

    def at_of(step, distance, offset=0):
        return pl.ds(pl.multiple_of((step * leaf_size + distance) * size + offset, rank), rank)

    top_down = jnp.zeros((rank, plane.shape[1]), jnp.float32)
    for distance in range(1, leaf_size):
        other = group ^ distance
        top = plane[at_of(0, distance, rank), :].astype(jnp.float32)
        for step in range(inner_size):
            top += planes[at_of(step, step ^ distance, rank), :].astype(jnp.float32)
        term = dot(couple[other], top.astype(jnp.bfloat16))
        top_down += jnp.where(jnp.abs(other - group) >= 2, term, 0.0)
    total = dot(mid_map[...], top_down.astype(jnp.bfloat16))
    for slot in range(mid_couple.shape[0]):
        live = slot < far_count[0]
        partner = jnp.where(live, far_ids[0, slot], group * inner_size)
        other, turn = partner // inner_size, inner ^ lax.rem(partner, inner_size)
        step = (group & (inner_size - 1)) ^ carrier(turn, inner_size)
        here, there = plane[at_of(0, group ^ other), :], planes[at_of(step, group ^ step ^ other), :]
        term = dot(mid_couple[slot], jnp.where(turn == 0, here, there))
        total += jnp.where(live, term, 0.0)
    leaf_down = dot(leaf_map[...], total.astype(jnp.bfloat16)).astype(jnp.bfloat16)
    leaves, _, rows = basis.shape
    for leaf in range(leaves):
        total_ref[leaf * rows : (leaf + 1) * rows, :] += dot_t(basis[leaf], leaf_down[leaf * rank : (leaf + 1) * rank, :])


def listed(ids_ref, lists, kind_of):
    leaves, near = ids_ref.shape
    first = (lax.axis_index("leaf") * lax.axis_size("inner") + lax.axis_index("inner")) * leaves

    def one(leaf, counts):
        for k in range(near):
            offset = ids_ref[leaf, k] - first
            grown = []
            for (slots, places), count, (member, place) in zip(lists, counts, kind_of(leaf, offset)):
                slots[count] = leaf * near + k
                places[count] = place
                grown.append(count + member.astype(jnp.int32))
            counts = tuple(grown)
        return counts

    return lax.fori_loop(0, leaves, one, (jnp.int32(0),) * len(lists))


def add_products(near, kind, count, blocks, x_ref, total, arrived=lambda slot: None):
    slots, places = kind
    rows = blocks.shape[1]
    half = rows // 2

    def product(i):
        slot = slots[i]
        arrived(slot)
        at = pl.ds(pl.multiple_of(places[i] * rows, rows), rows)
        here = slot // near * rows
        partner = x_ref[at, :]
        return here, [dot(blocks[slot, :half, :], partner), dot(blocks[slot, half:, :], partner)]

    def add(start, terms):
        for i, term in enumerate(terms):
            total[pl.ds(pl.multiple_of(start + i * half, half), half), :] += term

    def pair(j, carry):
        one, first = product(2 * j)
        two, second = product(2 * j + 1)
        add(one, first)
        add(two, second)
        return carry

    lax.fori_loop(0, count // 2, pair, 0)

    @pl.when(lax.rem(count, 2) == 1)
    def _():
        add(*product(count - 1))


def own_kernel(ids_ref, x_hbm, blocks_ref, *refs):
    count = (len(refs) - 8) // 2
    sources, total, blocks, targets = refs[:count], refs[count], refs[count + 1], refs[count + 2 : 2 * count + 2]
    own_slots, own_places, other_slots, other_places, x_ref, sems = refs[2 * count + 2 :]
    leaves, near = ids_ref.shape
    slots = leaves * near
    load = pltpu.make_async_copy(x_hbm, x_ref, sems.at[slots])
    load.start()

    def kind_of(leaf, offset):
        own = (offset >= 0) & (offset < leaves)
        return (own, offset), (jnp.logical_not(own), 0)

    kinds = ((own_slots, own_places), (other_slots, other_places))
    own_count, other_count = listed(ids_ref, kinds, kind_of)

    def copy(slot):
        return pltpu.make_async_copy(blocks_ref.at[slot], blocks.at[slot], sems.at[slot])

    def begin(slots):
        def one(i, carry):
            copy(slots[i]).start()
            return carry

        return one

    lax.fori_loop(0, own_count, begin(own_slots), 0)
    lax.fori_loop(0, other_count, begin(other_slots), 0)
    others = [pltpu.make_async_copy(source, target, sems.at[slots + 1 + i]) for i, (source, target) in enumerate(zip(sources, targets))]
    for other in others:
        other.start()
    total[...] = jnp.zeros_like(total)
    load.wait()
    add_products(near, kinds[0], own_count, blocks, x_ref, total, lambda slot: copy(slot).wait())

    def finish(i, carry):
        copy(other_slots[i]).wait()
        return carry

    lax.fori_loop(0, other_count, finish, 0)
    for other in others:
        other.wait()


def wave_kernel(lead, near_by, ids_ref, before, after, blocks, _, total, *lists):
    leaves, near = ids_ref.shape

    def kind_of(leaf, offset):
        return ((offset < 0) & (offset >= -lead), offset + lead), ((offset >= leaves) & (offset < leaves + near_by), offset - leaves)

    kinds = (lists[:2], lists[2:])
    counts = listed(ids_ref, kinds, kind_of)
    for kind, count, x_ref in zip(kinds, counts, (before, after)):
        add_products(near, kind, count, blocks, x_ref, total)


def last_kernel(lead, near_by, ids_ref, before, after, blocks, _, out_ref, total, *refs):
    lists, (result, sems) = refs[:4], refs[4:]
    leaves, near = ids_ref.shape
    rows = blocks.shape[1]

    def kind_of(leaf, offset):
        return (offset < -lead, offset + leaves), (offset >= leaves + near_by, offset - leaves - near_by)

    kinds = (lists[:2], lists[2:])
    counts = listed(ids_ref, kinds, kind_of)
    for kind, count, x_ref in zip(kinds, counts, (before, after)):
        add_products(near, kind, count, blocks, x_ref, total)
    stores = []
    for leaf in range(leaves):
        here = slice(leaf * rows, (leaf + 1) * rows)
        result[here, :] = total[here, :].astype(result.dtype)
        stores.append(pltpu.make_async_copy(result.at[here], out_ref.at[here], sems.at[leaf]))
        stores[-1].start()
    for store in stores:
        store.wait()


def local(anomalies, leaf_basis, near_blocks, near_ids, transfer_leaf, transfer_mid, far_ids, far_count, mid_couple, top_couple):
    leaves, rank, rows = leaf_basis.shape
    near = near_blocks.shape[1]
    columns = anomalies.shape[1]
    inner_size = lax.axis_size("inner")
    leaf_size = lax.axis_size("leaf")
    bf16 = jnp.bfloat16
    inner = lax.axis_index("inner")
    first, last = 0, inner_size - 1
    groups = range(leaf_size)

    def place(leaf, i):
        return leaf * inner_size + i

    def passed(x, pairs):
        return lax.ppermute(x, ("leaf", "inner"), pairs)

    def swapped(x, reach):
        return lax.ppermute(x, "leaf", [(i, i ^ reach) for i in groups])

    chain = [(i, i + 1) for i in range(leaf_size * inner_size - 1)]
    line = [(place(g, i), place(g, i + 1)) for g in groups for i in range(last)]
    hop = [(place(g, last), place(g + 1, last)) for g in groups[:-1]] + [(place(g, first), place(g - 1, first)) for g in groups[1:]]

    one = leaves * 5 // 8
    rest = leaves - one
    lead = leaves // 2
    tail = leaves - lead
    def kernel(body, out_shape, in_specs, out_specs, scratch, aliases=None, flops=1000):
        return call(body, out_shape, in_specs, out_specs, scratch, flops, 1000, 8 * MIB, aliases)

    ahead, back = lax.slice_in_dim(anomalies, tail * rows, leaves * rows), lax.slice_in_dim(anomalies, 0, one * rows)
    x_up, ahead, back = lax.optimization_barrier((anomalies, ahead, back))
    relay = lax.dynamic_slice_in_dim(x_up, jnp.where(inner == first, lead * rows, 0), tail * rows)
    relayed = passed(relay, hop)
    halo = [(passed(ahead, chain), passed(back, [(j, i) for i, j in chain]))]

    maps = (transfer_leaf.reshape(leaves * rank, rank), transfer_mid.reshape(rank, rank))
    operands = (x_up, leaf_basis, *maps)
    pieces = [jax.ShapeDtypeStruct((size * rows, columns), bf16) for size in (tail, rest)]
    part = kernel(
        up_kernel,
        jax.ShapeDtypeStruct((2 * rank, columns), bf16),
        [ANY] * 4,
        VMEM,
        [pltpu.VMEM(x.shape, bf16) for x in operands] + [pltpu.VMEM((leaves * rank, columns), bf16), pltpu.SemaphoreType.DMA((2 * leaves + 2,))],
    )(*[held(x, pltpu.HBM) for x in operands])
    parts = [part] + [swapped(part, reach) for reach in groups[1:]]
    slots = leaves * near
    parts, x_late, relayed = lax.optimization_barrier((parts, x_up, relayed))
    low, high, plane = kernel(
        pieces_kernel,
        (*pieces, jax.ShapeDtypeStruct((leaf_size * 2 * rank, columns), bf16)),
        [ANY] * 2 + [VMEM] * leaf_size,
        [VMEM] * 3,
        [pltpu.SemaphoreType.DMA((2,))],
    )(held(x_late, pltpu.HBM), relayed, *parts)
    low, high, plane, x_late = lax.optimization_barrier((low, high, plane, x_late))
    turns = [(place(g, i), place(g, i ^ turn_of(g, inner_size))) for g in groups for i in range(inner_size)]
    planes = passed(plane, [(i, j) for i, j in turns if i != j])
    halo.append(
        (
            passed(low, line + [(place(g, last), place(g, first)) for g in groups[1:]]),
            passed(high, [(j, i) for i, j in line] + [(place(g, first), place(g, last)) for g in groups[:-1]]),
        )
    )
    lists = [pltpu.SMEM((slots + 1,), jnp.int32)] * 2
    wide = resident(leaves * rows, columns, dtype=jnp.float32)
    later = (top_couple[0], mid_couple[0], maps[1], maps[0], leaf_basis)
    total, blocks, *later = kernel(
        own_kernel,
        [wide, resident(slots, rows, rows)] + [resident(*x.shape) for x in later],
        [SMEM] + [ANY] * (2 + len(later)),
        [VMEM] * (2 + len(later)),
        lists * 2 + [pltpu.VMEM(anomalies.shape, bf16), pltpu.SemaphoreType.DMA((slots + 1 + len(later),))],
        flops=1000,
    )(near_ids, *[held(x, pltpu.HBM) for x in (x_late, near_blocks.reshape(slots, rows, rows), *later)])
    blocks = held(blocks, pltpu.VMEM)
    planes, halo[0], total = lax.optimization_barrier((planes, halo[0], total))
    others = [swapped(planes, reach) for reach in range(1, inner_size)]
    total, planes = lax.optimization_barrier((total, planes))
    total = kernel(functools.partial(wave_kernel, lead, one), wide, [SMEM] + [VMEM] * 4, VMEM, lists * 2, aliases={4: 0}, flops=10**10)(
        near_ids, *halo[0], blocks, held(total, pltpu.VMEM)
    )
    others, total = lax.optimization_barrier((others, total))
    total = kernel(
        functools.partial(down_kernel, leaf_size, inner_size),
        wide,
        [SMEM] * 2 + [VMEM] * (7 + inner_size),
        VMEM,
        [pltpu.VMEM((inner_size * leaf_size * 2 * rank, columns), bf16)],
        aliases={8 + inner_size: 0},
    )(far_ids, far_count, plane, planes, *others, *later, held(total, pltpu.VMEM))
    out, _ = kernel(
        functools.partial(last_kernel, lead, one),
        (jax.ShapeDtypeStruct(anomalies.shape, bf16), wide),
        [SMEM] + [VMEM] * 4,
        (ANY, VMEM),
        lists * 2 + [pltpu.VMEM(anomalies.shape, bf16), pltpu.SemaphoreType.DMA((leaves,))],
        aliases={4: 1},
    )(near_ids, *halo[1], blocks, held(total, pltpu.VMEM))
    return out


def solution(mesh):
    return jax.shard_map(
        local,
        mesh=mesh,
        in_specs=(
            P(("leaf", "inner"), "groups"),
            P(("leaf", "inner"), None, None),
            P(("leaf", "inner"), None, None, None),
            P(("leaf", "inner"), None),
            P(("leaf", "inner"), None, None),
            P(("leaf", "inner"), None, None),
            P(("leaf", "inner"), None),
            P(("leaf", "inner")),
            P(("leaf", "inner"), None, None, None),
            P("leaf", None, None, None),
        ),
        out_specs=P(("leaf", "inner"), "groups"),
        check_vma=False,
    )
```

```python
import functools

import jax
import jax.numpy as jnp
from jax import lax
from jax.experimental import pallas as pl
from jax.experimental.pallas import tpu as pltpu
from jax.sharding import PartitionSpec as P

MIB = 1 << 20
VMEM = pl.BlockSpec(memory_space=pltpu.VMEM)
SMEM = pl.BlockSpec(memory_space=pltpu.SMEM)
ANY = pl.BlockSpec(memory_space=pl.ANY)


def held(x, space):
    return pltpu.with_memory_space_constraint(x, space)


def resident(*shape, dtype=jnp.bfloat16):
    return pltpu.VMEM(shape, dtype)


def turn_of(leaf, inner_size):
    return (3 * leaf + 2) % inner_size


def carrier(turn, inner_size):
    return lax.rem((turn + inner_size - 2 % inner_size) * pow(3, -1, inner_size), inner_size)


def dot(a, b):
    return lax.dot_general(a, b, (((1,), (0,)), ((), ())), preferred_element_type=jnp.float32)


def dot_t(a, b):
    return lax.dot_general(a, b, (((0,), (0,)), ((), ())), preferred_element_type=jnp.float32)


def call(kernel, out_shape, in_specs, out_specs, scratch, flops, moved, vmem, aliases=None):
    return pl.pallas_call(
        kernel,
        out_shape=out_shape,
        in_specs=in_specs,
        out_specs=out_specs,
        scratch_shapes=scratch,
        cost_estimate=pl.CostEstimate(flops=flops, bytes_accessed=moved, transcendentals=0),
        compiler_params=pltpu.CompilerParams(vmem_limit_bytes=vmem),
        input_output_aliases=aliases or {},
    )


def up_kernel(x_ref, basis_ref, leaf_map_ref, mid_map_ref, out_ref, x, basis, leaf_map, mid_map, skeleton, sems):
    leaves, rank, rows = basis.shape
    parts = []
    for leaf in range(leaves):
        here = slice(leaf * rows, (leaf + 1) * rows)
        parts.append(pltpu.make_async_copy(x_ref.at[here], x.at[here], sems.at[leaf]))
        parts.append(pltpu.make_async_copy(basis_ref.at[leaf], basis.at[leaf], sems.at[leaves + leaf]))
    maps = [pltpu.make_async_copy(leaf_map_ref, leaf_map, sems.at[2 * leaves]), pltpu.make_async_copy(mid_map_ref, mid_map, sems.at[2 * leaves + 1])]
    for copy in parts + maps:
        copy.start()
    for leaf in range(leaves):
        parts[2 * leaf].wait()
        parts[2 * leaf + 1].wait()
        skeleton[leaf * rank : (leaf + 1) * rank, :] = dot(basis[leaf], x[leaf * rows : (leaf + 1) * rows, :]).astype(jnp.bfloat16)
    for copy in maps:
        copy.wait()
    mid = dot_t(leaf_map[...], skeleton[...]).astype(jnp.bfloat16)
    out_ref[:rank, :] = mid
    out_ref[rank:, :] = dot_t(mid_map[...], mid).astype(jnp.bfloat16)


def pieces_kernel(x_ref, relayed, *refs):
    parts, (low, high, plane, sems) = refs[:-4], refs[-4:]
    inner = lax.axis_index("inner")
    size = low.shape[0]
    ends = (inner == lax.axis_size("inner") - 1, inner == 0)
    for i, (piece, at_end, first) in enumerate(zip((low, high), ends, (0, x_ref.shape[0] - size))):

        @pl.when(at_end)
        def _():
            pltpu.make_async_copy(relayed, piece, sems.at[i]).start()

        @pl.when(jnp.logical_not(at_end))
        def _():
            pltpu.make_async_copy(x_ref.at[first : first + size], piece, sems.at[i]).start()

    height = parts[0].shape[0]
    for i, part in enumerate(parts):
        plane[i * height : (i + 1) * height, :] = part[...]
    for i, piece in enumerate((low, high)):
        pltpu.make_async_copy(relayed, piece, sems.at[i]).wait()


def down_kernel(leaf_size, inner_size, far_ids, far_count, plane, *refs):
    found, refs = refs[:inner_size], refs[inner_size:]
    couple, mid_couple, mid_map, leaf_map, basis, _, total_ref, planes = refs
    rank = mid_map.shape[0]
    size = 2 * rank
    for step, part in enumerate(found):
        planes[step * leaf_size * size : (step + 1) * leaf_size * size, :] = part[...]
    group = lax.axis_index("leaf")
    inner = lax.axis_index("inner")

    def at_of(step, distance, offset=0):
        return pl.ds(pl.multiple_of((step * leaf_size + distance) * size + offset, rank), rank)

    top_down = jnp.zeros((rank, plane.shape[1]), jnp.float32)
    for distance in range(1, leaf_size):
        other = group ^ distance
        top = plane[at_of(0, distance, rank), :].astype(jnp.float32)
        for step in range(inner_size):
            top += planes[at_of(step, step ^ distance, rank), :].astype(jnp.float32)
        term = dot(couple[other], top.astype(jnp.bfloat16))
        top_down += jnp.where(jnp.abs(other - group) >= 2, term, 0.0)
    total = dot(mid_map[...], top_down.astype(jnp.bfloat16))
    for slot in range(mid_couple.shape[0]):
        live = slot < far_count[0]
        partner = jnp.where(live, far_ids[0, slot], group * inner_size)
        other, turn = partner // inner_size, inner ^ lax.rem(partner, inner_size)
        step = (group & (inner_size - 1)) ^ carrier(turn, inner_size)
        here, there = plane[at_of(0, group ^ other), :], planes[at_of(step, group ^ step ^ other), :]
        term = dot(mid_couple[slot], jnp.where(turn == 0, here, there))
        total += jnp.where(live, term, 0.0)
    leaf_down = dot(leaf_map[...], total.astype(jnp.bfloat16)).astype(jnp.bfloat16)
    leaves, _, rows = basis.shape
    for leaf in range(leaves):
        total_ref[leaf * rows : (leaf + 1) * rows, :] += dot_t(basis[leaf], leaf_down[leaf * rank : (leaf + 1) * rank, :])


def listed(ids_ref, lists, kind_of):
    leaves, near = ids_ref.shape
    first = (lax.axis_index("leaf") * lax.axis_size("inner") + lax.axis_index("inner")) * leaves

    def one(leaf, counts):
        for k in range(near):
            offset = ids_ref[leaf, k] - first
            grown = []
            for (slots, places), count, (member, place) in zip(lists, counts, kind_of(leaf, offset)):
                slots[count] = leaf * near + k
                places[count] = place
                grown.append(count + member.astype(jnp.int32))
            counts = tuple(grown)
        return counts

    return lax.fori_loop(0, leaves, one, (jnp.int32(0),) * len(lists))


def add_products(near, kind, count, blocks, x_ref, total, arrived=lambda slot: None):
    slots, places = kind
    rows = blocks.shape[1]
    half = rows // 2

    def product(i):
        slot = slots[i]
        arrived(slot)
        at = pl.ds(pl.multiple_of(places[i] * rows, rows), rows)
        here = slot // near * rows
        partner = x_ref[at, :]
        return here, [dot(blocks[slot, :half, :], partner), dot(blocks[slot, half:, :], partner)]

    def add(start, terms):
        for i, term in enumerate(terms):
            total[pl.ds(pl.multiple_of(start + i * half, half), half), :] += term

    def pair(j, carry):
        one, first = product(2 * j)
        two, second = product(2 * j + 1)
        add(one, first)
        add(two, second)
        return carry

    lax.fori_loop(0, count // 2, pair, 0)

    @pl.when(lax.rem(count, 2) == 1)
    def _():
        add(*product(count - 1))


def own_kernel(ids_ref, x_hbm, blocks_ref, *refs):
    count = (len(refs) - 8) // 2
    sources, total, blocks, targets = refs[:count], refs[count], refs[count + 1], refs[count + 2 : 2 * count + 2]
    own_slots, own_places, other_slots, other_places, x_ref, sems = refs[2 * count + 2 :]
    leaves, near = ids_ref.shape
    slots = leaves * near
    load = pltpu.make_async_copy(x_hbm, x_ref, sems.at[slots])
    load.start()

    def kind_of(leaf, offset):
        own = (offset >= 0) & (offset < leaves)
        return (own, offset), (jnp.logical_not(own), 0)

    kinds = ((own_slots, own_places), (other_slots, other_places))
    own_count, other_count = listed(ids_ref, kinds, kind_of)

    def copy(slot):
        return pltpu.make_async_copy(blocks_ref.at[slot], blocks.at[slot], sems.at[slot])

    def begin(slots):
        def one(i, carry):
            copy(slots[i]).start()
            return carry

        return one

    lax.fori_loop(0, own_count, begin(own_slots), 0)
    lax.fori_loop(0, other_count, begin(other_slots), 0)
    others = [pltpu.make_async_copy(source, target, sems.at[slots + 1 + i]) for i, (source, target) in enumerate(zip(sources, targets))]
    for other in others:
        other.start()
    total[...] = jnp.zeros_like(total)
    load.wait()
    add_products(near, kinds[0], own_count, blocks, x_ref, total, lambda slot: copy(slot).wait())

    def finish(i, carry):
        copy(other_slots[i]).wait()
        return carry

    lax.fori_loop(0, other_count, finish, 0)
    for other in others:
        other.wait()


def wave_kernel(near_by, ids_ref, before, after, blocks, _, total, *lists):
    leaves, near = ids_ref.shape

    def kind_of(leaf, offset):
        return ((offset < 0) & (offset >= -near_by), offset + near_by), ((offset >= leaves) & (offset < leaves + near_by), offset - leaves)

    kinds = (lists[:2], lists[2:])
    counts = listed(ids_ref, kinds, kind_of)
    for kind, count, x_ref in zip(kinds, counts, (before, after)):
        add_products(near, kind, count, blocks, x_ref, total)


def last_kernel(near_by, ids_ref, after, before, blocks, _, out_ref, total, *refs):
    lists, (result, sems) = refs[:4], refs[4:]
    leaves, near = ids_ref.shape
    rows = blocks.shape[1]

    def kind_of(leaf, offset):
        return (offset < -near_by, offset + leaves), (offset >= leaves + near_by, offset - leaves - near_by)

    kinds = (lists[:2], lists[2:])
    counts = listed(ids_ref, kinds, kind_of)
    for kind, count, x_ref in zip(kinds, counts, (before, after)):
        add_products(near, kind, count, blocks, x_ref, total)
    stores = []
    for leaf in range(leaves):
        here = slice(leaf * rows, (leaf + 1) * rows)
        result[here, :] = total[here, :].astype(result.dtype)
        stores.append(pltpu.make_async_copy(result.at[here], out_ref.at[here], sems.at[leaf]))
        stores[-1].start()
    for store in stores:
        store.wait()


def local(anomalies, leaf_basis, near_blocks, near_ids, transfer_leaf, transfer_mid, far_ids, far_count, mid_couple, top_couple):
    leaves, rank, rows = leaf_basis.shape
    near = near_blocks.shape[1]
    columns = anomalies.shape[1]
    inner_size = lax.axis_size("inner")
    leaf_size = lax.axis_size("leaf")
    bf16 = jnp.bfloat16
    inner = lax.axis_index("inner")
    first, last = 0, inner_size - 1
    groups = range(leaf_size)

    def place(leaf, i):
        return leaf * inner_size + i

    def passed(x, pairs):
        return lax.ppermute(x, ("leaf", "inner"), pairs)

    def swapped(x, reach):
        return lax.ppermute(x, "leaf", [(i, i ^ reach) for i in groups])

    chain = [(i, i + 1) for i in range(leaf_size * inner_size - 1)]
    line = [(place(g, i), place(g, i + 1)) for g in groups for i in range(last)]
    hop = [(place(g, last), place(g + 1, last)) for g in groups[:-1]] + [(place(g, first), place(g - 1, first)) for g in groups[1:]]

    one = leaves * 5 // 8
    rest = leaves - one
    def kernel(body, out_shape, in_specs, out_specs, scratch, aliases=None, flops=1000):
        return call(body, out_shape, in_specs, out_specs, scratch, flops, 1000, 8 * MIB, aliases)

    ahead, back = lax.slice_in_dim(anomalies, rest * rows, leaves * rows), lax.slice_in_dim(anomalies, 0, one * rows)
    x_up, ahead, back = lax.optimization_barrier((anomalies, ahead, back))
    relay = lax.dynamic_slice_in_dim(x_up, jnp.where(inner == first, one * rows, 0), rest * rows)
    relayed = passed(relay, hop)
    halo = [(passed(ahead, chain), passed(back, [(j, i) for i, j in chain]))]

    maps = (transfer_leaf.reshape(leaves * rank, rank), transfer_mid.reshape(rank, rank))
    operands = (x_up, leaf_basis, *maps)
    piece = jax.ShapeDtypeStruct((rest * rows, columns), bf16)
    part = kernel(
        up_kernel,
        jax.ShapeDtypeStruct((2 * rank, columns), bf16),
        [ANY] * 4,
        VMEM,
        [pltpu.VMEM(x.shape, bf16) for x in operands] + [pltpu.VMEM((leaves * rank, columns), bf16), pltpu.SemaphoreType.DMA((2 * leaves + 2,))],
    )(*[held(x, pltpu.HBM) for x in operands])
    parts = [part] + [swapped(part, reach) for reach in groups[1:]]
    slots = leaves * near
    parts, x_late, relayed = lax.optimization_barrier((parts, x_up, relayed))
    low, high, plane = kernel(
        pieces_kernel,
        (piece, piece, jax.ShapeDtypeStruct((leaf_size * 2 * rank, columns), bf16)),
        [ANY] * 2 + [VMEM] * leaf_size,
        [VMEM] * 3,
        [pltpu.SemaphoreType.DMA((2,))],
    )(held(x_late, pltpu.HBM), relayed, *parts)
    low, high, plane, x_late = lax.optimization_barrier((low, high, plane, x_late))
    turns = [(place(g, i), place(g, i ^ turn_of(g, inner_size))) for g in groups for i in range(inner_size)]
    planes = passed(plane, [(i, j) for i, j in turns if i != j])
    far_back = passed(high, [(j, i) for i, j in line] + [(place(g, first), place(g, last)) for g in groups[:-1]])
    far_ahead = passed(low, line + [(place(g, last), place(g, first)) for g in groups[1:]])
    halo.append((far_ahead, far_back))
    lists = [pltpu.SMEM((slots + 1,), jnp.int32)] * 2
    wide = resident(leaves * rows, columns, dtype=jnp.float32)
    later = (top_couple[0], mid_couple[0], maps[1], maps[0], leaf_basis)
    total, blocks, *later = kernel(
        own_kernel,
        [wide, resident(slots, rows, rows)] + [resident(*x.shape) for x in later],
        [SMEM] + [ANY] * (2 + len(later)),
        [VMEM] * (2 + len(later)),
        lists * 2 + [pltpu.VMEM(anomalies.shape, bf16), pltpu.SemaphoreType.DMA((slots + 1 + len(later),))],
        flops=1000,
    )(near_ids, *[held(x, pltpu.HBM) for x in (x_late, near_blocks.reshape(slots, rows, rows), *later)])
    blocks = held(blocks, pltpu.VMEM)
    planes, halo[0], total = lax.optimization_barrier((planes, halo[0], total))
    others = [swapped(planes, reach) for reach in range(1, inner_size)]
    total, planes = lax.optimization_barrier((total, planes))
    total = kernel(functools.partial(wave_kernel, one), wide, [SMEM] + [VMEM] * 4, VMEM, lists * 2, aliases={4: 0}, flops=10**10)(
        near_ids, *halo[0], blocks, held(total, pltpu.VMEM)
    )
    others, total = lax.optimization_barrier((others, total))
    total = kernel(
        functools.partial(down_kernel, leaf_size, inner_size),
        wide,
        [SMEM] * 2 + [VMEM] * (7 + inner_size),
        VMEM,
        [pltpu.VMEM((inner_size * leaf_size * 2 * rank, columns), bf16)],
        aliases={8 + inner_size: 0},
    )(far_ids, far_count, plane, planes, *others, *later, held(total, pltpu.VMEM))
    out, _ = kernel(
        functools.partial(last_kernel, one),
        (jax.ShapeDtypeStruct(anomalies.shape, bf16), wide),
        [SMEM] + [VMEM] * 4,
        (ANY, VMEM),
        lists * 2 + [pltpu.VMEM(anomalies.shape, bf16), pltpu.SemaphoreType.DMA((leaves,))],
        aliases={4: 1},
    )(near_ids, *halo[1][::-1], blocks, held(total, pltpu.VMEM))
    return out


def solution(mesh):
    return jax.shard_map(
        local,
        mesh=mesh,
        in_specs=(
            P(("leaf", "inner"), "groups"),
            P(("leaf", "inner"), None, None),
            P(("leaf", "inner"), None, None, None),
            P(("leaf", "inner"), None),
            P(("leaf", "inner"), None, None),
            P(("leaf", "inner"), None, None),
            P(("leaf", "inner"), None),
            P(("leaf", "inner")),
            P(("leaf", "inner"), None, None, None),
            P("leaf", None, None, None),
        ),
        out_specs=P(("leaf", "inner"), "groups"),
        check_vma=False,
    )
```
